32 devices in a mesh: grp: 4 (over y, x), head: 8 (over z, core).
Axes of the slice: x: 2, y: 2, z: 4, core: 2. Of those that a mesh axis runs over, the one named last changes fastest.
Arguments:
- prefill_token_rows: bfloat16 [256, 8192], P('grp', 'head'), may hold values from -6 to 6
- decode_token_rows: bfloat16 [3, 128, 8192], P(None, 'grp', 'head'), may hold values from -6 to 6
- input_weight: bfloat16 [8192, 2048], P('head'), may hold values from -0.0625 to 0.0625
- lowrank_weight: bfloat16 [8192, 384], P('head'), may hold values from -0.0625 to 0.0625
- step_size_weight: bfloat16 [8192, 16], P('head'), may hold values from -0.0625 to 0.0625
- adapter_up_weight: bfloat16 [128, 1024], P(None, 'head'), may hold values from -1.5 to 1.5
- output_weight: bfloat16 [1024, 8192], P('head'), may hold values from -0.25 to 0.25
- head_decay_rate: float32 [16], P('head'), may hold values from 0.0005 to 0.1
- head_step_bias: float32 [16], P('head'), may hold values from -1 to 1
- head_skip_scale: float32 [16], P('head'), may hold values from 0 to 3
- gated_norm_scale: float32 [1024], P('head'), may hold values from 0.1 to 1.9
- prompt_start_state: float32 [8, 16, 64, 128], P('grp', 'head'), may hold values from -18 to 18
- prompt_at_position: int32 [8], replicated, may hold values from 0 to 7, each once
- slot_sample_index: int32 [128], P('grp'), may hold values from 0 to 127, each once
- prompt_adapter_index: int32 [8], replicated, may hold values from 0 to 7
Outputs:
- prefill_out: float32 [256, 8192], P('grp', 'head')
- decode_out: float32 [3, 128, 8192], P(None, 'grp', 'head')
The draws below stay inside these ranges and needn't reach their ends.
Inputs may be any that keep to these rules, and one draw needn't show every extreme that they name: Position i of the prefill rows and of prompt_start_state holds prompt prompt_at_position[i]; every prompt stands once. Decode slot j carries sample slot_sample_index[j] of prompt slot_sample_index[j] // 16; every sample stands once. `prompt_adapter_index`: the adapter used by every row of that prompt and of its samples.
All inputs are finite; a program needn't handle non-finite values.
Results may differ from the reference program's by a relative error of at most 0.0027.
Values may be sent and summed in bfloat16 or wider, within the bound.
No kernel may reach another device: no remote copies, remote signals or barrier semaphores. Data moves between devices by JAX's collectives and lax.ppermute only.
A program may use at most 64 MiB of HBM per device.

```python
import math
import jax
import jax.numpy as jnp
from jax import lax

D = 8192
HEAD_CHANNELS = 64
STATE = 128
HEAD_DEV = 2
MIXER_HEADS = 16
INNER_CHANNELS = 1024
STRETCH = 32
PROMPTS = 8
SAMPLES = 16
ROWS = 128
STEPS = 3
ADAPTER_COUNT = 8
ADAPTER_RANK = 16


def with_ends(entries, own_key, least, high):
    spot = [jax.random.randint(jax.random.fold_in(own_key, axis), (), 0, length) for axis, length in enumerate(entries.shape)]
    longest = entries.shape.index(max(entries.shape))
    beside = spot[:longest] + [(spot[longest] + 1) % entries.shape[longest]] + spot[longest + 1:]
    return entries.at[tuple(spot)].set(least).at[tuple(beside)].set(high)


def with_spikes(values, key, source, target, blocks, factor):
    owner, partner = [(jnp.arange(values.shape[dim]) // (values.shape[dim] // blocks)).reshape([-1 if axis == dim else 1 for axis in range(values.ndim)]) for dim in (source, target)]
    chosen = jax.random.permutation(key, blocks)[partner]
    strong = (owner == chosen) | (owner == (partner + blocks // 2) % blocks)
    return jnp.where(strong, factor * values, values)


def steps_of(key, extent, split, smallest, largest):
    factor_of, own = 1.0, jax.random.fold_in(key, 6)
    for axis_at, parts in split:
        heights = jnp.exp(jax.random.uniform(jax.random.fold_in(own, axis_at), (parts,), jnp.float32, smallest / len(split), largest / len(split)))
        factor_of = factor_of * jnp.repeat(heights, extent[axis_at] // parts).reshape([-1 if axis == axis_at else 1 for axis in range(len(extent))])
    return factor_of


def centred(own_key, dims, scale, reach, split=(), kind=jnp.bfloat16):
    values = scale * jax.random.normal(own_key, dims, jnp.float32)
    if split:
        values = values * steps_of(own_key, dims, split, -0.22, 0.18)
    return jnp.clip(values, -reach, reach).astype(kind)


def heavy_noise(own_key, dims, deviation, limit, shards, heavy, kind=jnp.bfloat16):
    drawn = deviation * jax.random.normal(own_key, dims, jnp.float32)
    if shards:
        drawn = drawn * steps_of(own_key, dims, shards, -0.22, 0.18)
    return jnp.clip(with_spikes(drawn, jax.random.fold_in(own_key, 3), *heavy), -limit, limit).astype(kind)


def setup_inputs(seed: int = 0) -> dict:
    key_of = jax.random.split(jax.random.key(seed), 16)
    return {
        "prefill_token_rows": centred(key_of[0], (PROMPTS * STRETCH, D), 1.0, 6.0, ((0, 4), (1, 8))),
        "decode_token_rows": centred(key_of[1], (STEPS, ROWS, D), 1.0, 6.0, ((1, 4), (2, 8))),
        "input_weight": centred(key_of[2], (D, 2 * INNER_CHANNELS), D ** -0.5, 0.0625, ((0, 8),)),
        "lowrank_weight": centred(key_of[3], (D, 2 * STATE + ADAPTER_COUNT * ADAPTER_RANK), D ** -0.5, 0.0625, ((0, 8),)),
        "step_size_weight": centred(key_of[4], (D, MIXER_HEADS), D ** -0.5, 0.0625, ((0, 8),)),
        "adapter_up_weight": centred(key_of[5], (ADAPTER_COUNT * ADAPTER_RANK, INNER_CHANNELS), ADAPTER_RANK ** -0.5, 1.5, ((1, 8),)),
        "output_weight": heavy_noise(key_of[6], (INNER_CHANNELS, D), INNER_CHANNELS ** -0.5, 0.25, ((0, 8),), (0, 1, 8, 2.0)),
        "head_decay_rate": jnp.clip(jnp.exp(math.log(0.1) - 5.2983173 * jax.random.uniform(key_of[7], (MIXER_HEADS,), jnp.float32) ** steps_of(key_of[7], (MIXER_HEADS,), ((0, 8),), -0.2, 0.2)), 0.0005, 0.1),
        "head_step_bias": jnp.clip(jax.random.uniform(key_of[8], (MIXER_HEADS,), jnp.float32, -1.0, 1.0) * steps_of(key_of[8], (MIXER_HEADS,), ((0, 8),), -0.4, 0.0), -1.0, 1.0),
        "head_skip_scale": jnp.clip(3.0 * jax.random.uniform(key_of[9], (MIXER_HEADS,), jnp.float32) ** steps_of(key_of[9], (MIXER_HEADS,), ((0, 8),), -0.2, 0.2), 0.0, 3.0),
        "gated_norm_scale": jnp.clip(1.0 + 0.18 * jax.random.normal(key_of[10], (INNER_CHANNELS,), jnp.float32), 0.1, 1.9),
        "prompt_start_state": centred(key_of[11], (PROMPTS, MIXER_HEADS, HEAD_CHANNELS, STATE), 3.0, 18.0, ((0, 4), (1, 8)), jnp.float32),
        "prompt_at_position": jax.random.permutation(key_of[12], PROMPTS).astype(jnp.int32),
        "slot_sample_index": jax.random.permutation(key_of[13], ROWS).astype(jnp.int32),
        "prompt_adapter_index": with_ends(jax.random.randint(key_of[14], (PROMPTS,), 0, ADAPTER_COUNT), jax.random.fold_in(key_of[14], 1), 0, ADAPTER_COUNT - 1).astype(jnp.int32),
    }


def block_pass(value_channels, write_vector, read_vector, head_step_length, initial, rate, skip):
    length = value_channels.shape[0]
    log_decay = -(head_step_length * rate[None, :])
    running = jnp.cumsum(log_decay, axis=0).T
    later = jnp.arange(length, dtype=jnp.int32)[:, None] >= jnp.arange(length, dtype=jnp.int32)[None, :]
    spread = jnp.where(later[None], running[:, :, None] - running[:, None, :], 0.0)
    weights = jnp.where(later[None], jnp.exp(spread), 0.0) * head_step_length.T[:, None, :]
    scores = jnp.dot(read_vector, write_vector.T, precision=lax.Precision.HIGHEST)
    mixed = weights * scores[None]
    result = jnp.einsum('hts,shp->thp', mixed, value_channels, precision=lax.Precision.HIGHEST)
    carried = jnp.einsum('hpn,tn->thp', initial, read_vector, precision=lax.Precision.HIGHEST)
    result = result + jnp.exp(running).T[:, :, None] * carried + skip[None, :, None] * value_channels
    ending = running[:, -1]
    tail = jnp.exp(ending[None, :] - running.T) * head_step_length
    final = jnp.exp(ending)[:, None, None] * initial + jnp.einsum('sh,shp,sn->hpn', tail, value_channels, write_vector, precision=lax.Precision.HIGHEST)
    return (result, final)

def prepare_inputs(token_rows, adapter_index, input_weight, lowrank_weight, step_size_weight, adapter_up_weight, head_step_bias):
    token_count = token_rows.shape[0]
    proj = jnp.dot(token_rows, input_weight, preferred_element_type=jnp.float32).reshape(token_count, MIXER_HEADS, 2, HEAD_CHANNELS)
    low = jnp.dot(token_rows, lowrank_weight, preferred_element_type=jnp.float32)
    raw = jnp.dot(token_rows, step_size_weight, preferred_element_type=jnp.float32)
    slot_lanes = jnp.arange(ADAPTER_COUNT * ADAPTER_RANK, dtype=jnp.int32) // ADAPTER_RANK
    selected_rows = jnp.where(slot_lanes[None, :] == adapter_index[:, None], low[:, 2 * STATE:], 0.0).astype(jnp.bfloat16)
    step_delta = jnp.dot(selected_rows, adapter_up_weight, preferred_element_type=jnp.float32).reshape(token_count, MIXER_HEADS, HEAD_CHANNELS)
    value_channels = proj[:, :, 0, :] + step_delta
    gate_branch = proj[:, :, 1, :]
    head_step_length = jax.nn.softplus(raw + head_step_bias[None, :])
    return (value_channels, gate_branch, low[:, :STATE], low[:, STATE:2 * STATE], head_step_length)

def finish(result, gate_branch, token_rows, gated_norm_scale, output_weight):
    token_count = result.shape[0]
    groups = MIXER_HEADS // HEAD_DEV
    width = HEAD_DEV * HEAD_CHANNELS
    gated = (result * jax.nn.silu(gate_branch)).reshape(token_count, groups, width)
    scale = lax.rsqrt(lax.optimization_barrier(jnp.mean(gated * gated, axis=-1, keepdims=True)) + 1e-05)
    normed = (gated * scale * gated_norm_scale.reshape(groups, width)[None]).reshape(token_count, groups * width).astype(jnp.bfloat16)
    summed = jnp.dot(normed, output_weight, preferred_element_type=jnp.float32)
    return token_rows.astype(jnp.float32) + summed

def reference(prefill_token_rows, decode_token_rows, input_weight, lowrank_weight, step_size_weight, adapter_up_weight, output_weight, head_decay_rate, head_step_bias, head_skip_scale, gated_norm_scale, prompt_start_state, prompt_at_position, slot_sample_index, prompt_adapter_index):
    position = jnp.zeros((PROMPTS,), jnp.int32).at[prompt_at_position].set(jnp.arange(PROMPTS, dtype=jnp.int32))
    prefill_tenant_index = jnp.repeat(prompt_adapter_index[prompt_at_position], STRETCH)
    value_channels, gate_branch, write_vector, read_vector, head_step_length = prepare_inputs(prefill_token_rows, prefill_tenant_index, input_weight, lowrank_weight, step_size_weight, adapter_up_weight, head_step_bias)
    shaped = (value_channels.reshape(PROMPTS, STRETCH, MIXER_HEADS, HEAD_CHANNELS), write_vector.reshape(PROMPTS, STRETCH, STATE), read_vector.reshape(PROMPTS, STRETCH, STATE), head_step_length.reshape(PROMPTS, STRETCH, MIXER_HEADS), prompt_start_state)
    results, finals = lax.map(lambda group_args: block_pass(group_args[0], group_args[1], group_args[2], group_args[3], group_args[4], head_decay_rate, head_skip_scale), shaped)
    prefill_out = finish(results.reshape(PROMPTS * STRETCH, MIXER_HEADS, HEAD_CHANNELS), gate_branch, prefill_token_rows, gated_norm_scale, output_weight)
    sample_prompt = slot_sample_index // SAMPLES
    state = finals[position[sample_prompt]]
    row_adapter_index = prompt_adapter_index[sample_prompt]
    outputs = []
    for step in range(STEPS):
        token_rows = decode_token_rows[step]
        value_channels, gate_branch, write_vector, read_vector, head_step_length = prepare_inputs(token_rows, row_adapter_index, input_weight, lowrank_weight, step_size_weight, adapter_up_weight, head_step_bias)
        decay = jnp.exp(-head_step_length * head_decay_rate[None, :])
        state = decay[:, :, None, None] * state + (head_step_length[:, :, None] * value_channels)[:, :, :, None] * write_vector[:, None, None, :]
        result = jnp.einsum('rhpn,rn->rhp', state, read_vector, precision=lax.Precision.HIGHEST) + head_skip_scale[None, :, None] * value_channels
        outputs.append(finish(result, gate_branch, token_rows, gated_norm_scale, output_weight))
    return (prefill_out, jnp.stack(outputs))
```

```python
import jax
import jax.numpy as jnp
from jax import lax
from jax.experimental import pallas as pl
from jax.experimental.pallas import tpu as pltpu
from jax.sharding import PartitionSpec as P

HEAD_CHANNELS = 64
STATE = 128
HEAD_DEV = 2
STRETCH = 32
SAMPLES = 16
STEPS = 3
ADAPTER_RANK = 16
LANES = 128
F32 = jnp.float32
BF16 = jnp.bfloat16
F16 = jnp.float16
EXACT = lax.Precision.HIGHEST
VMEM = pl.BlockSpec(memory_space=pltpu.VMEM)
SMEM = pl.BlockSpec(memory_space=pltpu.SMEM)
BIG = 48 * 1024 * 1024


def mxu(a, b):
    return jnp.dot(a, b, preferred_element_type=F32)


def dot_nt(a, b):
    return lax.dot_general(a, b, (((1,), (1,)), ((), ())), precision=EXACT, preferred_element_type=F32)


def dot_tn(a, b):
    return lax.dot_general(a, b, (((0,), (0,)), ((), ())), precision=EXACT, preferred_element_type=F32)


def lane_ids(rows):
    return lax.broadcasted_iota(jnp.int32, (rows, LANES), 1)


def row_ids(rows, width=1):
    return lax.broadcasted_iota(jnp.int32, (rows, width), 0)


def row_prompts(slots_ref, slots):
    rows = row_ids(slots)
    found = jnp.zeros((slots, 1), jnp.int32)
    for j in range(slots):
        found = jnp.where(rows == j, slots_ref[j] // SAMPLES, found)
    return found


def row_tenants(slots_ref, held_ref, tenants_ref, group, owned, slots):
    prompts = row_prompts(slots_ref, slots)
    decode = jnp.zeros((slots, 1), jnp.int32)
    for p in range(tenants_ref.shape[0]):
        decode = jnp.where(prompts == p, tenants_ref[p], decode)
    prefill = [
        jnp.full((STRETCH, 1), tenants_ref[held_ref[group * owned + i]], jnp.int32) for i in range(owned)
    ]
    return jnp.concatenate(prefill + [decode] * STEPS, axis=0)


def place_order(chips):
    bits = chips.bit_length() - 1
    order = []
    for p in range(chips):
        j = chips - 1 - p
        order.append(sum(((j >> b) & 1) << (bits - 1 - b) for b in range(bits)))
    return order


def project(where, prefill_rows, decode_rows, input_weight, lowrank_weight, step_weight, slots, held, tenants, owned):
    rows_prefill, depth = prefill_rows.shape
    rows = rows_prefill + decode_rows.shape[0]
    width = 2 * HEAD_DEV * HEAD_CHANNELS
    pieces = width // LANES
    chips = input_weight.shape[1] // width // 2
    bits = chips.bit_length() - 1
    low_width = lowrank_weight.shape[1]
    low_blocks = 2 * STATE // LANES + 1
    heads = step_weight.shape[1]
    slot_count = slots.shape[0]

    def column(i, odd, at_ref):
        j = chips - 1 - i
        rev = 0
        for b in range(bits):
            rev = rev + (((j >> b) & 1) << (bits - 1 - b))
        return (rev * 2 + odd) ^ at_ref[0]

    def send_body(at_ref, slots_ref, held_ref, tenants_ref, up_ref, ud_ref, w_ref, l_ref, s_ref, o_ref, u_ref):
        i = pl.program_id(0)

        @pl.when(i == 0)
        def _():
            u_ref[:rows_prefill] = up_ref[...]
            u_ref[rows_prefill:] = ud_ref[...]

        part = mxu(u_ref[...], w_ref[...])
        for k in range(pieces):
            o_ref[i * pieces + k] = part[:, k * LANES : (k + 1) * LANES]

        @pl.when(i == chips - 1)
        def _():
            low = mxu(u_ref[...], l_ref[...])
            base = chips * pieces
            for k in range(low_blocks - 1):
                o_ref[base + k] = low[:, k * LANES : (k + 1) * LANES]
            tenant = row_tenants(slots_ref, held_ref, tenants_ref, at_ref[1], owned, slot_count)
            lanes = lane_ids(rows)
            picked = jnp.where(lanes // ADAPTER_RANK == tenant, low[:, 2 * STATE :], 0.0)
            shift = LANES // 2
            while shift >= ADAPTER_RANK:
                picked = picked + pltpu.roll(picked, shift, 1)
                shift //= 2
            o_ref[base + low_blocks - 1] = picked
            o_ref[base + low_blocks - 1, :, ADAPTER_RANK : ADAPTER_RANK + heads] = mxu(u_ref[...], s_ref[...])

    def keep_body(at_ref, up_ref, ud_ref, w_ref, o_ref, u_ref):
        i = pl.program_id(0)

        @pl.when(i == 0)
        def _():
            u_ref[:rows_prefill] = up_ref[...]
            u_ref[rows_prefill:] = ud_ref[...]

        part = mxu(u_ref[...], w_ref[...])
        for k in range(pieces):
            o_ref[i * pieces + k] = part[:, k * LANES : (k + 1) * LANES]

    def whole(shape):
        return pl.BlockSpec(shape, lambda i, *_: (0,) * len(shape))

    def call(body, odd, prefetch, low, blocks, operands):
        specs = [
            whole(prefill_rows.shape),
            whole(decode_rows.shape),
            pl.BlockSpec((depth, width), lambda i, at_ref, *_: (0, column(i, odd, at_ref))),
        ]
        specs += [whole(lowrank_weight.shape), whole(step_weight.shape)] if low else []
        return pl.pallas_call(
            body,
            out_shape=jax.ShapeDtypeStruct((blocks, rows, LANES), F32),
            grid_spec=pltpu.PrefetchScalarGridSpec(
                num_scalar_prefetch=prefetch,
                grid=(chips,),
                in_specs=specs,
                out_specs=whole((blocks, rows, LANES)),
                scratch_shapes=[pltpu.VMEM((rows, depth), BF16)],
            ),
            compiler_params=pltpu.CompilerParams(vmem_limit_bytes=BIG),
            cost_estimate=pl.CostEstimate(
                flops=2 * rows * depth * width * chips, bytes_accessed=2 * depth * width * chips, transcendentals=0
            ),
        )(*operands)

    send = call(
        send_body, 1, 4, True, chips * pieces + low_blocks,
        (where, slots, held, tenants, prefill_rows, decode_rows, input_weight, lowrank_weight, step_weight),
    )
    keep = call(keep_body, 0, 1, False, chips * pieces, (where, prefill_rows, decode_rows, input_weight))
    return send, keep


def step_lengths(mixed, me, bias_ref):
    lanes = lane_ids(mixed.shape[0])
    lengths = []
    for h in range(HEAD_DEV):
        raw = jnp.sum(jnp.where(lanes == ADAPTER_RANK + me * HEAD_DEV + h, mixed, 0.0), axis=1, keepdims=True)
        raw = raw + bias_ref[h]
        lengths.append(jnp.maximum(raw, 0.0) + jnp.log1p(jnp.exp(-jnp.abs(raw))))
    return lengths


def by_head(first, second, rows):
    return jnp.where(lane_ids(rows) < HEAD_CHANNELS, first, second)


def prefill_decay(lengths, rate_ref, rows):
    t_at = lax.broadcasted_iota(jnp.int32, (rows, rows), 0)
    s_at = lax.broadcasted_iota(jnp.int32, (rows, rows), 1)
    same = t_at // STRETCH == s_at // STRETCH
    columns, lines, steps = [], [], []
    for h in range(HEAD_DEV):
        length = lengths[h][:rows]
        decay = -(length * rate_ref[h])
        line = jnp.sum(jnp.where(same & (t_at <= s_at), decay, 0.0), axis=0, keepdims=True)
        lines.append(line)
        columns.append(jnp.sum(jnp.where(t_at == s_at, line, 0.0), axis=1, keepdims=True))
        steps.append(jnp.sum(jnp.where(t_at == s_at, length, 0.0), axis=0, keepdims=True))
    return columns, lines, steps, same & (t_at >= s_at)


def end_states(where, summed, adapter_up, bias, rate, start, slots, held, tenants):
    rows = summed.shape[1]
    owned = start.shape[0]
    prefill = owned * STRETCH
    slot_count = slots.shape[0]

    def body(at_ref, slots_ref, held_ref, tenants_ref, bias_ref, rate_ref, x_ref, a_ref, s_ref, v_ref, f_ref):
        me, group = at_ref[0], at_ref[1]
        mixed = x_ref[4]
        lanes = lane_ids(rows)
        tenant = row_tenants(slots_ref, held_ref, tenants_ref, group, owned, slot_count)
        picked = jnp.where(lanes < ADAPTER_RANK, mixed, 0.0)
        shift = ADAPTER_RANK
        while shift < LANES:
            picked = picked + pltpu.roll(picked, shift, 1)
            shift *= 2
        picked = jnp.where(lanes // ADAPTER_RANK == tenant, picked, 0.0).astype(BF16)
        values = by_head(x_ref[0], pltpu.roll(x_ref[1], HEAD_CHANNELS, 1), rows)
        values = values + mxu(picked, a_ref[...])
        v_ref[...] = values
        lengths = step_lengths(mixed[:prefill], me, bias_ref)
        columns, _, _, _ = prefill_decay(lengths, rate_ref, prefill)
        for i in range(owned):
            lo, hi = i * STRETCH, (i + 1) * STRETCH
            ends = [columns[h][hi - 1 : hi] for h in range(HEAD_DEV)]
            tails = [jnp.exp(ends[h] - columns[h][lo:hi]) * lengths[h][lo:hi] for h in range(HEAD_DEV)]
            added = dot_tn(by_head(tails[0], tails[1], STRETCH) * values[lo:hi], x_ref[2, lo:hi])
            for h in range(HEAD_DEV):
                at = slice(h * HEAD_CHANNELS, (h + 1) * HEAD_CHANNELS)
                f_ref[i, at] = jnp.exp(ends[h]) * s_ref[i, at] + added[at]

    return pl.pallas_call(
        body,
        out_shape=(
            jax.ShapeDtypeStruct((rows, LANES), F32),
            jax.ShapeDtypeStruct((owned, LANES, STATE), F32),
        ),
        in_specs=[SMEM] * 6 + [VMEM] * 3,
        out_specs=(VMEM, VMEM),
        compiler_params=pltpu.CompilerParams(vmem_limit_bytes=BIG),
    )(where, slots, held, tenants, bias, rate, summed, adapter_up, start)


def normalise(result, gate, scale_ref):
    gated = result * (gate * (1.0 / (1.0 + jnp.exp(-gate))))
    spread = jnp.mean(gated * gated, axis=1, keepdims=True)
    return (gated * lax.rsqrt(spread + 1e-05) * scale_ref[...]).astype(BF16)


def gates(x_ref, at):
    first, second = x_ref[0, at], x_ref[1, at]
    return by_head(pltpu.roll(first, HEAD_CHANNELS, 1), second, first.shape[0])


def rows_within(where, summed, values, start, bias, rate, skip, norm_scale):
    rows = summed.shape[1]
    owned = start.shape[0]
    prefill = owned * STRETCH
    slot_count = (rows - prefill) // STEPS

    def body(at_ref, bias_ref, rate_ref, skip_ref, x_ref, v_ref, s_ref, g_ref, n_ref, y_ref):
        me = at_ref[0]
        lengths = step_lengths(x_ref[4], me, bias_ref)
        columns, lines, steps, later = prefill_decay(lengths, rate_ref, prefill)
        now = slice(0, prefill)
        values = v_ref[now]
        scores = dot_nt(x_ref[3, now], x_ref[2, now])
        sums = []
        for h in range(HEAD_DEV):
            weights = jnp.where(later, jnp.exp(jnp.where(later, columns[h] - lines[h], 0.0)), 0.0) * steps[h]
            sums.append(jnp.dot(weights * scores, values, precision=EXACT, preferred_element_type=F32))
        result = by_head(sums[0], sums[1], prefill)
        carried = jnp.concatenate(
            [dot_nt(x_ref[3, i * STRETCH : (i + 1) * STRETCH], s_ref[i]) for i in range(owned)], axis=0
        )
        kept = by_head(jnp.exp(columns[0]), jnp.exp(columns[1]), prefill)
        skipped = by_head(skip_ref[0], skip_ref[1], prefill)
        result = result + kept * carried + skipped * values
        n_ref[...] = normalise(result, gates(x_ref, now), g_ref)
        at = [slice(prefill + s * slot_count, prefill + (s + 1) * slot_count) for s in range(STEPS)]
        run = [[], []]
        for h in range(HEAD_DEV):
            total = jnp.zeros((slot_count, 1), F32)
            for s in range(STEPS):
                total = total - lengths[h][at[s]] * rate_ref[h]
                run[h].append(total)
        skipped = by_head(skip_ref[0], skip_ref[1], slot_count)
        for s in range(STEPS):
            total = skipped * v_ref[at[s]]
            for u in range(s + 1):
                score = jnp.sum(x_ref[3, at[s]] * x_ref[2, at[u]], axis=1, keepdims=True)
                factor = [jnp.exp(run[h][s] - run[h][u]) * lengths[h][at[u]] * score for h in range(HEAD_DEV)]
                total = total + by_head(factor[0], factor[1], slot_count) * v_ref[at[u]]
            y_ref[s * slot_count : (s + 1) * slot_count] = total

    return pl.pallas_call(
        body,
        out_shape=(
            jax.ShapeDtypeStruct((prefill, LANES), BF16),
            jax.ShapeDtypeStruct((rows - prefill, LANES), F32),
        ),
        in_specs=[SMEM] * 4 + [VMEM] * 4,
        out_specs=(VMEM, VMEM),
        compiler_params=pltpu.CompilerParams(vmem_limit_bytes=BIG),
    )(where, bias, rate, skip, summed, values, start, norm_scale)


def decode_rows_out(where, summed, within, prefill_normed, finals, bias, rate, norm_scale, slots, held):
    rows = summed.shape[1]
    prefill = prefill_normed.shape[0]
    owned = finals[0].shape[0]
    slot_count = slots.shape[0]
    parts = len(finals)

    def body(at_ref, slots_ref, held_ref, bias_ref, rate_ref, x_ref, y_ref, p_ref, g_ref, *rest):
        f_refs, n_ref = rest[:parts], rest[parts]
        me, group = at_ref[0], at_ref[1]
        now = slice(prefill, rows)
        prompts = row_prompts(slots_ref, slot_count)
        prompts = jnp.concatenate([prompts] * STEPS, axis=0)
        reader = x_ref[3, now]
        carried = jnp.zeros((rows - prefill, LANES), F32)
        for j in range(parts):
            for i in range(owned):
                mine = prompts == held_ref[(group ^ j) * owned + i]
                carried = carried + dot_nt(jnp.where(mine, reader, 0.0), f_refs[j][i])
        lengths = step_lengths(x_ref[4, now], me, bias_ref)
        kept = []
        for h in range(HEAD_DEV):
            total = jnp.zeros((slot_count, 1), F32)
            runs = []
            for s in range(STEPS):
                total = total - lengths[h][s * slot_count : (s + 1) * slot_count] * rate_ref[h]
                runs.append(total)
            kept.append(jnp.exp(jnp.concatenate(runs, axis=0)))
        result = y_ref[...] + by_head(kept[0], kept[1], rows - prefill) * carried
        n_ref[:prefill] = p_ref[...]
        n_ref[prefill:] = normalise(result, gates(x_ref, now), g_ref)

    return pl.pallas_call(
        body,
        out_shape=jax.ShapeDtypeStruct((rows, LANES), BF16),
        in_specs=[SMEM] * 5 + [VMEM] * (4 + parts),
        out_specs=VMEM,
        compiler_params=pltpu.CompilerParams(vmem_limit_bytes=BIG),
    )(where, slots, held, bias, rate, summed, within, prefill_normed, norm_scale, *finals)


def output_rows(where, near, far, weights, prefill_rows, decode_rows):
    chips, rows, _ = near.shape
    prefill, width = prefill_rows.shape
    parts = len(weights)
    per_part = chips // parts
    tile = width // 4 if width % 512 == 0 else width

    def body(at_ref, a_ref, b_ref, up_ref, ud_ref, *rest):
        w_refs, (op_ref, od_ref) = rest[:parts], rest[parts:]
        total = jnp.zeros((rows, tile), F32)
        for j in range(parts):
            for k in range(per_part):
                chip = (at_ref[1] ^ j) + parts * k
                pair = jnp.concatenate([a_ref[chip], b_ref[chip]], axis=1)
                total = total + mxu(pair, w_refs[j][k])
        op_ref[...] = up_ref[...].astype(F32) + total[:prefill]
        od_ref[...] = ud_ref[...].astype(F32) + total[prefill:]

    def column(shape):
        return pl.BlockSpec(shape, lambda i, *_: (0,) * (len(shape) - 1) + (i,))

    def whole(shape):
        return pl.BlockSpec(shape, lambda i, *_: (0,) * len(shape))

    return pl.pallas_call(
        body,
        out_shape=(
            jax.ShapeDtypeStruct(prefill_rows.shape, F32),
            jax.ShapeDtypeStruct(decode_rows.shape, F32),
        ),
        grid_spec=pltpu.PrefetchScalarGridSpec(
            num_scalar_prefetch=1,
            grid=(width // tile,),
            in_specs=[
                whole(near.shape),
                whole(far.shape),
                column((prefill, tile)),
                column((rows - prefill, tile)),
            ]
            + [column(w.shape[:-1] + (tile,)) for w in weights],
            out_specs=(column((prefill, tile)), column((rows - prefill, tile))),
        ),
        compiler_params=pltpu.CompilerParams(vmem_limit_bytes=BIG),
    )(where, near, far, prefill_rows, decode_rows, *weights)


def solution(mesh):
    groups, heads = mesh.shape["grp"], mesh.shape["head"]
    chips = heads // 2
    stages = [1 << b for b in range(chips.bit_length() - 1)]
    order = place_order(chips)

    def across(x, distance):
        return lax.ppermute(x, "head", [(i, i ^ distance) for i in range(heads)])

    def over_groups(x, distance):
        return lax.ppermute(x, "grp", [(i, i ^ distance) for i in range(groups)])

    def weight_columns(output_weight, head, group):
        own_rows = output_weight.shape[0]
        width = output_weight.shape[1] // heads
        core = head % 2
        pieces = []
        for k in range(chips // groups):
            target = (head // 2) ^ (group + groups * k)
            piece = lax.dynamic_slice_in_dim(output_weight, target * 2 * width, 2 * width, 1)
            pairs = [
                (g * heads + h, g * heads + (h ^ (2 * (g + groups * k)))) for g in range(groups) for h in range(heads)
            ]
            pieces.append(lax.ppermute(piece, ("grp", "head"), pairs))
        held = jnp.stack(pieces)
        own = lax.dynamic_slice_in_dim(held, core * width, width, 2)
        other = across(lax.dynamic_slice_in_dim(held, (1 - core) * width, width, 2), 1)
        both = jnp.concatenate([own, other], axis=1)
        return [both] + [over_groups(both, j) for j in range(1, groups)]

    def on_device(
        prefill_token_rows,
        decode_token_rows,
        input_weight,
        lowrank_weight,
        step_size_weight,
        adapter_up_weight,
        output_weight,
        head_decay_rate,
        head_step_bias,
        head_skip_scale,
        gated_norm_scale,
        prompt_start_state,
        prompt_at_position,
        slot_sample_index,
        prompt_adapter_index,
    ):
        head, group = lax.axis_index("head"), lax.axis_index("grp")
        where = jnp.stack([head, group]).astype(jnp.int32)
        owned = prompt_start_state.shape[0]
        slots = slot_sample_index.shape[0]
        start = prompt_start_state.reshape(owned, HEAD_DEV * HEAD_CHANNELS, STATE)
        decode_rows = decode_token_rows.reshape(STEPS * slots, decode_token_rows.shape[2])
        norm_scale = gated_norm_scale.reshape(1, HEAD_DEV * HEAD_CHANNELS)
        weights = weight_columns(output_weight, head, group)
        send, keep = project(
            where, prefill_token_rows, decode_rows, input_weight, lowrank_weight, step_size_weight,
            slot_sample_index, prompt_at_position, prompt_adapter_index, owned,
        )
        split = keep.shape[0]
        summed = jnp.concatenate([keep, send[split:]]) + across(send, 1)
        for distance in stages:
            half = split // 2
            outgoing = jnp.concatenate([summed[:half], summed[split:]]).astype(F16)
            summed = summed[half:] + across(outgoing, 2 * distance).astype(F32)
            split = half
        values, finals = end_states(
            where, summed, adapter_up_weight, head_step_bias, head_decay_rate, start,
            slot_sample_index, prompt_at_position, prompt_adapter_index,
        )
        all_finals = [finals] + [over_groups(finals, j) for j in range(1, groups)]
        prefill_normed, within = rows_within(
            where, summed, values, start, head_step_bias, head_decay_rate, head_skip_scale, norm_scale
        )
        normed = decode_rows_out(
            where, summed, within, prefill_normed, all_finals, head_step_bias, head_decay_rate, norm_scale,
            slot_sample_index, prompt_at_position,
        )
        near = normed[None]
        have = [0]
        for distance in reversed(stages):
            near = jnp.concatenate([near, across(near, 2 * distance)])
            have = have + [c ^ distance for c in have]
        near = jnp.concatenate([near[have.index(c)][None] for c in range(chips)])
        far = across(near, 1)
        prefill_out, decode_out = output_rows(where, near, far, weights, prefill_token_rows, decode_rows)
        return prefill_out, decode_out.reshape(decode_token_rows.shape)

    placed = (
        P("grp", "head"),
        P(None, "grp", "head"),
        P("head", None),
        P("head", None),
        P("head", None),
        P(None, "head"),
        P("head", None),
        P("head"),
        P("head"),
        P("head"),
        P("head"),
        P("grp", "head", None, None),
        P(),
        P("grp"),
        P(),
    )
    return jax.shard_map(
        on_device,
        mesh=mesh,
        in_specs=placed,
        out_specs=(P("grp", "head"), P(None, "grp", "head")),
        check_vma=False,
    )
```

```python
import itertools

import jax
import jax.numpy as jnp
from jax import lax
from jax.experimental import pallas as pl
from jax.experimental.pallas import tpu as pltpu
from jax.sharding import PartitionSpec as P

HEAD_CHANNELS = 64
STATE = 128
HEAD_DEV = 2
STRETCH = 32
SAMPLES = 16
STEPS = 3
ADAPTER_RANK = 16
LANES = 128
F32 = jnp.float32
BF16 = jnp.bfloat16
F16 = jnp.float16
EXACT = lax.Precision.HIGHEST
VMEM = pl.BlockSpec(memory_space=pltpu.VMEM)
BIG = 24 * 1024 * 1024


def mxu(a, b):
    return jnp.dot(a, b, preferred_element_type=F32)


def in_hbm(x):
    return pltpu.with_memory_space_constraint(x, pltpu.HBM)


def dot_nt(a, b):
    return lax.dot_general(a, b, (((1,), (1,)), ((), ())), precision=EXACT, preferred_element_type=F32)


def dot_tn(a, b):
    return lax.dot_general(a, b, (((0,), (0,)), ((), ())), precision=EXACT, preferred_element_type=F32)


def lane_ids(rows):
    return lax.broadcasted_iota(jnp.int32, (rows, LANES), 1)


def row_ids(rows, width=1):
    return lax.broadcasted_iota(jnp.int32, (rows, width), 0)


def as_row(ref):
    return ref[...].reshape(1, ref.shape[0])


def entry(row, at):
    lanes = lax.broadcasted_iota(jnp.int32, row.shape, 1)
    return jnp.sum(jnp.where(lanes == at, row, 0.0), axis=1, keepdims=True)


def numbers(ref):
    return as_row(ref).astype(F32)


def row_prompts(slots_ref, slots):
    row = (as_row(slots_ref) // SAMPLES).astype(F32)
    return jnp.sum(jnp.where(row_ids(slots, slots) == lax.broadcasted_iota(jnp.int32, (slots, slots), 1), row, 0.0), axis=1, keepdims=True)


def row_tenants(slots_ref, held_ref, tenants_ref, group, owned, slots):
    prompts = row_prompts(slots_ref, slots)
    tenants, held = numbers(tenants_ref), numbers(held_ref)
    lanes = lax.broadcasted_iota(jnp.int32, tenants.shape, 1).astype(F32)
    decode = jnp.sum(jnp.where(lanes == prompts, tenants, 0.0), axis=1, keepdims=True)
    prefill = []
    for i in range(owned):
        prompt = entry(held, group * owned + i)
        tenant = jnp.sum(jnp.where(lanes == prompt, tenants, 0.0), axis=1, keepdims=True)
        prefill.append(jnp.broadcast_to(tenant, (STRETCH, 1)))
    return jnp.concatenate(prefill + [decode] * STEPS, axis=0)


def tenant_lanes(rows):
    return (lane_ids(rows) // ADAPTER_RANK).astype(F32)


def place_order(chips):
    bits = chips.bit_length() - 1
    order = []
    for p in range(chips):
        j = chips - 1 - p
        order.append(sum(((j >> b) & 1) << (bits - 1 - b) for b in range(bits)))
    return order


def packing(rows, heads):
    lanes = ADAPTER_RANK + heads
    pack = 1
    while 2 * pack * lanes <= LANES and rows % (2 * pack * 8) == 0:
        pack *= 2
    return pack


def pack_rows(mixed, pack):
    part, span = mixed.shape[0] // pack, LANES // pack
    total = mixed[:part]
    for q in range(1, pack):
        total = total + pltpu.roll(mixed[q * part : (q + 1) * part], q * span, 1)
    return total


def unpack_rows(packed, pack):
    span = LANES // pack
    parts = [packed] + [pltpu.roll(packed, LANES - q * span, 1) for q in range(1, pack)]
    return jnp.concatenate(parts, axis=0)


def project(prefill_rows, decode_rows, input_weight, lowrank_weight, step_lines, slots, held, tenants, owned):
    rows_prefill, depth = prefill_rows.shape
    rows = rows_prefill + decode_rows.shape[0]
    width = 2 * HEAD_DEV * HEAD_CHANNELS
    pieces = width // LANES
    chips = input_weight.shape[1] // width // 2
    order = place_order(chips)
    low_blocks = 2 * STATE // LANES
    heads = step_lines.shape[0]
    pack = packing(rows, heads)
    packed = rows // pack
    base = chips * pieces * rows
    total = base + low_blocks * rows + packed
    slot_count = slots.shape[0]

    def fetches(up_ref, ud_ref, w_ref, u_ref, w_all, sems, odd):
        me = lax.axis_index("head")
        copies = [
            pltpu.make_async_copy(up_ref, u_ref.at[:rows_prefill], sems.at[0]),
            pltpu.make_async_copy(ud_ref, u_ref.at[rows_prefill:], sems.at[1]),
        ]
        for i in range(chips):
            column = pl.multiple_of(((order[i] * 2 + odd) ^ me) * width, width)
            copies.append(pltpu.make_async_copy(w_ref.at[:, pl.ds(column, width)], w_all.at[i], sems.at[2 + i]))
        return copies

    def products(copies, u_ref, w_all, o_ref):
        for i in range(chips):
            copies[2 + i].wait()
            part = mxu(u_ref[...], w_all[i])
            for k in range(pieces):
                at = (i * pieces + k) * rows
                o_ref[at : at + rows] = part[:, k * LANES : (k + 1) * LANES]

    def send_body(
        slots_hbm, held_hbm, tenants_hbm, up_ref, ud_ref, w_ref, l_ref, s_ref, o_ref,
        u_ref, w_all, l_all, s_all, m_ref, slots_ref, held_ref, tenants_ref, sems,
    ):
        copies = fetches(up_ref, ud_ref, w_ref, u_ref, w_all, sems, 1)
        low_copies = [
            pltpu.make_async_copy(l_ref, l_all, sems.at[2 + chips]),
            pltpu.make_async_copy(s_ref, s_all, sems.at[3 + chips]),
        ]
        index_copies = [
            pltpu.make_async_copy(slots_hbm, slots_ref, sems.at[4 + chips]),
            pltpu.make_async_copy(held_hbm, held_ref, sems.at[5 + chips]),
            pltpu.make_async_copy(tenants_hbm, tenants_ref, sems.at[6 + chips]),
        ]
        for copy in index_copies + copies[:2] + low_copies + copies[2:]:
            copy.start()
        for copy in index_copies:
            copy.wait()
        lanes = tenant_lanes(rows)
        mine = lanes == row_tenants(slots_ref, held_ref, tenants_ref, lax.axis_index("grp"), owned, slot_count)
        for copy in copies[:2] + low_copies:
            copy.wait()
        low = mxu(u_ref[...], l_all[...])
        for k in range(low_blocks):
            o_ref[base + k * rows : base + (k + 1) * rows] = low[:, k * LANES : (k + 1) * LANES]
        picked = jnp.where(mine, low[:, 2 * STATE :], 0.0)
        shift = LANES // 2
        while shift >= ADAPTER_RANK:
            picked = picked + pltpu.roll(picked, shift, 1)
            shift //= 2
        m_ref[...] = jnp.where(lane_ids(rows) < ADAPTER_RANK, picked, 0.0)
        m_ref[:, ADAPTER_RANK : ADAPTER_RANK + heads] = lax.dot_general(
            u_ref[...], s_all[...], (((1,), (1,)), ((), ())), preferred_element_type=F32
        )
        o_ref[base + low_blocks * rows :] = pack_rows(m_ref[...], pack)
        products(copies, u_ref, w_all, o_ref)

    def keep_body(up_ref, ud_ref, w_ref, o_ref, u_ref, w_all, sems):
        copies = fetches(up_ref, ud_ref, w_ref, u_ref, w_all, sems, 0)
        for copy in copies:
            copy.start()
        for copy in copies[:2]:
            copy.wait()
        products(copies, u_ref, w_all, o_ref)

    hbm = pl.BlockSpec(memory_space=pltpu.HBM)
    scratch = [pltpu.VMEM((rows, depth), BF16), pltpu.VMEM((chips, depth, width), BF16)]
    cost = pl.CostEstimate(
        flops=2 * rows * depth * width * chips, bytes_accessed=2 * depth * width * chips, transcendentals=0
    )
    params = pltpu.CompilerParams(vmem_limit_bytes=BIG)
    send = pl.pallas_call(
        send_body,
        out_shape=jax.ShapeDtypeStruct((total, LANES), F32),
        in_specs=[hbm] * 8,
        out_specs=VMEM,
        scratch_shapes=scratch
        + [
            pltpu.VMEM(lowrank_weight.shape, BF16),
            pltpu.VMEM(step_lines.shape, BF16),
            pltpu.VMEM((rows, LANES), F32),
            pltpu.VMEM(slots.shape, jnp.int32),
            pltpu.VMEM(held.shape, jnp.int32),
            pltpu.VMEM(tenants.shape, jnp.int32),
            pltpu.SemaphoreType.DMA((chips + 7,)),
        ],
        compiler_params=params,
        cost_estimate=cost,
    )(
        *[
            in_hbm(x)
            for x in (slots, held, tenants, prefill_rows, decode_rows, input_weight, lowrank_weight, step_lines)
        ]
    )
    keep = pl.pallas_call(
        keep_body,
        out_shape=jax.ShapeDtypeStruct((base, LANES), F32),
        in_specs=[hbm] * 3,
        out_specs=VMEM,
        scratch_shapes=scratch + [pltpu.SemaphoreType.DMA((chips + 2,))],
        compiler_params=params,
        cost_estimate=cost,
    )(*[in_hbm(x) for x in (prefill_rows, decode_rows, input_weight)])
    return send, keep


def line_load(route):
    steps = [0] * (2 * len(route))
    for a, b in enumerate(route):
        for link in range(min(a, b), max(a, b)):
            steps[2 * link + (a < b)] += 1
    return max(steps)


def chip_routes(chips, groups):
    wanted = [tuple(z ^ shift for z in range(chips)) for shift in range(chips)]
    if chips <= 4:
        ranked = sorted(itertools.permutations(range(chips)), key=lambda route: (line_load(route), route))

        def fill(rows, most):
            if len(rows) == chips:
                return rows
            for route in ranked:
                if line_load(route) <= most and all(a != b for row in rows for a, b in zip(row, route)):
                    found = fill(rows + [route], most)
                    if found:
                        return found
            return None

        for most in range(chips + 1):
            found = fill([], most)
            if found:
                wanted = found
                break
    return [wanted[groups * k : groups * (k + 1)] for k in range(chips // groups)]


def piece(x_ref, k, rows, at=slice(None)):
    low, high, _ = at.indices(rows)
    return x_ref[k * rows + low : k * rows + high]


def mixed_rows(x_ref, rows):
    return unpack_rows(x_ref[4 * rows :], rows // (x_ref.shape[0] - 4 * rows))


def looked_up(table, group, chip):
    found = jnp.int32(0)
    for g, row in enumerate(table):
        for z, value in enumerate(row):
            found = jnp.where((group == g) & (chip == z), value, found)
    return found


def weight_pieces(output_weight, routes, heads):
    own_rows, all_width = output_weight.shape
    width = all_width // heads
    count = len(routes)

    def body(w_ref, o_ref, sems):
        group, head = lax.axis_index("grp"), lax.axis_index("head")
        copies = []
        for k, rows in enumerate(routes):
            target = looked_up(rows, group, head // 2)
            for side in range(2):
                column = pl.multiple_of((2 * target + ((head % 2) ^ side)) * width, width)
                copies.append(
                    pltpu.make_async_copy(w_ref.at[:, pl.ds(column, width)], o_ref.at[k, side], sems.at[2 * k + side])
                )
        for copy in copies:
            copy.start()
        for copy in copies:
            copy.wait()

    return pl.pallas_call(
        body,
        out_shape=jax.ShapeDtypeStruct((count, 2, own_rows, width), BF16),
        in_specs=[pl.BlockSpec(memory_space=pltpu.HBM)],
        out_specs=VMEM,
        scratch_shapes=[pltpu.SemaphoreType.DMA((2 * count,))],
        compiler_params=pltpu.CompilerParams(vmem_limit_bytes=BIG),
    )(in_hbm(output_weight))


def step_lengths(mixed, bias_ref):
    lanes = lane_ids(mixed.shape[0])
    me = lax.axis_index("head")
    bias = as_row(bias_ref)
    lengths = []
    for h in range(HEAD_DEV):
        raw = jnp.sum(jnp.where(lanes == ADAPTER_RANK + me * HEAD_DEV + h, mixed, 0.0), axis=1, keepdims=True)
        raw = raw + bias[:, h : h + 1]
        lengths.append(jnp.maximum(raw, 0.0) + jnp.log1p(jnp.exp(-jnp.abs(raw))))
    return lengths


def by_head(first, second, rows):
    return jnp.where(lane_ids(rows) < HEAD_CHANNELS, first, second)


def prefill_decay(lengths, rate_ref, rows):
    t_at = lax.broadcasted_iota(jnp.int32, (rows, rows), 0)
    s_at = lax.broadcasted_iota(jnp.int32, (rows, rows), 1)
    same = t_at // STRETCH == s_at // STRETCH
    columns, lines, steps = [], [], []
    rate = as_row(rate_ref)
    for h in range(HEAD_DEV):
        length = lengths[h][:rows]
        decay = -(length * rate[:, h : h + 1])
        line = jnp.sum(jnp.where(same & (t_at <= s_at), decay, 0.0), axis=0, keepdims=True)
        lines.append(line)
        columns.append(jnp.sum(jnp.where(t_at == s_at, line, 0.0), axis=1, keepdims=True))
        steps.append(jnp.sum(jnp.where(t_at == s_at, length, 0.0), axis=0, keepdims=True))
    return columns, lines, steps, same & (t_at >= s_at)


def end_states(rows, summed, adapter_up, bias, rate, start, slots, held, tenants):
    owned = start.shape[0]
    prefill = owned * STRETCH
    slot_count = slots.shape[0]

    def body(slots_ref, held_ref, tenants_ref, bias_ref, rate_ref, x_ref, a_ref, s_ref, v_ref, f_ref):
        group = lax.axis_index("grp")
        mixed = mixed_rows(x_ref, rows)
        lanes = lane_ids(rows)
        mine = tenant_lanes(rows) == row_tenants(slots_ref, held_ref, tenants_ref, group, owned, slot_count)
        picked = jnp.where(lanes < ADAPTER_RANK, mixed, 0.0)
        shift = ADAPTER_RANK
        while shift < LANES:
            picked = picked + pltpu.roll(picked, shift, 1)
            shift *= 2
        picked = jnp.where(mine, picked, 0.0).astype(BF16)
        values = by_head(piece(x_ref, 0, rows), pltpu.roll(piece(x_ref, 1, rows), HEAD_CHANNELS, 1), rows)
        values = values + mxu(picked, a_ref[...])
        v_ref[...] = values
        lengths = step_lengths(mixed[:prefill], bias_ref)
        columns, _, _, _ = prefill_decay(lengths, rate_ref, prefill)
        for i in range(owned):
            lo, hi = i * STRETCH, (i + 1) * STRETCH
            ends = [columns[h][hi - 1 : hi] for h in range(HEAD_DEV)]
            tails = [jnp.exp(ends[h] - columns[h][lo:hi]) * lengths[h][lo:hi] for h in range(HEAD_DEV)]
            added = dot_tn(by_head(tails[0], tails[1], STRETCH) * values[lo:hi], piece(x_ref, 2, rows, slice(lo, hi)))
            for h in range(HEAD_DEV):
                at = slice(h * HEAD_CHANNELS, (h + 1) * HEAD_CHANNELS)
                f_ref[i, at] = jnp.exp(ends[h]) * s_ref[i, at] + added[at]

    return pl.pallas_call(
        body,
        out_shape=(
            jax.ShapeDtypeStruct((rows, LANES), F32),
            jax.ShapeDtypeStruct((owned, LANES, STATE), F32),
        ),
        in_specs=[VMEM] * 8,
        out_specs=(VMEM, VMEM),
        compiler_params=pltpu.CompilerParams(vmem_limit_bytes=BIG),
    )(slots, held, tenants, bias, rate, summed, adapter_up, start)


def normalise(result, gate, scale_ref):
    gated = result * (gate * (1.0 / (1.0 + jnp.exp(-gate))))
    spread = jnp.mean(gated * gated, axis=1, keepdims=True)
    return (gated * lax.rsqrt(spread + 1e-05) * scale_ref[...]).astype(BF16)


def gates(x_ref, rows, at):
    first, second = piece(x_ref, 0, rows, at), piece(x_ref, 1, rows, at)
    return by_head(pltpu.roll(first, HEAD_CHANNELS, 1), second, first.shape[0])


def rows_within(summed, values, start, bias, rate, skip, norm_scale):
    rows = values.shape[0]
    owned = start.shape[0]
    prefill = owned * STRETCH
    slot_count = (rows - prefill) // STEPS

    def body(bias_ref, rate_ref, skip_ref, x_ref, v_ref, s_ref, g_ref, n_ref, y_ref):
        rate, skip = as_row(rate_ref), as_row(skip_ref)
        lengths = step_lengths(mixed_rows(x_ref, rows), bias_ref)
        columns, lines, steps, later = prefill_decay(lengths, rate_ref, prefill)
        now = slice(0, prefill)
        values = v_ref[now]
        scores = dot_nt(piece(x_ref, 3, rows, now), piece(x_ref, 2, rows, now))
        sums = []
        for h in range(HEAD_DEV):
            weights = jnp.where(later, jnp.exp(jnp.where(later, columns[h] - lines[h], 0.0)), 0.0) * steps[h]
            sums.append(jnp.dot(weights * scores, values, precision=EXACT, preferred_element_type=F32))
        result = by_head(sums[0], sums[1], prefill)
        carried = jnp.concatenate(
            [dot_nt(piece(x_ref, 3, rows, slice(i * STRETCH, (i + 1) * STRETCH)), s_ref[i]) for i in range(owned)], axis=0
        )
        kept = by_head(jnp.exp(columns[0]), jnp.exp(columns[1]), prefill)
        skipped = by_head(skip[:, :1], skip[:, 1:], prefill)
        result = result + kept * carried + skipped * values
        n_ref[...] = normalise(result, gates(x_ref, rows, now), g_ref)
        at = [slice(prefill + s * slot_count, prefill + (s + 1) * slot_count) for s in range(STEPS)]
        run = [[], []]
        for h in range(HEAD_DEV):
            total = jnp.zeros((slot_count, 1), F32)
            for s in range(STEPS):
                total = total - lengths[h][at[s]] * rate[:, h : h + 1]
                run[h].append(total)
        skipped = by_head(skip[:, :1], skip[:, 1:], slot_count)
        for s in range(STEPS):
            total = skipped * v_ref[at[s]]
            for u in range(s + 1):
                score = jnp.sum(piece(x_ref, 3, rows, at[s]) * piece(x_ref, 2, rows, at[u]), axis=1, keepdims=True)
                factor = [jnp.exp(run[h][s] - run[h][u]) * lengths[h][at[u]] * score for h in range(HEAD_DEV)]
                total = total + by_head(factor[0], factor[1], slot_count) * v_ref[at[u]]
            y_ref[s * slot_count : (s + 1) * slot_count] = total

    return pl.pallas_call(
        body,
        out_shape=(
            jax.ShapeDtypeStruct((prefill, LANES), BF16),
            jax.ShapeDtypeStruct((rows - prefill, LANES), F32),
        ),
        in_specs=[VMEM] * 7,
        out_specs=(VMEM, VMEM),
        compiler_params=pltpu.CompilerParams(vmem_limit_bytes=BIG),
    )(bias, rate, skip, summed, values, start, norm_scale)


def decode_rows_out(summed, within, prefill_normed, finals, bias, rate, norm_scale, slots, held):
    prefill = prefill_normed.shape[0]
    rows = prefill + within.shape[0]
    owned = finals[0].shape[0]
    slot_count = slots.shape[0]
    parts = len(finals)

    def body(slots_ref, held_ref, bias_ref, rate_ref, x_ref, y_ref, p_ref, g_ref, *rest):
        f_refs, n_ref = rest[:parts], rest[parts]
        group = lax.axis_index("grp")
        held, rate = numbers(held_ref), as_row(rate_ref)
        now = slice(prefill, rows)
        prompts = row_prompts(slots_ref, slot_count)
        prompts = jnp.concatenate([prompts] * STEPS, axis=0)
        reader = piece(x_ref, 3, rows, now)
        carried = jnp.zeros((rows - prefill, LANES), F32)
        for j in range(parts):
            for i in range(owned):
                mine = prompts == entry(held, (group ^ j) * owned + i)
                carried = carried + dot_nt(jnp.where(mine, reader, 0.0), f_refs[j][i])
        lengths = step_lengths(mixed_rows(x_ref, rows)[now], bias_ref)
        kept = []
        for h in range(HEAD_DEV):
            total = jnp.zeros((slot_count, 1), F32)
            runs = []
            for s in range(STEPS):
                total = total - lengths[h][s * slot_count : (s + 1) * slot_count] * rate[:, h : h + 1]
                runs.append(total)
            kept.append(jnp.exp(jnp.concatenate(runs, axis=0)))
        result = y_ref[...] + by_head(kept[0], kept[1], rows - prefill) * carried
        n_ref[:prefill] = p_ref[...]
        n_ref[prefill:] = normalise(result, gates(x_ref, rows, now), g_ref)

    return pl.pallas_call(
        body,
        out_shape=jax.ShapeDtypeStruct((rows, LANES), BF16),
        in_specs=[VMEM] * (8 + parts),
        out_specs=VMEM,
        compiler_params=pltpu.CompilerParams(vmem_limit_bytes=BIG),
    )(slots, held, bias, rate, summed, within, prefill_normed, norm_scale, *finals)


def output_rows(sources, near, far, weights, prefill_rows, decode_rows):
    chips, rows, _ = near.shape
    prefill, width = prefill_rows.shape
    parts = len(weights)
    per_part = chips // parts
    tile = width // 4 if width % 512 == 0 else width
    flat = [w for part in weights for w in part]

    def body(a_ref, b_ref, up_ref, ud_ref, *rest):
        w_refs, (op_ref, od_ref) = list(rest[: len(flat)]), rest[len(flat) :]
        total = jnp.zeros((rows, tile), F32)
        for j in range(parts):
            mine = [w_refs.pop(0) for _ in weights[j]]
            for k in range(per_part):
                chip = looked_up(sources[k], lax.axis_index("grp") ^ j, lax.axis_index("head") // 2)
                if len(mine) == 1:
                    pair = jnp.concatenate([a_ref[chip], b_ref[chip]], axis=1)
                    total = total + mxu(pair, mine[0][k].reshape(pair.shape[1], tile))
                else:
                    total = total + mxu(a_ref[chip], mine[0][k]) + mxu(b_ref[chip], mine[1][k])
        op_ref[...] = up_ref[...].astype(F32) + total[:prefill]
        od_ref[...] = ud_ref[...].astype(F32) + total[prefill:]

    def column(shape):
        return pl.BlockSpec(shape, lambda i, *_: (0,) * (len(shape) - 1) + (i,))

    def whole(shape):
        return pl.BlockSpec(shape, lambda i, *_: (0,) * len(shape))

    return pl.pallas_call(
        body,
        out_shape=(
            jax.ShapeDtypeStruct(prefill_rows.shape, F32),
            jax.ShapeDtypeStruct(decode_rows.shape, F32),
        ),
        grid=(width // tile,),
        in_specs=[whole(near.shape), whole(far.shape), column((prefill, tile)), column((rows - prefill, tile))]
        + [column(w.shape[:-1] + (tile,)) for w in flat],
        out_specs=(column((prefill, tile)), column((rows - prefill, tile))),
        compiler_params=pltpu.CompilerParams(vmem_limit_bytes=BIG),
    )(near, far, prefill_rows, decode_rows, *flat)


def solution(mesh):
    groups, heads = mesh.shape["grp"], mesh.shape["head"]
    chips = heads // 2
    stages = [1 << b for b in range(chips.bit_length() - 1)]

    def across(x, distance):
        return lax.ppermute(x, "head", [(i, i ^ distance) for i in range(heads)])

    def over_groups(x, distance):
        return lax.ppermute(x, "grp", [(i, i ^ distance) for i in range(groups)])

    routes = chip_routes(chips, groups)

    def weights_over_head(output_weight):
        pieces = weight_pieces(output_weight, routes, heads)
        parts = []
        for k, rows in enumerate(routes):
            pairs = [
                (g * heads + h, g * heads + 2 * rows[g][h // 2] + h % 2) for g in range(groups) for h in range(heads)
            ]
            parts.append(lax.ppermute(pieces[k], ("grp", "head"), pairs))
        return parts

    def weights_over_groups(parts):
        both = jnp.stack([piece.at[1].set(across(piece[1], 1)) for piece in parts])
        if groups != 4:
            return [(both,)] + [(over_groups(both, j),) for j in range(1, groups)]
        near, side = over_groups(both, 1), over_groups(both, 2)
        return [(both,), (near,), (side,), (over_groups(side[:, 0], 1), over_groups(near[:, 1], 2))]

    sources = [[[z ^ row.index(z) for z in range(chips)] for row in rows] for rows in routes]

    def on_device(
        prefill_token_rows,
        decode_token_rows,
        input_weight,
        lowrank_weight,
        step_size_weight,
        adapter_up_weight,
        output_weight,
        head_decay_rate,
        head_step_bias,
        head_skip_scale,
        gated_norm_scale,
        prompt_start_state,
        prompt_at_position,
        slot_sample_index,
        prompt_adapter_index,
    ):
        owned = prompt_start_state.shape[0]
        slots = slot_sample_index.shape[0]
        start = prompt_start_state.reshape(owned, HEAD_DEV * HEAD_CHANNELS, STATE)
        decode_rows = decode_token_rows.reshape(STEPS * slots, decode_token_rows.shape[2])
        norm_scale = gated_norm_scale.reshape(1, HEAD_DEV * HEAD_CHANNELS)
        parts = weights_over_head(output_weight)
        send, keep = project(
            prefill_token_rows, decode_rows, input_weight, lowrank_weight, step_size_weight.T,
            slot_sample_index, prompt_at_position, prompt_adapter_index, owned,
        )
        rows = prefill_token_rows.shape[0] + decode_rows.shape[0]
        split = keep.shape[0]
        summed = jnp.concatenate([keep, send[split:]]) + across(send, 1)
        for distance in stages:
            half = split // 2
            outgoing = jnp.concatenate([summed[:half], summed[split:]]).astype(F16)
            summed = summed[half:] + across(outgoing, 2 * distance).astype(F32)
            split = half
        weights = weights_over_groups(parts)
        values, finals = end_states(
            rows, summed, adapter_up_weight, head_step_bias, head_decay_rate, start,
            slot_sample_index, prompt_at_position, prompt_adapter_index,
        )
        all_finals = [finals] + [over_groups(finals, j) for j in range(1, groups)]
        prefill_normed, within = rows_within(
            summed, values, start, head_step_bias, head_decay_rate, head_skip_scale, norm_scale
        )
        normed = decode_rows_out(
            summed, within, prefill_normed, all_finals, head_step_bias, head_decay_rate, norm_scale,
            slot_sample_index, prompt_at_position,
        )
        near = normed[None]
        have = [0]
        for distance in reversed(stages):
            near = jnp.concatenate([near, across(near, 2 * distance)])
            have = have + [c ^ distance for c in have]
        near = jnp.concatenate([near[have.index(c)][None] for c in range(chips)])
        far = across(near, 1)
        prefill_out, decode_out = output_rows(sources, near, far, weights, prefill_token_rows, decode_rows)
        return prefill_out, decode_out.reshape(decode_token_rows.shape)

    placed = (
        P("grp", "head"),
        P(None, "grp", "head"),
        P("head", None),
        P("head", None),
        P("head", None),
        P(None, "head"),
        P("head", None),
        P("head"),
        P("head"),
        P("head"),
        P("head"),
        P("grp", "head", None, None),
        P(),
        P("grp"),
        P(),
    )
    return jax.shard_map(
        on_device,
        mesh=mesh,
        in_specs=placed,
        out_specs=(P("grp", "head"), P(None, "grp", "head")),
        check_vma=False,
    )
```

```python
import itertools

import jax
import jax.numpy as jnp
from jax import lax
from jax.experimental import pallas as pl
from jax.experimental.pallas import tpu as pltpu
from jax.sharding import PartitionSpec as P

HEAD_CHANNELS = 64
STATE = 128
HEAD_DEV = 2
STRETCH = 32
SAMPLES = 16
STEPS = 3
ADAPTER_RANK = 16
LANES = 128
F32 = jnp.float32
BF16 = jnp.bfloat16
F16 = jnp.float16
EXACT = lax.Precision.HIGHEST
VMEM = pl.BlockSpec(memory_space=pltpu.VMEM)
BIG = 24 * 1024 * 1024


def mxu(a, b):
    return jnp.dot(a, b, preferred_element_type=F32)


def in_hbm(x):
    return pltpu.with_memory_space_constraint(x, pltpu.HBM)


def dot_nt(a, b):
    return lax.dot_general(a, b, (((1,), (1,)), ((), ())), precision=EXACT, preferred_element_type=F32)


def dot_tn(a, b):
    return lax.dot_general(a, b, (((0,), (0,)), ((), ())), precision=EXACT, preferred_element_type=F32)


def lane_ids(rows):
    return lax.broadcasted_iota(jnp.int32, (rows, LANES), 1)


def row_ids(rows, width=1):
    return lax.broadcasted_iota(jnp.int32, (rows, width), 0)


def as_row(ref):
    return ref[...].reshape(1, ref.shape[0])


def entry(row, at):
    lanes = lax.broadcasted_iota(jnp.int32, row.shape, 1)
    return jnp.sum(jnp.where(lanes == at, row, 0.0), axis=1, keepdims=True)


def numbers(ref):
    return as_row(ref).astype(F32)


def row_prompts(slots_ref, slots):
    row = (as_row(slots_ref) // SAMPLES).astype(F32)
    return jnp.sum(jnp.where(row_ids(slots, slots) == lax.broadcasted_iota(jnp.int32, (slots, slots), 1), row, 0.0), axis=1, keepdims=True)


def row_tenants(slots_ref, held_ref, tenants_ref, group, owned, slots):
    prompts = row_prompts(slots_ref, slots)
    tenants, held = numbers(tenants_ref), numbers(held_ref)
    lanes = lax.broadcasted_iota(jnp.int32, tenants.shape, 1).astype(F32)
    decode = jnp.sum(jnp.where(lanes == prompts, tenants, 0.0), axis=1, keepdims=True)
    prefill = []
    for i in range(owned):
        prompt = entry(held, group * owned + i)
        tenant = jnp.sum(jnp.where(lanes == prompt, tenants, 0.0), axis=1, keepdims=True)
        prefill.append(jnp.broadcast_to(tenant, (STRETCH, 1)))
    return jnp.concatenate(prefill + [decode] * STEPS, axis=0)


def tenant_lanes(rows):
    return (lane_ids(rows) // ADAPTER_RANK).astype(F32)


def place_order(chips):
    bits = chips.bit_length() - 1
    order = []
    for p in range(chips):
        j = chips - 1 - p
        order.append(sum(((j >> b) & 1) << (bits - 1 - b) for b in range(bits)))
    return order


def packing(rows, heads):
    lanes = ADAPTER_RANK + heads
    pack = 1
    while 2 * pack * lanes <= LANES and rows % (2 * pack * 8) == 0:
        pack *= 2
    return pack


def pack_rows(mixed, pack):
    part, span = mixed.shape[0] // pack, LANES // pack
    total = mixed[:part]
    for q in range(1, pack):
        total = total + pltpu.roll(mixed[q * part : (q + 1) * part], q * span, 1)
    return total


def unpack_rows(packed, pack):
    span = LANES // pack
    parts = [packed] + [pltpu.roll(packed, LANES - q * span, 1) for q in range(1, pack)]
    return jnp.concatenate(parts, axis=0)


def project(
    routes, prefill_rows, decode_rows, input_weight, lowrank_weight, step_lines, slots, held, tenants, output_weight, owned
):
    rows_prefill, depth = prefill_rows.shape
    rows = rows_prefill + decode_rows.shape[0]
    width = 2 * HEAD_DEV * HEAD_CHANNELS
    pieces = width // LANES
    chips = input_weight.shape[1] // width // 2
    order = place_order(chips)
    low_blocks = 2 * STATE // LANES
    heads = step_lines.shape[0]
    pack = packing(rows, heads)
    packed = rows // pack
    base = chips * pieces * rows
    total = base + low_blocks * rows + packed
    slot_count = slots.shape[0]
    count = len(routes)
    column_width = output_weight.shape[1] // (2 * chips)

    def piece_copies(v_ref, p_ref, sems):
        group, head = lax.axis_index("grp"), lax.axis_index("head")
        copies = []
        for k, rows_of in enumerate(routes):
            target = looked_up(rows_of, group, head // 2)
            for side in range(2):
                column = pl.multiple_of((2 * target + ((head % 2) ^ side)) * column_width, column_width)
                copies.append(
                    pltpu.make_async_copy(
                        v_ref.at[:, pl.ds(column, column_width)], p_ref.at[k, side], sems.at[2 * k + side]
                    )
                )
        return copies

    def fetches(up_ref, ud_ref, w_ref, u_ref, w_all, sems, odd):
        me = lax.axis_index("head")
        copies = [
            pltpu.make_async_copy(up_ref, u_ref.at[:rows_prefill], sems.at[0]),
            pltpu.make_async_copy(ud_ref, u_ref.at[rows_prefill:], sems.at[1]),
        ]
        for i in range(chips):
            column = pl.multiple_of(((order[i] * 2 + odd) ^ me) * width, width)
            copies.append(pltpu.make_async_copy(w_ref.at[:, pl.ds(column, width)], w_all.at[i], sems.at[2 + i]))
        return copies

    def products(copies, u_ref, w_all, o_ref):
        for i in range(chips):
            copies[2 + i].wait()
            part = mxu(u_ref[...], w_all[i])
            for k in range(pieces):
                at = (i * pieces + k) * rows
                o_ref[at : at + rows] = part[:, k * LANES : (k + 1) * LANES]

    def send_body(
        slots_hbm, held_hbm, tenants_hbm, up_ref, ud_ref, w_ref, l_ref, s_ref, v_ref, o_ref, p_ref,
        u_ref, w_all, l_all, s_all, m_ref, slots_ref, held_ref, tenants_ref, sems, piece_sems,
    ):
        copies = fetches(up_ref, ud_ref, w_ref, u_ref, w_all, sems, 1)
        low_copies = [
            pltpu.make_async_copy(l_ref, l_all, sems.at[2 + chips]),
            pltpu.make_async_copy(s_ref, s_all, sems.at[3 + chips]),
        ]
        index_copies = [
            pltpu.make_async_copy(slots_hbm, slots_ref, sems.at[4 + chips]),
            pltpu.make_async_copy(held_hbm, held_ref, sems.at[5 + chips]),
            pltpu.make_async_copy(tenants_hbm, tenants_ref, sems.at[6 + chips]),
        ]
        moved = piece_copies(v_ref, p_ref, piece_sems)
        for copy in index_copies + copies[:2] + low_copies + copies[2:] + moved:
            copy.start()
        for copy in index_copies:
            copy.wait()
        lanes = tenant_lanes(rows)
        mine = lanes == row_tenants(slots_ref, held_ref, tenants_ref, lax.axis_index("grp"), owned, slot_count)
        for copy in copies[:2] + low_copies:
            copy.wait()
        low = mxu(u_ref[...], l_all[...])
        for k in range(low_blocks):
            o_ref[base + k * rows : base + (k + 1) * rows] = low[:, k * LANES : (k + 1) * LANES]
        picked = jnp.where(mine, low[:, 2 * STATE :], 0.0)
        shift = LANES // 2
        while shift >= ADAPTER_RANK:
            picked = picked + pltpu.roll(picked, shift, 1)
            shift //= 2
        m_ref[...] = jnp.where(lane_ids(rows) < ADAPTER_RANK, picked, 0.0)
        m_ref[:, ADAPTER_RANK : ADAPTER_RANK + heads] = lax.dot_general(
            u_ref[...], s_all[...], (((1,), (1,)), ((), ())), preferred_element_type=F32
        )
        o_ref[base + low_blocks * rows :] = pack_rows(m_ref[...], pack)
        products(copies, u_ref, w_all, o_ref)
        for copy in moved:
            copy.wait()

    def keep_body(up_ref, ud_ref, w_ref, o_ref, u_ref, w_all, sems):
        copies = fetches(up_ref, ud_ref, w_ref, u_ref, w_all, sems, 0)
        for copy in copies:
            copy.start()
        for copy in copies[:2]:
            copy.wait()
        products(copies, u_ref, w_all, o_ref)

    hbm = pl.BlockSpec(memory_space=pltpu.HBM)
    scratch = [pltpu.VMEM((rows, depth), BF16), pltpu.VMEM((chips, depth, width), BF16)]
    cost = pl.CostEstimate(
        flops=2 * rows * depth * width * chips, bytes_accessed=2 * depth * width * chips, transcendentals=0
    )
    params = pltpu.CompilerParams(vmem_limit_bytes=BIG)
    send, pieces_out = pl.pallas_call(
        send_body,
        out_shape=(
            jax.ShapeDtypeStruct((total, LANES), F32),
            jax.ShapeDtypeStruct((count, 2, output_weight.shape[0], column_width), BF16),
        ),
        in_specs=[hbm] * 9,
        out_specs=(VMEM, VMEM),
        scratch_shapes=scratch
        + [
            pltpu.VMEM(lowrank_weight.shape, BF16),
            pltpu.VMEM(step_lines.shape, BF16),
            pltpu.VMEM((rows, LANES), F32),
            pltpu.VMEM(slots.shape, jnp.int32),
            pltpu.VMEM(held.shape, jnp.int32),
            pltpu.VMEM(tenants.shape, jnp.int32),
            pltpu.SemaphoreType.DMA((chips + 7,)),
            pltpu.SemaphoreType.DMA((2 * count,)),
        ],
        compiler_params=params,
        cost_estimate=cost,
    )(
        *[
            in_hbm(x)
            for x in (
                slots, held, tenants, prefill_rows, decode_rows, input_weight, lowrank_weight, step_lines, output_weight
            )
        ]
    )
    keep = pl.pallas_call(
        keep_body,
        out_shape=jax.ShapeDtypeStruct((base, LANES), F32),
        in_specs=[hbm] * 3,
        out_specs=VMEM,
        scratch_shapes=scratch + [pltpu.SemaphoreType.DMA((chips + 2,))],
        compiler_params=params,
        cost_estimate=cost,
    )(*[in_hbm(x) for x in (prefill_rows, decode_rows, input_weight)])
    return send, keep, pieces_out


def line_load(route):
    steps = [0] * (2 * len(route))
    for a, b in enumerate(route):
        for link in range(min(a, b), max(a, b)):
            steps[2 * link + (a < b)] += 1
    return max(steps)


def chip_routes(chips, groups):
    wanted = [tuple(z ^ shift for z in range(chips)) for shift in range(chips)]
    if chips <= 4:
        ranked = sorted(itertools.permutations(range(chips)), key=lambda route: (line_load(route), route))

        def fill(rows, most):
            if len(rows) == chips:
                return rows
            for route in ranked:
                if line_load(route) <= most and all(a != b for row in rows for a, b in zip(row, route)):
                    found = fill(rows + [route], most)
                    if found:
                        return found
            return None

        for most in range(chips + 1):
            found = fill([], most)
            if found:
                wanted = found
                break
    return [wanted[groups * k : groups * (k + 1)] for k in range(chips // groups)]


def piece(x_ref, k, rows, at=slice(None)):
    low, high, _ = at.indices(rows)
    return x_ref[k * rows + low : k * rows + high]


def mixed_rows(x_ref, rows):
    return unpack_rows(x_ref[4 * rows :], rows // (x_ref.shape[0] - 4 * rows))


def piece(x_ref, k, rows, at=slice(None)):
    low, high, _ = at.indices(rows)
    return x_ref[k * rows + low : k * rows + high]


def mixed_rows(x_ref, rows):
    return unpack_rows(x_ref[4 * rows :], rows // (x_ref.shape[0] - 4 * rows))


def looked_up(table, group, chip):
    found = jnp.int32(0)
    for g, row in enumerate(table):
        for z, value in enumerate(row):
            found = jnp.where((group == g) & (chip == z), value, found)
    return found


def piece(x_ref, k, rows, at=slice(None)):
    low, high, _ = at.indices(rows)
    return x_ref[k * rows + low : k * rows + high]


def mixed_rows(x_ref, rows):
    return unpack_rows(x_ref[4 * rows :], rows // (x_ref.shape[0] - 4 * rows))


def looked_up(table, group, chip):
    found = jnp.int32(0)
    for g, row in enumerate(table):
        for z, value in enumerate(row):
            found = jnp.where((group == g) & (chip == z), value, found)
    return found


def weight_pieces(output_weight, routes, heads):
    own_rows, all_width = output_weight.shape
    width = all_width // heads
    count = len(routes)

    def body(w_ref, o_ref, sems):
        group, head = lax.axis_index("grp"), lax.axis_index("head")
        copies = []
        for k, rows in enumerate(routes):
            target = looked_up(rows, group, head // 2)
            for side in range(2):
                column = pl.multiple_of((2 * target + ((head % 2) ^ side)) * width, width)
                copies.append(
                    pltpu.make_async_copy(w_ref.at[:, pl.ds(column, width)], o_ref.at[k, side], sems.at[2 * k + side])
                )
        for copy in copies:
            copy.start()
        for copy in copies:
            copy.wait()

    return pl.pallas_call(
        body,
        out_shape=jax.ShapeDtypeStruct((count, 2, own_rows, width), BF16),
        in_specs=[pl.BlockSpec(memory_space=pltpu.HBM)],
        out_specs=VMEM,
        scratch_shapes=[pltpu.SemaphoreType.DMA((2 * count,))],
        compiler_params=pltpu.CompilerParams(vmem_limit_bytes=BIG),
    )(in_hbm(output_weight))


def step_lengths(mixed, bias_ref):
    lanes = lane_ids(mixed.shape[0])
    me = lax.axis_index("head")
    bias = as_row(bias_ref)
    lengths = []
    for h in range(HEAD_DEV):
        raw = jnp.sum(jnp.where(lanes == ADAPTER_RANK + me * HEAD_DEV + h, mixed, 0.0), axis=1, keepdims=True)
        raw = raw + bias[:, h : h + 1]
        lengths.append(jnp.maximum(raw, 0.0) + jnp.log1p(jnp.exp(-jnp.abs(raw))))
    return lengths


def by_head(first, second, rows):
    return jnp.where(lane_ids(rows) < HEAD_CHANNELS, first, second)


def prefill_decay(lengths, rate_ref, rows):
    t_at = lax.broadcasted_iota(jnp.int32, (rows, rows), 0)
    s_at = lax.broadcasted_iota(jnp.int32, (rows, rows), 1)
    same = t_at // STRETCH == s_at // STRETCH
    columns, lines, steps = [], [], []
    rate = as_row(rate_ref)
    for h in range(HEAD_DEV):
        length = lengths[h][:rows]
        decay = -(length * rate[:, h : h + 1])
        line = jnp.sum(jnp.where(same & (t_at <= s_at), decay, 0.0), axis=0, keepdims=True)
        lines.append(line)
        columns.append(jnp.sum(jnp.where(t_at == s_at, line, 0.0), axis=1, keepdims=True))
        steps.append(jnp.sum(jnp.where(t_at == s_at, length, 0.0), axis=0, keepdims=True))
    return columns, lines, steps, same & (t_at >= s_at)


def end_states(rows, summed, adapter_up, bias, rate, start, slots, held, tenants):
    owned = start.shape[0]
    prefill = owned * STRETCH
    slot_count = slots.shape[0]

    def body(slots_ref, held_ref, tenants_ref, bias_ref, rate_ref, x_ref, a_ref, s_ref, v_ref, f_ref):
        group = lax.axis_index("grp")
        mixed = mixed_rows(x_ref, rows)
        lanes = lane_ids(rows)
        mine = tenant_lanes(rows) == row_tenants(slots_ref, held_ref, tenants_ref, group, owned, slot_count)
        picked = jnp.where(lanes < ADAPTER_RANK, mixed, 0.0)
        shift = ADAPTER_RANK
        while shift < LANES:
            picked = picked + pltpu.roll(picked, shift, 1)
            shift *= 2
        picked = jnp.where(mine, picked, 0.0).astype(BF16)
        values = by_head(piece(x_ref, 0, rows), pltpu.roll(piece(x_ref, 1, rows), HEAD_CHANNELS, 1), rows)
        values = values + mxu(picked, a_ref[...])
        v_ref[...] = values
        lengths = step_lengths(mixed[:prefill], bias_ref)
        columns, _, _, _ = prefill_decay(lengths, rate_ref, prefill)
        for i in range(owned):
            lo, hi = i * STRETCH, (i + 1) * STRETCH
            ends = [columns[h][hi - 1 : hi] for h in range(HEAD_DEV)]
            tails = [jnp.exp(ends[h] - columns[h][lo:hi]) * lengths[h][lo:hi] for h in range(HEAD_DEV)]
            added = dot_tn(by_head(tails[0], tails[1], STRETCH) * values[lo:hi], piece(x_ref, 2, rows, slice(lo, hi)))
            for h in range(HEAD_DEV):
                at = slice(h * HEAD_CHANNELS, (h + 1) * HEAD_CHANNELS)
                f_ref[i, at] = jnp.exp(ends[h]) * s_ref[i, at] + added[at]

    return pl.pallas_call(
        body,
        out_shape=(
            jax.ShapeDtypeStruct((rows, LANES), F32),
            jax.ShapeDtypeStruct((owned, LANES, STATE), F32),
        ),
        in_specs=[VMEM] * 8,
        out_specs=(VMEM, VMEM),
        compiler_params=pltpu.CompilerParams(vmem_limit_bytes=BIG),
    )(slots, held, tenants, bias, rate, summed, adapter_up, start)


def normalise(result, gate, scale_ref):
    gated = result * (gate * (1.0 / (1.0 + jnp.exp(-gate))))
    spread = jnp.mean(gated * gated, axis=1, keepdims=True)
    return (gated * lax.rsqrt(spread + 1e-05) * scale_ref[...]).astype(BF16)


def gates(x_ref, rows, at):
    first, second = piece(x_ref, 0, rows, at), piece(x_ref, 1, rows, at)
    return by_head(pltpu.roll(first, HEAD_CHANNELS, 1), second, first.shape[0])


def rows_within(summed, values, start, bias, rate, skip, norm_scale):
    rows = values.shape[0]
    owned = start.shape[0]
    prefill = owned * STRETCH
    slot_count = (rows - prefill) // STEPS

    def body(bias_ref, rate_ref, skip_ref, x_ref, v_ref, s_ref, g_ref, n_ref, y_ref):
        rate, skip = as_row(rate_ref), as_row(skip_ref)
        lengths = step_lengths(mixed_rows(x_ref, rows), bias_ref)
        columns, lines, steps, later = prefill_decay(lengths, rate_ref, prefill)
        now = slice(0, prefill)
        values = v_ref[now]
        scores = dot_nt(piece(x_ref, 3, rows, now), piece(x_ref, 2, rows, now))
        sums = []
        for h in range(HEAD_DEV):
            weights = jnp.where(later, jnp.exp(jnp.where(later, columns[h] - lines[h], 0.0)), 0.0) * steps[h]
            sums.append(jnp.dot(weights * scores, values, precision=EXACT, preferred_element_type=F32))
        result = by_head(sums[0], sums[1], prefill)
        carried = jnp.concatenate(
            [dot_nt(piece(x_ref, 3, rows, slice(i * STRETCH, (i + 1) * STRETCH)), s_ref[i]) for i in range(owned)], axis=0
        )
        kept = by_head(jnp.exp(columns[0]), jnp.exp(columns[1]), prefill)
        skipped = by_head(skip[:, :1], skip[:, 1:], prefill)
        result = result + kept * carried + skipped * values
        n_ref[...] = normalise(result, gates(x_ref, rows, now), g_ref)
        at = [slice(prefill + s * slot_count, prefill + (s + 1) * slot_count) for s in range(STEPS)]
        run = [[], []]
        for h in range(HEAD_DEV):
            total = jnp.zeros((slot_count, 1), F32)
            for s in range(STEPS):
                total = total - lengths[h][at[s]] * rate[:, h : h + 1]
                run[h].append(total)
        skipped = by_head(skip[:, :1], skip[:, 1:], slot_count)
        for s in range(STEPS):
            total = skipped * v_ref[at[s]]
            for u in range(s + 1):
                score = jnp.sum(piece(x_ref, 3, rows, at[s]) * piece(x_ref, 2, rows, at[u]), axis=1, keepdims=True)
                factor = [jnp.exp(run[h][s] - run[h][u]) * lengths[h][at[u]] * score for h in range(HEAD_DEV)]
                total = total + by_head(factor[0], factor[1], slot_count) * v_ref[at[u]]
            y_ref[s * slot_count : (s + 1) * slot_count] = total

    return pl.pallas_call(
        body,
        out_shape=(
            jax.ShapeDtypeStruct((prefill, LANES), BF16),
            jax.ShapeDtypeStruct((rows - prefill, LANES), F32),
        ),
        in_specs=[VMEM] * 7,
        out_specs=(VMEM, VMEM),
        compiler_params=pltpu.CompilerParams(vmem_limit_bytes=BIG),
    )(bias, rate, skip, summed, values, start, norm_scale)


def decode_rows_out(summed, within, prefill_normed, finals, bias, rate, norm_scale, slots, held):
    prefill = prefill_normed.shape[0]
    rows = prefill + within.shape[0]
    owned = finals[0].shape[0]
    slot_count = slots.shape[0]
    parts = len(finals)

    def body(slots_ref, held_ref, bias_ref, rate_ref, x_ref, y_ref, p_ref, g_ref, *rest):
        f_refs, n_ref = rest[:parts], rest[parts]
        group = lax.axis_index("grp")
        held, rate = numbers(held_ref), as_row(rate_ref)
        now = slice(prefill, rows)
        prompts = row_prompts(slots_ref, slot_count)
        prompts = jnp.concatenate([prompts] * STEPS, axis=0)
        reader = piece(x_ref, 3, rows, now)
        carried = jnp.zeros((rows - prefill, LANES), F32)
        for j in range(parts):
            for i in range(owned):
                mine = prompts == entry(held, (group ^ j) * owned + i)
                carried = carried + dot_nt(jnp.where(mine, reader, 0.0), f_refs[j][i])
        lengths = step_lengths(mixed_rows(x_ref, rows)[now], bias_ref)
        kept = []
        for h in range(HEAD_DEV):
            total = jnp.zeros((slot_count, 1), F32)
            runs = []
            for s in range(STEPS):
                total = total - lengths[h][s * slot_count : (s + 1) * slot_count] * rate[:, h : h + 1]
                runs.append(total)
            kept.append(jnp.exp(jnp.concatenate(runs, axis=0)))
        result = y_ref[...] + by_head(kept[0], kept[1], rows - prefill) * carried
        n_ref[:prefill] = p_ref[...]
        n_ref[prefill:] = normalise(result, gates(x_ref, rows, now), g_ref)

    return pl.pallas_call(
        body,
        out_shape=jax.ShapeDtypeStruct((rows, LANES), BF16),
        in_specs=[VMEM] * (8 + parts),
        out_specs=VMEM,
        compiler_params=pltpu.CompilerParams(vmem_limit_bytes=BIG),
    )(slots, held, bias, rate, summed, within, prefill_normed, norm_scale, *finals)


def output_rows(sources, near, far, weights, prefill_rows, decode_rows):
    chips, rows, _ = near.shape
    prefill, width = prefill_rows.shape
    parts = len(weights)
    per_part = chips // parts
    tile = width // 4 if width % 512 == 0 else width
    flat = [w for part in weights for w in part]

    def body(a_ref, b_ref, up_ref, ud_ref, *rest):
        w_refs, (op_ref, od_ref) = list(rest[: len(flat)]), rest[len(flat) :]
        total = jnp.zeros((rows, tile), F32)
        for j in range(parts):
            mine = [w_refs.pop(0) for _ in weights[j]]
            for k in range(per_part):
                chip = looked_up(sources[k], lax.axis_index("grp") ^ j, lax.axis_index("head") // 2)
                if len(mine) == 1:
                    pair = jnp.concatenate([a_ref[chip], b_ref[chip]], axis=1)
                    total = total + mxu(pair, mine[0][k].reshape(pair.shape[1], tile))
                else:
                    total = total + mxu(a_ref[chip], mine[0][k]) + mxu(b_ref[chip], mine[1][k])
        op_ref[...] = up_ref[...].astype(F32) + total[:prefill]
        od_ref[...] = ud_ref[...].astype(F32) + total[prefill:]

    def column(shape):
        return pl.BlockSpec(shape, lambda i, *_: (0,) * (len(shape) - 1) + (i,))

    def whole(shape):
        return pl.BlockSpec(shape, lambda i, *_: (0,) * len(shape))

    return pl.pallas_call(
        body,
        out_shape=(
            jax.ShapeDtypeStruct(prefill_rows.shape, F32),
            jax.ShapeDtypeStruct(decode_rows.shape, F32),
        ),
        grid=(width // tile,),
        in_specs=[whole(near.shape), whole(far.shape), column((prefill, tile)), column((rows - prefill, tile))]
        + [column(w.shape[:-1] + (tile,)) for w in flat],
        out_specs=(column((prefill, tile)), column((rows - prefill, tile))),
        compiler_params=pltpu.CompilerParams(vmem_limit_bytes=BIG),
    )(near, far, prefill_rows, decode_rows, *flat)


def solution(mesh):
    groups, heads = mesh.shape["grp"], mesh.shape["head"]
    chips = heads // 2
    stages = [1 << b for b in range(chips.bit_length() - 1)]

    def across(x, distance):
        return lax.ppermute(x, "head", [(i, i ^ distance) for i in range(heads)])

    def over_groups(x, distance):
        return lax.ppermute(x, "grp", [(i, i ^ distance) for i in range(groups)])

    routes = chip_routes(chips, groups)

    def weights_over_head(pieces):
        parts = []
        for k, rows in enumerate(routes):
            pairs = [
                (g * heads + h, g * heads + 2 * rows[g][h // 2] + h % 2) for g in range(groups) for h in range(heads)
            ]
            crossed = [(a, b ^ 1) for a, b in pairs]
            parts.append(
                jnp.stack(
                    [lax.ppermute(pieces[k, 0], ("grp", "head"), pairs), lax.ppermute(pieces[k, 1], ("grp", "head"), crossed)]
                )
            )
        return parts

    def weights_over_groups(parts, summed):
        both = jnp.stack(parts)
        if groups != 4:
            return [(both,)] + [(over_groups(both, j),) for j in range(1, groups)], summed
        near, side = over_groups(both, 1), over_groups(both, 2)
        summed, near, side = lax.optimization_barrier((summed, near, side))
        return [(both,), (near,), (side,), (over_groups(side[:, 0], 1), over_groups(near[:, 1], 2))], summed

    sources = [[[z ^ row.index(z) for z in range(chips)] for row in rows] for rows in routes]

    def on_device(
        prefill_token_rows,
        decode_token_rows,
        input_weight,
        lowrank_weight,
        step_size_weight,
        adapter_up_weight,
        output_weight,
        head_decay_rate,
        head_step_bias,
        head_skip_scale,
        gated_norm_scale,
        prompt_start_state,
        prompt_at_position,
        slot_sample_index,
        prompt_adapter_index,
    ):
        owned = prompt_start_state.shape[0]
        slots = slot_sample_index.shape[0]
        start = prompt_start_state.reshape(owned, HEAD_DEV * HEAD_CHANNELS, STATE)
        decode_rows = decode_token_rows.reshape(STEPS * slots, decode_token_rows.shape[2])
        norm_scale = gated_norm_scale.reshape(1, HEAD_DEV * HEAD_CHANNELS)
        send, keep, pieces = project(
            routes, prefill_token_rows, decode_rows, input_weight, lowrank_weight, step_size_weight.T,
            slot_sample_index, prompt_at_position, prompt_adapter_index, output_weight, owned,
        )
        parts = weights_over_head(pieces)
        rows = prefill_token_rows.shape[0] + decode_rows.shape[0]
        split = keep.shape[0]
        summed = jnp.concatenate([keep, send[split:]]) + across(send, 1)
        for distance in stages:
            half = split // 2
            outgoing = jnp.concatenate([summed[:half], summed[split:]]).astype(F16)
            summed = summed[half:] + across(outgoing, 2 * distance).astype(F32)
            split = half
        weights, summed = weights_over_groups(parts, summed)
        values, finals = end_states(
            rows, summed, adapter_up_weight, head_step_bias, head_decay_rate, start,
            slot_sample_index, prompt_at_position, prompt_adapter_index,
        )
        all_finals = [finals] + [over_groups(finals, j) for j in range(1, groups)]
        prefill_normed, within = rows_within(
            summed, values, start, head_step_bias, head_decay_rate, head_skip_scale, norm_scale
        )
        normed = decode_rows_out(
            summed, within, prefill_normed, all_finals, head_step_bias, head_decay_rate, norm_scale,
            slot_sample_index, prompt_at_position,
        )
        near = normed[None]
        have = [0]
        for distance in reversed(stages):
            near = jnp.concatenate([near, across(near, 2 * distance)])
            have = have + [c ^ distance for c in have]
        near = jnp.concatenate([near[have.index(c)][None] for c in range(chips)])
        far = across(near, 1)
        prefill_out, decode_out = output_rows(sources, near, far, weights, prefill_token_rows, decode_rows)
        return prefill_out, decode_out.reshape(decode_token_rows.shape)

    placed = (
        P("grp", "head"),
        P(None, "grp", "head"),
        P("head", None),
        P("head", None),
        P("head", None),
        P(None, "head"),
        P("head", None),
        P("head"),
        P("head"),
        P("head"),
        P("head"),
        P("grp", "head", None, None),
        P(),
        P("grp"),
        P(),
    )
    return jax.shard_map(
        on_device,
        mesh=mesh,
        in_specs=placed,
        out_specs=(P("grp", "head"), P(None, "grp", "head")),
        check_vma=False,
    )
```

```python
import itertools

import jax
import jax.numpy as jnp
from jax import lax
from jax.experimental import pallas as pl
from jax.experimental.pallas import tpu as pltpu
from jax.sharding import PartitionSpec as P

HEAD_CHANNELS = 64
STATE = 128
HEAD_DEV = 2
STRETCH = 32
SAMPLES = 16
STEPS = 3
ADAPTER_RANK = 16
LANES = 128
F32 = jnp.float32
BF16 = jnp.bfloat16
F16 = jnp.float16
EXACT = lax.Precision.HIGHEST
VMEM = pl.BlockSpec(memory_space=pltpu.VMEM)
BIG = 24 * 1024 * 1024


def mxu(a, b):
    return jnp.dot(a, b, preferred_element_type=F32)


def in_hbm(x):
    return pltpu.with_memory_space_constraint(x, pltpu.HBM)


def dot_nt(a, b):
    return lax.dot_general(a, b, (((1,), (1,)), ((), ())), precision=EXACT, preferred_element_type=F32)


def dot_tn(a, b):
    return lax.dot_general(a, b, (((0,), (0,)), ((), ())), precision=EXACT, preferred_element_type=F32)


def lane_ids(rows):
    return lax.broadcasted_iota(jnp.int32, (rows, LANES), 1)


def row_ids(rows, width=1):
    return lax.broadcasted_iota(jnp.int32, (rows, width), 0)


def as_row(ref):
    return ref[...].reshape(1, ref.shape[0])


def entry(row, at):
    lanes = lax.broadcasted_iota(jnp.int32, row.shape, 1)
    return jnp.sum(jnp.where(lanes == at, row, 0.0), axis=1, keepdims=True)


def numbers(ref):
    return as_row(ref).astype(F32)


def row_prompts(slots_ref, slots):
    row = (as_row(slots_ref) // SAMPLES).astype(F32)
    return jnp.sum(jnp.where(row_ids(slots, slots) == lax.broadcasted_iota(jnp.int32, (slots, slots), 1), row, 0.0), axis=1, keepdims=True)


def row_tenants(slots_ref, held_ref, tenants_ref, group, owned, slots):
    prompts = row_prompts(slots_ref, slots)
    tenants, held = numbers(tenants_ref), numbers(held_ref)
    lanes = lax.broadcasted_iota(jnp.int32, tenants.shape, 1).astype(F32)
    decode = jnp.sum(jnp.where(lanes == prompts, tenants, 0.0), axis=1, keepdims=True)
    prefill = []
    for i in range(owned):
        prompt = entry(held, group * owned + i)
        tenant = jnp.sum(jnp.where(lanes == prompt, tenants, 0.0), axis=1, keepdims=True)
        prefill.append(jnp.broadcast_to(tenant, (STRETCH, 1)))
    return jnp.concatenate(prefill + [decode] * STEPS, axis=0)


def tenant_lanes(rows):
    return (lane_ids(rows) // ADAPTER_RANK).astype(F32)


def place_order(chips):
    bits = chips.bit_length() - 1
    order = []
    for p in range(chips):
        j = chips - 1 - p
        order.append(sum(((j >> b) & 1) << (bits - 1 - b) for b in range(bits)))
    return order


def packing(rows, heads):
    lanes = ADAPTER_RANK + heads
    pack = 1
    while 2 * pack * lanes <= LANES and rows % (2 * pack * 8) == 0:
        pack *= 2
    return pack


def pack_rows(mixed, pack):
    part, span = mixed.shape[0] // pack, LANES // pack
    total = mixed[:part]
    for q in range(1, pack):
        total = total + pltpu.roll(mixed[q * part : (q + 1) * part], q * span, 1)
    return total


def unpack_rows(packed, pack):
    span = LANES // pack
    parts = [packed] + [pltpu.roll(packed, LANES - q * span, 1) for q in range(1, pack)]
    return jnp.concatenate(parts, axis=0)


def project(
    routes, prefill_rows, decode_rows, input_weight, lowrank_weight, step_lines, slots, held, tenants, output_weight, owned
):
    rows_prefill, depth = prefill_rows.shape
    rows = rows_prefill + decode_rows.shape[0]
    width = 2 * HEAD_DEV * HEAD_CHANNELS
    pieces = width // LANES
    chips = input_weight.shape[1] // width // 2
    order = place_order(chips)
    low_blocks = 2 * STATE // LANES
    heads = step_lines.shape[0]
    pack = packing(rows, heads)
    packed = rows // pack
    base = chips * pieces * rows
    total = base + low_blocks * rows + packed
    slot_count = slots.shape[0]
    count = len(routes)
    column_width = output_weight.shape[1] // (2 * chips)

    def piece_copies(v_ref, p_ref, sems):
        group, head = lax.axis_index("grp"), lax.axis_index("head")
        copies = []
        for k, rows_of in enumerate(routes):
            target = looked_up(rows_of, group, head // 2)
            for side in range(2):
                column = pl.multiple_of((2 * target + ((head % 2) ^ side)) * column_width, column_width)
                copies.append(
                    pltpu.make_async_copy(
                        v_ref.at[:, pl.ds(column, column_width)], p_ref.at[k, side], sems.at[2 * k + side]
                    )
                )
        return copies

    def fetches(up_ref, ud_ref, w_ref, u_ref, w_all, sems, odd):
        me = lax.axis_index("head")
        copies = [
            pltpu.make_async_copy(up_ref, u_ref.at[:rows_prefill], sems.at[0]),
            pltpu.make_async_copy(ud_ref, u_ref.at[rows_prefill:], sems.at[1]),
        ]
        for i in range(chips):
            column = pl.multiple_of(((order[i] * 2 + odd) ^ me) * width, width)
            copies.append(pltpu.make_async_copy(w_ref.at[:, pl.ds(column, width)], w_all.at[i], sems.at[2 + i]))
        return copies

    def products(copies, u_ref, w_all, o_ref):
        for i in range(chips):
            copies[2 + i].wait()
            part = mxu(u_ref[...], w_all[i])
            for k in range(pieces):
                at = (i * pieces + k) * rows
                o_ref[at : at + rows] = part[:, k * LANES : (k + 1) * LANES]

    def send_body(
        slots_hbm, held_hbm, tenants_hbm, up_ref, ud_ref, w_ref, l_ref, s_ref, v_ref, o_ref, p_ref,
        u_ref, w_all, l_all, s_all, m_ref, slots_ref, held_ref, tenants_ref, sems, piece_sems,
    ):
        copies = fetches(up_ref, ud_ref, w_ref, u_ref, w_all, sems, 1)
        low_copies = [
            pltpu.make_async_copy(l_ref, l_all, sems.at[2 + chips]),
            pltpu.make_async_copy(s_ref, s_all, sems.at[3 + chips]),
        ]
        index_copies = [
            pltpu.make_async_copy(slots_hbm, slots_ref, sems.at[4 + chips]),
            pltpu.make_async_copy(held_hbm, held_ref, sems.at[5 + chips]),
            pltpu.make_async_copy(tenants_hbm, tenants_ref, sems.at[6 + chips]),
        ]
        moved = piece_copies(v_ref, p_ref, piece_sems)
        for copy in index_copies + copies[:2] + low_copies + copies[2:] + moved:
            copy.start()
        for copy in index_copies:
            copy.wait()
        lanes = tenant_lanes(rows)
        mine = lanes == row_tenants(slots_ref, held_ref, tenants_ref, lax.axis_index("grp"), owned, slot_count)
        for copy in copies[:2] + low_copies:
            copy.wait()
        low = mxu(u_ref[...], l_all[...])
        for k in range(low_blocks):
            o_ref[base + k * rows : base + (k + 1) * rows] = low[:, k * LANES : (k + 1) * LANES]
        picked = jnp.where(mine, low[:, 2 * STATE :], 0.0)
        shift = LANES // 2
        while shift >= ADAPTER_RANK:
            picked = picked + pltpu.roll(picked, shift, 1)
            shift //= 2
        m_ref[...] = jnp.where(lane_ids(rows) < ADAPTER_RANK, picked, 0.0)
        m_ref[:, ADAPTER_RANK : ADAPTER_RANK + heads] = lax.dot_general(
            u_ref[...], s_all[...], (((1,), (1,)), ((), ())), preferred_element_type=F32
        )
        o_ref[base + low_blocks * rows :] = pack_rows(m_ref[...], pack)
        products(copies, u_ref, w_all, o_ref)
        for copy in moved:
            copy.wait()

    def keep_body(up_ref, ud_ref, w_ref, o_ref, u_ref, w_all, sems):
        copies = fetches(up_ref, ud_ref, w_ref, u_ref, w_all, sems, 0)
        for copy in copies:
            copy.start()
        for copy in copies[:2]:
            copy.wait()
        products(copies, u_ref, w_all, o_ref)

    hbm = pl.BlockSpec(memory_space=pltpu.HBM)
    scratch = [pltpu.VMEM((rows, depth), BF16), pltpu.VMEM((chips, depth, width), BF16)]
    cost = pl.CostEstimate(
        flops=2 * rows * depth * width * chips, bytes_accessed=2 * depth * width * chips, transcendentals=0
    )
    params = pltpu.CompilerParams(vmem_limit_bytes=BIG)
    send, pieces_out = pl.pallas_call(
        send_body,
        out_shape=(
            jax.ShapeDtypeStruct((total, LANES), F32),
            jax.ShapeDtypeStruct((count, 2, output_weight.shape[0], column_width), BF16),
        ),
        in_specs=[hbm] * 9,
        out_specs=(VMEM, VMEM),
        scratch_shapes=scratch
        + [
            pltpu.VMEM(lowrank_weight.shape, BF16),
            pltpu.VMEM(step_lines.shape, BF16),
            pltpu.VMEM((rows, LANES), F32),
            pltpu.VMEM(slots.shape, jnp.int32),
            pltpu.VMEM(held.shape, jnp.int32),
            pltpu.VMEM(tenants.shape, jnp.int32),
            pltpu.SemaphoreType.DMA((chips + 7,)),
            pltpu.SemaphoreType.DMA((2 * count,)),
        ],
        compiler_params=params,
        cost_estimate=cost,
    )(
        *[
            in_hbm(x)
            for x in (
                slots, held, tenants, prefill_rows, decode_rows, input_weight, lowrank_weight, step_lines, output_weight
            )
        ]
    )
    keep = pl.pallas_call(
        keep_body,
        out_shape=jax.ShapeDtypeStruct((base, LANES), F32),
        in_specs=[hbm] * 3,
        out_specs=VMEM,
        scratch_shapes=scratch + [pltpu.SemaphoreType.DMA((chips + 2,))],
        compiler_params=params,
        cost_estimate=cost,
    )(*[in_hbm(x) for x in (prefill_rows, decode_rows, input_weight)])
    return send, keep, pieces_out


def line_load(route):
    steps = [0] * (2 * len(route))
    for a, b in enumerate(route):
        for link in range(min(a, b), max(a, b)):
            steps[2 * link + (a < b)] += 1
    return max(steps)


def chip_routes(chips, groups):
    wanted = [tuple(z ^ shift for z in range(chips)) for shift in range(chips)]
    if chips <= 4:
        ranked = sorted(itertools.permutations(range(chips)), key=lambda route: (line_load(route), route))

        def fill(rows, most):
            if len(rows) == chips:
                return rows
            for route in ranked:
                if line_load(route) <= most and all(a != b for row in rows for a, b in zip(row, route)):
                    found = fill(rows + [route], most)
                    if found:
                        return found
            return None

        for most in range(chips + 1):
            found = fill([], most)
            if found:
                wanted = found
                break
    return [wanted[groups * k : groups * (k + 1)] for k in range(chips // groups)]


def piece(x_ref, k, rows, at=slice(None)):
    low, high, _ = at.indices(rows)
    return x_ref[k * rows + low : k * rows + high]


def mixed_rows(x_ref, rows):
    return unpack_rows(x_ref[4 * rows :], rows // (x_ref.shape[0] - 4 * rows))


def piece(x_ref, k, rows, at=slice(None)):
    low, high, _ = at.indices(rows)
    return x_ref[k * rows + low : k * rows + high]


def mixed_rows(x_ref, rows):
    return unpack_rows(x_ref[4 * rows :], rows // (x_ref.shape[0] - 4 * rows))


def looked_up(table, group, chip):
    found = jnp.int32(0)
    for g, row in enumerate(table):
        for z, value in enumerate(row):
            found = jnp.where((group == g) & (chip == z), value, found)
    return found


def piece(x_ref, k, rows, at=slice(None)):
    low, high, _ = at.indices(rows)
    return x_ref[k * rows + low : k * rows + high]


def mixed_rows(x_ref, rows):
    return unpack_rows(x_ref[4 * rows :], rows // (x_ref.shape[0] - 4 * rows))


def looked_up(table, group, chip):
    found = jnp.int32(0)
    for g, row in enumerate(table):
        for z, value in enumerate(row):
            found = jnp.where((group == g) & (chip == z), value, found)
    return found


def weight_pieces(output_weight, routes, heads):
    own_rows, all_width = output_weight.shape
    width = all_width // heads
    count = len(routes)

    def body(w_ref, o_ref, sems):
        group, head = lax.axis_index("grp"), lax.axis_index("head")
        copies = []
        for k, rows in enumerate(routes):
            target = looked_up(rows, group, head // 2)
            for side in range(2):
                column = pl.multiple_of((2 * target + ((head % 2) ^ side)) * width, width)
                copies.append(
                    pltpu.make_async_copy(w_ref.at[:, pl.ds(column, width)], o_ref.at[k, side], sems.at[2 * k + side])
                )
        for copy in copies:
            copy.start()
        for copy in copies:
            copy.wait()

    return pl.pallas_call(
        body,
        out_shape=jax.ShapeDtypeStruct((count, 2, own_rows, width), BF16),
        in_specs=[pl.BlockSpec(memory_space=pltpu.HBM)],
        out_specs=VMEM,
        scratch_shapes=[pltpu.SemaphoreType.DMA((2 * count,))],
        compiler_params=pltpu.CompilerParams(vmem_limit_bytes=BIG),
    )(in_hbm(output_weight))


def step_lengths(mixed, bias_ref):
    lanes = lane_ids(mixed.shape[0])
    me = lax.axis_index("head")
    bias = as_row(bias_ref)
    lengths = []
    for h in range(HEAD_DEV):
        raw = jnp.sum(jnp.where(lanes == ADAPTER_RANK + me * HEAD_DEV + h, mixed, 0.0), axis=1, keepdims=True)
        raw = raw + bias[:, h : h + 1]
        lengths.append(jnp.maximum(raw, 0.0) + jnp.log1p(jnp.exp(-jnp.abs(raw))))
    return lengths


def by_head(first, second, rows):
    return jnp.where(lane_ids(rows) < HEAD_CHANNELS, first, second)


def prefill_decay(lengths, rate_ref, rows):
    t_at = lax.broadcasted_iota(jnp.int32, (rows, rows), 0)
    s_at = lax.broadcasted_iota(jnp.int32, (rows, rows), 1)
    same = t_at // STRETCH == s_at // STRETCH
    columns, lines, steps = [], [], []
    rate = as_row(rate_ref)
    for h in range(HEAD_DEV):
        length = lengths[h][:rows]
        decay = -(length * rate[:, h : h + 1])
        line = jnp.sum(jnp.where(same & (t_at <= s_at), decay, 0.0), axis=0, keepdims=True)
        lines.append(line)
        columns.append(jnp.sum(jnp.where(t_at == s_at, line, 0.0), axis=1, keepdims=True))
        steps.append(jnp.sum(jnp.where(t_at == s_at, length, 0.0), axis=0, keepdims=True))
    return columns, lines, steps, same & (t_at >= s_at)


def end_states(rows, summed, adapter_up, bias, rate, start, slots, held, tenants):
    owned = start.shape[0]
    prefill = owned * STRETCH
    slot_count = slots.shape[0]

    def body(slots_ref, held_ref, tenants_ref, bias_ref, rate_ref, x_ref, a_ref, s_ref, v_ref, f_ref):
        group = lax.axis_index("grp")
        mixed = mixed_rows(x_ref, rows)
        lanes = lane_ids(rows)
        mine = tenant_lanes(rows) == row_tenants(slots_ref, held_ref, tenants_ref, group, owned, slot_count)
        picked = jnp.where(lanes < ADAPTER_RANK, mixed, 0.0)
        shift = ADAPTER_RANK
        while shift < LANES:
            picked = picked + pltpu.roll(picked, shift, 1)
            shift *= 2
        picked = jnp.where(mine, picked, 0.0).astype(BF16)
        values = by_head(piece(x_ref, 0, rows), pltpu.roll(piece(x_ref, 1, rows), HEAD_CHANNELS, 1), rows)
        values = values + mxu(picked, a_ref[...])
        v_ref[...] = values
        lengths = step_lengths(mixed[:prefill], bias_ref)
        columns, _, _, _ = prefill_decay(lengths, rate_ref, prefill)
        for i in range(owned):
            lo, hi = i * STRETCH, (i + 1) * STRETCH
            ends = [columns[h][hi - 1 : hi] for h in range(HEAD_DEV)]
            tails = [jnp.exp(ends[h] - columns[h][lo:hi]) * lengths[h][lo:hi] for h in range(HEAD_DEV)]
            added = dot_tn(by_head(tails[0], tails[1], STRETCH) * values[lo:hi], piece(x_ref, 2, rows, slice(lo, hi)))
            for h in range(HEAD_DEV):
                at = slice(h * HEAD_CHANNELS, (h + 1) * HEAD_CHANNELS)
                f_ref[i, at] = jnp.exp(ends[h]) * s_ref[i, at] + added[at]

    return pl.pallas_call(
        body,
        out_shape=(
            jax.ShapeDtypeStruct((rows, LANES), F32),
            jax.ShapeDtypeStruct((owned, LANES, STATE), F32),
        ),
        in_specs=[VMEM] * 8,
        out_specs=(VMEM, VMEM),
        compiler_params=pltpu.CompilerParams(vmem_limit_bytes=BIG),
    )(slots, held, tenants, bias, rate, summed, adapter_up, start)


def normalise(result, gate, scale_ref):
    gated = result * (gate * (1.0 / (1.0 + jnp.exp(-gate))))
    spread = jnp.mean(gated * gated, axis=1, keepdims=True)
    return (gated * lax.rsqrt(spread + 1e-05) * scale_ref[...]).astype(BF16)


def gates(x_ref, rows, at):
    first, second = piece(x_ref, 0, rows, at), piece(x_ref, 1, rows, at)
    return by_head(pltpu.roll(first, HEAD_CHANNELS, 1), second, first.shape[0])


def rows_within(summed, values, start, bias, rate, skip, norm_scale):
    rows = values.shape[0]
    owned = start.shape[0]
    prefill = owned * STRETCH
    slot_count = (rows - prefill) // STEPS

    def body(bias_ref, rate_ref, skip_ref, x_ref, v_ref, s_ref, g_ref, n_ref, y_ref):
        rate, skip = as_row(rate_ref), as_row(skip_ref)
        lengths = step_lengths(mixed_rows(x_ref, rows), bias_ref)
        columns, lines, steps, later = prefill_decay(lengths, rate_ref, prefill)
        now = slice(0, prefill)
        values = v_ref[now]
        scores = dot_nt(piece(x_ref, 3, rows, now), piece(x_ref, 2, rows, now))
        sums = []
        for h in range(HEAD_DEV):
            weights = jnp.where(later, jnp.exp(jnp.where(later, columns[h] - lines[h], 0.0)), 0.0) * steps[h]
            sums.append(jnp.dot(weights * scores, values, precision=EXACT, preferred_element_type=F32))
        result = by_head(sums[0], sums[1], prefill)
        carried = jnp.concatenate(
            [dot_nt(piece(x_ref, 3, rows, slice(i * STRETCH, (i + 1) * STRETCH)), s_ref[i]) for i in range(owned)], axis=0
        )
        kept = by_head(jnp.exp(columns[0]), jnp.exp(columns[1]), prefill)
        skipped = by_head(skip[:, :1], skip[:, 1:], prefill)
        result = result + kept * carried + skipped * values
        n_ref[...] = normalise(result, gates(x_ref, rows, now), g_ref)
        at = [slice(prefill + s * slot_count, prefill + (s + 1) * slot_count) for s in range(STEPS)]
        run = [[], []]
        for h in range(HEAD_DEV):
            total = jnp.zeros((slot_count, 1), F32)
            for s in range(STEPS):
                total = total - lengths[h][at[s]] * rate[:, h : h + 1]
                run[h].append(total)
        skipped = by_head(skip[:, :1], skip[:, 1:], slot_count)
        for s in range(STEPS):
            total = skipped * v_ref[at[s]]
            for u in range(s + 1):
                score = jnp.sum(piece(x_ref, 3, rows, at[s]) * piece(x_ref, 2, rows, at[u]), axis=1, keepdims=True)
                factor = [jnp.exp(run[h][s] - run[h][u]) * lengths[h][at[u]] * score for h in range(HEAD_DEV)]
                total = total + by_head(factor[0], factor[1], slot_count) * v_ref[at[u]]
            y_ref[s * slot_count : (s + 1) * slot_count] = total

    return pl.pallas_call(
        body,
        out_shape=(
            jax.ShapeDtypeStruct((prefill, LANES), BF16),
            jax.ShapeDtypeStruct((rows - prefill, LANES), F32),
        ),
        in_specs=[VMEM] * 7,
        out_specs=(VMEM, VMEM),
        compiler_params=pltpu.CompilerParams(vmem_limit_bytes=BIG),
    )(bias, rate, skip, summed, values, start, norm_scale)


def decode_rows_out(summed, within, prefill_normed, finals, bias, rate, norm_scale, slots, held):
    prefill = prefill_normed.shape[0]
    rows = prefill + within.shape[0]
    owned = finals[0].shape[0]
    slot_count = slots.shape[0]
    parts = len(finals)

    def body(slots_ref, held_ref, bias_ref, rate_ref, x_ref, y_ref, p_ref, g_ref, *rest):
        f_refs, n_ref = rest[:parts], rest[parts]
        group = lax.axis_index("grp")
        held, rate = numbers(held_ref), as_row(rate_ref)
        now = slice(prefill, rows)
        prompts = row_prompts(slots_ref, slot_count)
        prompts = jnp.concatenate([prompts] * STEPS, axis=0)
        reader = piece(x_ref, 3, rows, now)
        carried = jnp.zeros((rows - prefill, LANES), F32)
        for j in range(parts):
            for i in range(owned):
                mine = prompts == entry(held, (group ^ j) * owned + i)
                carried = carried + dot_nt(jnp.where(mine, reader, 0.0), f_refs[j][i])
        lengths = step_lengths(mixed_rows(x_ref, rows)[now], bias_ref)
        kept = []
        for h in range(HEAD_DEV):
            total = jnp.zeros((slot_count, 1), F32)
            runs = []
            for s in range(STEPS):
                total = total - lengths[h][s * slot_count : (s + 1) * slot_count] * rate[:, h : h + 1]
                runs.append(total)
            kept.append(jnp.exp(jnp.concatenate(runs, axis=0)))
        result = y_ref[...] + by_head(kept[0], kept[1], rows - prefill) * carried
        n_ref[:prefill] = p_ref[...]
        n_ref[prefill:] = normalise(result, gates(x_ref, rows, now), g_ref)

    return pl.pallas_call(
        body,
        out_shape=jax.ShapeDtypeStruct((rows, LANES), BF16),
        in_specs=[VMEM] * (8 + parts),
        out_specs=VMEM,
        compiler_params=pltpu.CompilerParams(vmem_limit_bytes=BIG),
    )(slots, held, bias, rate, summed, within, prefill_normed, norm_scale, *finals)


def output_rows(sources, near, far, weights, prefill_rows, decode_rows):
    chips, rows, _ = near.shape
    prefill, width = prefill_rows.shape
    parts = len(weights)
    per_part = chips // parts
    tile = width // 4 if width % 512 == 0 else width
    tiles = width // tile
    flat = [w for part in weights for w in part]

    def body(a_ref, b_ref, up_ref, ud_ref, *rest):
        w_refs = rest[: len(flat)]
        op_ref, od_ref, total_ref, sems = rest[len(flat) :]
        lefts, rights, at = [], [], 0
        for j in range(parts):
            for k in range(per_part):
                chip = looked_up(sources[k], lax.axis_index("grp") ^ j, lax.axis_index("head") // 2)
                if len(weights[j]) == 1:
                    lefts.append(jnp.concatenate([a_ref[chip], b_ref[chip]], axis=1))
                    rights.append((w_refs[at], (k,), 2))
                else:
                    lefts.extend([a_ref[chip], b_ref[chip]])
                    rights.extend([(w_refs[at], (k,), 1), (w_refs[at + 1], (k,), 1)])
            at += len(weights[j])
        copies = []
        for t in range(tiles):
            columns = slice(t * tile, (t + 1) * tile)
            total = jnp.concatenate([up_ref[:, columns], ud_ref[:, columns]], axis=0).astype(F32)
            for left, (w_ref, (k,), cores) in zip(lefts, rights):
                if cores == 2:
                    total = total + mxu(left, w_ref[k, :, :, columns].reshape(left.shape[1], tile))
                else:
                    total = total + mxu(left, w_ref[k, :, columns])
            total_ref[t] = total
            copies.append(pltpu.make_async_copy(total_ref.at[t, :prefill], op_ref.at[:, columns], sems.at[2 * t]))
            copies.append(pltpu.make_async_copy(total_ref.at[t, prefill:], od_ref.at[:, columns], sems.at[2 * t + 1]))
            copies[-2].start()
            copies[-1].start()
        for copy in copies:
            copy.wait()

    return pl.pallas_call(
        body,
        out_shape=(
            jax.ShapeDtypeStruct(prefill_rows.shape, F32),
            jax.ShapeDtypeStruct(decode_rows.shape, F32),
        ),
        in_specs=[VMEM] * (4 + len(flat)),
        out_specs=(pl.BlockSpec(memory_space=pltpu.HBM),) * 2,
        scratch_shapes=[pltpu.VMEM((tiles, rows, tile), F32), pltpu.SemaphoreType.DMA((2 * tiles,))],
        compiler_params=pltpu.CompilerParams(vmem_limit_bytes=BIG),
    )(near, far, prefill_rows, decode_rows, *flat)


def solution(mesh):
    groups, heads = mesh.shape["grp"], mesh.shape["head"]
    chips = heads // 2
    stages = [1 << b for b in range(chips.bit_length() - 1)]

    def across(x, distance):
        return lax.ppermute(x, "head", [(i, i ^ distance) for i in range(heads)])

    def over_groups(x, distance):
        return lax.ppermute(x, "grp", [(i, i ^ distance) for i in range(groups)])

    routes = chip_routes(chips, groups)

    def weights_over_head(pieces):
        parts = []
        for k, rows in enumerate(routes):
            pairs = [
                (g * heads + h, g * heads + 2 * rows[g][h // 2] + h % 2) for g in range(groups) for h in range(heads)
            ]
            crossed = [(a, b ^ 1) for a, b in pairs]
            parts.append(
                jnp.stack(
                    [lax.ppermute(pieces[k, 0], ("grp", "head"), pairs), lax.ppermute(pieces[k, 1], ("grp", "head"), crossed)]
                )
            )
        return parts

    def weights_over_groups(parts, summed):
        both = jnp.stack(parts)
        if groups != 4:
            return [(both,)] + [(over_groups(both, j),) for j in range(1, groups)], summed
        near, side = over_groups(both, 1), over_groups(both, 2)
        summed, near, side = lax.optimization_barrier((summed, near, side))
        return [(both,), (near,), (side,), (over_groups(side[:, 0], 1), over_groups(near[:, 1], 2))], summed

    sources = [[[z ^ row.index(z) for z in range(chips)] for row in rows] for rows in routes]

    def on_device(
        prefill_token_rows,
        decode_token_rows,
        input_weight,
        lowrank_weight,
        step_size_weight,
        adapter_up_weight,
        output_weight,
        head_decay_rate,
        head_step_bias,
        head_skip_scale,
        gated_norm_scale,
        prompt_start_state,
        prompt_at_position,
        slot_sample_index,
        prompt_adapter_index,
    ):
        owned = prompt_start_state.shape[0]
        slots = slot_sample_index.shape[0]
        start = prompt_start_state.reshape(owned, HEAD_DEV * HEAD_CHANNELS, STATE)
        decode_rows = decode_token_rows.reshape(STEPS * slots, decode_token_rows.shape[2])
        norm_scale = gated_norm_scale.reshape(1, HEAD_DEV * HEAD_CHANNELS)
        send, keep, pieces = project(
            routes, prefill_token_rows, decode_rows, input_weight, lowrank_weight, step_size_weight.T,
            slot_sample_index, prompt_at_position, prompt_adapter_index, output_weight, owned,
        )
        parts = weights_over_head(pieces)
        rows = prefill_token_rows.shape[0] + decode_rows.shape[0]
        split = keep.shape[0]
        summed = jnp.concatenate([keep, send[split:]]) + across(send, 1)
        for distance in stages:
            half = split // 2
            outgoing = jnp.concatenate([summed[:half], summed[split:]]).astype(F16)
            summed = summed[half:] + across(outgoing, 2 * distance).astype(F32)
            split = half
        weights, summed = weights_over_groups(parts, summed)
        values, finals = end_states(
            rows, summed, adapter_up_weight, head_step_bias, head_decay_rate, start,
            slot_sample_index, prompt_at_position, prompt_adapter_index,
        )
        all_finals = [finals] + [over_groups(finals, j) for j in range(1, groups)]
        prefill_normed, within = rows_within(
            summed, values, start, head_step_bias, head_decay_rate, head_skip_scale, norm_scale
        )
        normed = decode_rows_out(
            summed, within, prefill_normed, all_finals, head_step_bias, head_decay_rate, norm_scale,
            slot_sample_index, prompt_at_position,
        )
        near = normed[None]
        have = [0]
        for distance in reversed(stages):
            near = jnp.concatenate([near, across(near, 2 * distance)])
            have = have + [c ^ distance for c in have]
        near = jnp.concatenate([near[have.index(c)][None] for c in range(chips)])
        far = across(near, 1)
        prefill_out, decode_out = output_rows(sources, near, far, weights, prefill_token_rows, decode_rows)
        return prefill_out, decode_out.reshape(decode_token_rows.shape)

    placed = (
        P("grp", "head"),
        P(None, "grp", "head"),
        P("head", None),
        P("head", None),
        P("head", None),
        P(None, "head"),
        P("head", None),
        P("head"),
        P("head"),
        P("head"),
        P("head"),
        P("grp", "head", None, None),
        P(),
        P("grp"),
        P(),
    )
    return jax.shard_map(
        on_device,
        mesh=mesh,
        in_specs=placed,
        out_specs=(P("grp", "head"), P(None, "grp", "head")),
        check_vma=False,
    )
```

```python
import itertools

import jax
import jax.numpy as jnp
from jax import lax
from jax.experimental import pallas as pl
from jax.experimental.pallas import tpu as pltpu
from jax.sharding import PartitionSpec as P

HEAD_CHANNELS = 64
STATE = 128
HEAD_DEV = 2
STRETCH = 32
SAMPLES = 16
STEPS = 3
ADAPTER_RANK = 16
LANES = 128
F32 = jnp.float32
BF16 = jnp.bfloat16
F16 = jnp.float16
EXACT = lax.Precision.HIGHEST
VMEM = pl.BlockSpec(memory_space=pltpu.VMEM)
PAD = 16
BIG = 24 * 1024 * 1024


def mxu(a, b):
    return jnp.dot(a, b, preferred_element_type=F32)


def in_hbm(x):
    return pltpu.with_memory_space_constraint(x, pltpu.HBM)


def dot_nt(a, b):
    return lax.dot_general(a, b, (((1,), (1,)), ((), ())), precision=EXACT, preferred_element_type=F32)


def dot_tn(a, b):
    return lax.dot_general(a, b, (((0,), (0,)), ((), ())), precision=EXACT, preferred_element_type=F32)


def lane_ids(rows):
    return lax.broadcasted_iota(jnp.int32, (rows, LANES), 1)


def row_ids(rows, width=1):
    return lax.broadcasted_iota(jnp.int32, (rows, width), 0)


def as_row(ref):
    return ref[...].reshape(1, ref.shape[0])


def entry(row, at):
    lanes = lax.broadcasted_iota(jnp.int32, row.shape, 1)
    return jnp.sum(jnp.where(lanes == at, row, 0.0), axis=1, keepdims=True)


def numbers(ref):
    return as_row(ref).astype(F32)


def row_prompts(slots_ref, slots):
    row = (as_row(slots_ref) // SAMPLES).astype(F32)
    return jnp.sum(jnp.where(row_ids(slots, slots) == lax.broadcasted_iota(jnp.int32, (slots, slots), 1), row, 0.0), axis=1, keepdims=True)


def row_tenants(slots_ref, held_ref, tenants_ref, group, owned, slots):
    prompts = row_prompts(slots_ref, slots)
    tenants, held = numbers(tenants_ref), numbers(held_ref)
    lanes = lax.broadcasted_iota(jnp.int32, tenants.shape, 1).astype(F32)
    decode = jnp.sum(jnp.where(lanes == prompts, tenants, 0.0), axis=1, keepdims=True)
    prefill = []
    for i in range(owned):
        prompt = entry(held, group * owned + i)
        tenant = jnp.sum(jnp.where(lanes == prompt, tenants, 0.0), axis=1, keepdims=True)
        prefill.append(jnp.broadcast_to(tenant, (STRETCH, 1)))
    return jnp.concatenate(prefill + [decode] * STEPS, axis=0)


def tenant_lanes(rows):
    return (lane_ids(rows) // ADAPTER_RANK).astype(F32)


def place_order(chips):
    bits = chips.bit_length() - 1
    order = []
    for p in range(chips):
        j = chips - 1 - p
        order.append(sum(((j >> b) & 1) << (bits - 1 - b) for b in range(bits)))
    return order


def packing(rows, heads):
    lanes = ADAPTER_RANK + heads
    pack = 1
    while 2 * pack * lanes <= LANES and rows % (2 * pack * 8) == 0:
        pack *= 2
    return pack


def pack_rows(mixed, pack):
    part, span = mixed.shape[0] // pack, LANES // pack
    total = mixed[:part]
    for q in range(1, pack):
        total = total + pltpu.roll(mixed[q * part : (q + 1) * part], q * span, 1)
    return total


def unpack_rows(packed, pack):
    span = LANES // pack
    parts = [packed] + [pltpu.roll(packed, LANES - q * span, 1) for q in range(1, pack)]
    return jnp.concatenate(parts, axis=0)


def project(
    routes, prefill_rows, decode_rows, input_weight, lowrank_weight, step_lines, slots, held, tenants, output_weight, owned
):
    rows_prefill, depth = prefill_rows.shape
    rows = rows_prefill + decode_rows.shape[0]
    width = 2 * HEAD_DEV * HEAD_CHANNELS
    pieces = width // LANES
    chips = input_weight.shape[1] // width // 2
    order = place_order(chips)
    low_blocks = 2 * STATE // LANES
    heads = step_lines.shape[0]
    pack = packing(rows, heads)
    packed = rows // pack
    base = chips * pieces * rows
    total = base + low_blocks * rows + packed
    slot_count = slots.shape[0]
    count = len(routes)
    column_width = output_weight.shape[1] // (2 * chips)

    def piece_copies(v_ref, p_ref, sems):
        group, head = lax.axis_index("grp"), lax.axis_index("head")
        copies = []
        for k, rows_of in enumerate(routes):
            target = looked_up(rows_of, group, head // 2)
            for side in range(2):
                column = pl.multiple_of((2 * target + ((head % 2) ^ side)) * column_width, column_width)
                copies.append(
                    pltpu.make_async_copy(
                        v_ref.at[:, pl.ds(column, column_width)], p_ref.at[k, side], sems.at[2 * k + side]
                    )
                )
        return copies

    def fetches(up_ref, ud_ref, w_ref, u_ref, w_all, sems, odd):
        me = lax.axis_index("head")
        copies = [
            pltpu.make_async_copy(up_ref, u_ref.at[:rows_prefill], sems.at[0]),
            pltpu.make_async_copy(ud_ref, u_ref.at[rows_prefill:], sems.at[1]),
        ]
        for i in range(chips):
            column = pl.multiple_of(((order[i] * 2 + odd) ^ me) * width, width)
            copies.append(pltpu.make_async_copy(w_ref.at[:, pl.ds(column, width)], w_all.at[i], sems.at[2 + i]))
        return copies

    def products(copies, u_ref, w_all, o_ref):
        for i in range(chips):
            copies[2 + i].wait()
            part = mxu(u_ref[...], w_all[i])
            for k in range(pieces):
                at = (i * pieces + k) * rows
                o_ref[at : at + rows] = part[:, k * LANES : (k + 1) * LANES]

    def send_body(
        slots_hbm, held_hbm, tenants_hbm, up_ref, ud_ref, w_ref, l_ref, s_ref, v_ref, o_ref, p_ref,
        u_ref, w_all, l_all, s_all, m_ref, slots_ref, held_ref, tenants_ref, sems, piece_sems,
    ):
        copies = fetches(up_ref, ud_ref, w_ref, u_ref, w_all, sems, 1)
        low_copies = [
            pltpu.make_async_copy(l_ref, l_all, sems.at[2 + chips]),
            pltpu.make_async_copy(s_ref, s_all, sems.at[3 + chips]),
        ]
        index_copies = [
            pltpu.make_async_copy(slots_hbm, slots_ref, sems.at[4 + chips]),
            pltpu.make_async_copy(held_hbm, held_ref, sems.at[5 + chips]),
            pltpu.make_async_copy(tenants_hbm, tenants_ref, sems.at[6 + chips]),
        ]
        moved = piece_copies(v_ref, p_ref, piece_sems)
        for copy in index_copies + copies[:2] + low_copies + copies[2:] + moved:
            copy.start()
        for copy in index_copies:
            copy.wait()
        lanes = tenant_lanes(rows)
        mine = lanes == row_tenants(slots_ref, held_ref, tenants_ref, lax.axis_index("grp"), owned, slot_count)
        for copy in copies[:2] + low_copies:
            copy.wait()
        low = mxu(u_ref[...], l_all[...])
        for k in range(low_blocks):
            o_ref[base + k * rows : base + (k + 1) * rows] = low[:, k * LANES : (k + 1) * LANES]
        picked = jnp.where(mine, low[:, 2 * STATE :], 0.0)
        shift = LANES // 2
        while shift >= ADAPTER_RANK:
            picked = picked + pltpu.roll(picked, shift, 1)
            shift //= 2
        m_ref[...] = jnp.where(lane_ids(rows) < ADAPTER_RANK, picked, 0.0)
        m_ref[:, ADAPTER_RANK : ADAPTER_RANK + heads] = lax.dot_general(
            u_ref[...], s_all[...], (((1,), (1,)), ((), ())), preferred_element_type=F32
        )
        o_ref[base + low_blocks * rows :] = pack_rows(m_ref[...], pack)
        products(copies, u_ref, w_all, o_ref)
        for copy in moved:
            copy.wait()

    def keep_body(up_ref, ud_ref, w_ref, o_ref, u_ref, w_all, sems):
        copies = fetches(up_ref, ud_ref, w_ref, u_ref, w_all, sems, 0)
        for copy in copies:
            copy.start()
        for copy in copies[:2]:
            copy.wait()
        products(copies, u_ref, w_all, o_ref)

    hbm = pl.BlockSpec(memory_space=pltpu.HBM)
    scratch = [pltpu.VMEM((rows, depth), BF16), pltpu.VMEM((chips, depth, width), BF16)]
    cost = pl.CostEstimate(
        flops=2 * rows * depth * width * chips, bytes_accessed=2 * depth * width * chips, transcendentals=0
    )
    params = pltpu.CompilerParams(vmem_limit_bytes=BIG)
    send, pieces_out = pl.pallas_call(
        send_body,
        out_shape=(
            jax.ShapeDtypeStruct((total, LANES), F32),
            jax.ShapeDtypeStruct((count, 2, output_weight.shape[0], column_width), BF16),
        ),
        in_specs=[hbm] * 9,
        out_specs=(VMEM, VMEM),
        scratch_shapes=scratch
        + [
            pltpu.VMEM(lowrank_weight.shape, BF16),
            pltpu.VMEM(step_lines.shape, BF16),
            pltpu.VMEM((rows, LANES), F32),
            pltpu.VMEM(slots.shape, jnp.int32),
            pltpu.VMEM(held.shape, jnp.int32),
            pltpu.VMEM(tenants.shape, jnp.int32),
            pltpu.SemaphoreType.DMA((chips + 7,)),
            pltpu.SemaphoreType.DMA((2 * count,)),
        ],
        compiler_params=params,
        cost_estimate=cost,
    )(
        *[
            in_hbm(x)
            for x in (
                slots, held, tenants, prefill_rows, decode_rows, input_weight, lowrank_weight, step_lines, output_weight
            )
        ]
    )
    keep = pl.pallas_call(
        keep_body,
        out_shape=jax.ShapeDtypeStruct((base, LANES), F32),
        in_specs=[hbm] * 3,
        out_specs=VMEM,
        scratch_shapes=scratch + [pltpu.SemaphoreType.DMA((chips + 2,))],
        compiler_params=params,
        cost_estimate=cost,
    )(*[in_hbm(x) for x in (prefill_rows, decode_rows, input_weight)])
    return send, keep, pieces_out


def line_load(route):
    steps = [0] * (2 * len(route))
    for a, b in enumerate(route):
        for link in range(min(a, b), max(a, b)):
            steps[2 * link + (a < b)] += 1
    return max(steps)


def chip_routes(chips, groups):
    wanted = [tuple(z ^ shift for z in range(chips)) for shift in range(chips)]
    if chips <= 4:
        ranked = sorted(itertools.permutations(range(chips)), key=lambda route: (line_load(route), route))

        def fill(rows, most):
            if len(rows) == chips:
                return rows
            for route in ranked:
                if line_load(route) <= most and all(a != b for row in rows for a, b in zip(row, route)):
                    found = fill(rows + [route], most)
                    if found:
                        return found
            return None

        for most in range(chips + 1):
            found = fill([], most)
            if found:
                wanted = found
                break
    return [wanted[groups * k : groups * (k + 1)] for k in range(chips // groups)]


def piece(x_ref, k, rows, at=slice(None)):
    low, high, _ = at.indices(rows)
    return x_ref[k * rows + low : k * rows + high]


def mixed_rows(x_ref, rows):
    return unpack_rows(x_ref[4 * rows :], rows // (x_ref.shape[0] - 4 * rows))


def piece(x_ref, k, rows, at=slice(None)):
    low, high, _ = at.indices(rows)
    return x_ref[k * rows + low : k * rows + high]


def mixed_rows(x_ref, rows):
    return unpack_rows(x_ref[4 * rows :], rows // (x_ref.shape[0] - 4 * rows))


def looked_up(table, group, chip):
    found = jnp.int32(0)
    for g, row in enumerate(table):
        for z, value in enumerate(row):
            found = jnp.where((group == g) & (chip == z), value, found)
    return found


def piece(x_ref, k, rows, at=slice(None)):
    low, high, _ = at.indices(rows)
    return x_ref[k * rows + low : k * rows + high]


def mixed_rows(x_ref, rows):
    return unpack_rows(x_ref[4 * rows :], rows // (x_ref.shape[0] - 4 * rows))


def looked_up(table, group, chip):
    found = jnp.int32(0)
    for g, row in enumerate(table):
        for z, value in enumerate(row):
            found = jnp.where((group == g) & (chip == z), value, found)
    return found


def weight_pieces(output_weight, routes, heads):
    own_rows, all_width = output_weight.shape
    width = all_width // heads
    count = len(routes)

    def body(w_ref, o_ref, sems):
        group, head = lax.axis_index("grp"), lax.axis_index("head")
        copies = []
        for k, rows in enumerate(routes):
            target = looked_up(rows, group, head // 2)
            for side in range(2):
                column = pl.multiple_of((2 * target + ((head % 2) ^ side)) * width, width)
                copies.append(
                    pltpu.make_async_copy(w_ref.at[:, pl.ds(column, width)], o_ref.at[k, side], sems.at[2 * k + side])
                )
        for copy in copies:
            copy.start()
        for copy in copies:
            copy.wait()

    return pl.pallas_call(
        body,
        out_shape=jax.ShapeDtypeStruct((count, 2, own_rows, width), BF16),
        in_specs=[pl.BlockSpec(memory_space=pltpu.HBM)],
        out_specs=VMEM,
        scratch_shapes=[pltpu.SemaphoreType.DMA((2 * count,))],
        compiler_params=pltpu.CompilerParams(vmem_limit_bytes=BIG),
    )(in_hbm(output_weight))


def step_lengths(mixed, bias_ref):
    lanes = lane_ids(mixed.shape[0])
    me = lax.axis_index("head")
    bias = as_row(bias_ref)
    lengths = []
    for h in range(HEAD_DEV):
        raw = jnp.sum(jnp.where(lanes == ADAPTER_RANK + me * HEAD_DEV + h, mixed, 0.0), axis=1, keepdims=True)
        raw = raw + bias[:, h : h + 1]
        lengths.append(jnp.maximum(raw, 0.0) + jnp.log1p(jnp.exp(-jnp.abs(raw))))
    return lengths


def by_head(first, second, rows):
    return jnp.where(lane_ids(rows) < HEAD_CHANNELS, first, second)


def prefill_decay(lengths, rate_ref, rows):
    t_at = lax.broadcasted_iota(jnp.int32, (rows, rows), 0)
    s_at = lax.broadcasted_iota(jnp.int32, (rows, rows), 1)
    same = t_at // STRETCH == s_at // STRETCH
    columns, lines, steps = [], [], []
    rate = as_row(rate_ref)
    for h in range(HEAD_DEV):
        length = lengths[h][:rows]
        decay = -(length * rate[:, h : h + 1])
        line = jnp.sum(jnp.where(same & (t_at <= s_at), decay, 0.0), axis=0, keepdims=True)
        lines.append(line)
        columns.append(jnp.sum(jnp.where(t_at == s_at, line, 0.0), axis=1, keepdims=True))
        steps.append(jnp.sum(jnp.where(t_at == s_at, length, 0.0), axis=0, keepdims=True))
    return columns, lines, steps, same & (t_at >= s_at)


def end_states(rows, summed, adapter_up, bias, rate, start, slots, held, tenants):
    owned = start.shape[0]
    prefill = owned * STRETCH
    slot_count = slots.shape[0]

    def body(slots_ref, held_ref, tenants_ref, bias_ref, rate_ref, x_ref, a_ref, s_ref, v_ref, f_ref):
        corner = row_ids(LANES, LANES) == lane_ids(LANES)
        group = lax.axis_index("grp")
        mixed = mixed_rows(x_ref, rows)
        lanes = lane_ids(rows)
        mine = tenant_lanes(rows) == row_tenants(slots_ref, held_ref, tenants_ref, group, owned, slot_count)
        picked = jnp.where(lanes < ADAPTER_RANK, mixed, 0.0)
        shift = ADAPTER_RANK
        while shift < LANES:
            picked = picked + pltpu.roll(picked, shift, 1)
            shift *= 2
        picked = jnp.where(mine, picked, 0.0).astype(BF16)
        values = by_head(piece(x_ref, 0, rows), pltpu.roll(piece(x_ref, 1, rows), HEAD_CHANNELS, 1), rows)
        values = values + mxu(picked, a_ref[...])
        v_ref[...] = values
        lengths = step_lengths(mixed[:prefill], bias_ref)
        columns, _, _, _ = prefill_decay(lengths, rate_ref, prefill)
        for i in range(owned):
            lo, hi = i * STRETCH, (i + 1) * STRETCH
            ends = [columns[h][hi - 1 : hi] for h in range(HEAD_DEV)]
            tails = [jnp.exp(ends[h] - columns[h][lo:hi]) * lengths[h][lo:hi] for h in range(HEAD_DEV)]
            added = dot_tn(by_head(tails[0], tails[1], STRETCH) * values[lo:hi], piece(x_ref, 2, rows, slice(lo, hi)))
            kept = jnp.where(row_ids(LANES) < HEAD_CHANNELS, jnp.exp(ends[0]), jnp.exp(ends[1]))
            state = kept * s_ref[i] + added
            largest = jnp.max(jnp.abs(state), axis=1, keepdims=True)
            power = jnp.ceil(jnp.log2(jnp.maximum(largest, 1e-30)))
            f_ref[i * LANES : (i + 1) * LANES] = state * jnp.exp2(-power)
            line = jnp.sum(jnp.where(corner, power, 0.0), axis=0, keepdims=True)
            f_ref[owned * LANES + i * PAD : owned * LANES + (i + 1) * PAD] = jnp.broadcast_to(line, (PAD, LANES))

    return pl.pallas_call(
        body,
        out_shape=(
            jax.ShapeDtypeStruct((rows, LANES), F32),
            jax.ShapeDtypeStruct((owned * (LANES + PAD), STATE), F32),
        ),
        in_specs=[VMEM] * 8,
        out_specs=(VMEM, VMEM),
        compiler_params=pltpu.CompilerParams(vmem_limit_bytes=BIG),
    )(slots, held, tenants, bias, rate, summed, adapter_up, start)


def normalise(result, gate, scale_ref):
    gated = result * (gate * (1.0 / (1.0 + jnp.exp(-gate))))
    spread = jnp.mean(gated * gated, axis=1, keepdims=True)
    return (gated * lax.rsqrt(spread + 1e-05) * scale_ref[...]).astype(BF16)


def gates(x_ref, rows, at):
    first, second = piece(x_ref, 0, rows, at), piece(x_ref, 1, rows, at)
    return by_head(pltpu.roll(first, HEAD_CHANNELS, 1), second, first.shape[0])


def rows_within(summed, values, start, bias, rate, skip, norm_scale):
    rows = values.shape[0]
    owned = start.shape[0]
    prefill = owned * STRETCH
    slot_count = (rows - prefill) // STEPS

    def body(bias_ref, rate_ref, skip_ref, x_ref, v_ref, s_ref, g_ref, n_ref, y_ref):
        rate, skip = as_row(rate_ref), as_row(skip_ref)
        lengths = step_lengths(mixed_rows(x_ref, rows), bias_ref)
        columns, lines, steps, later = prefill_decay(lengths, rate_ref, prefill)
        now = slice(0, prefill)
        values = v_ref[now]
        scores = dot_nt(piece(x_ref, 3, rows, now), piece(x_ref, 2, rows, now))
        sums = []
        for h in range(HEAD_DEV):
            weights = jnp.where(later, jnp.exp(jnp.where(later, columns[h] - lines[h], 0.0)), 0.0) * steps[h]
            sums.append(jnp.dot(weights * scores, values, precision=EXACT, preferred_element_type=F32))
        result = by_head(sums[0], sums[1], prefill)
        carried = jnp.concatenate(
            [dot_nt(piece(x_ref, 3, rows, slice(i * STRETCH, (i + 1) * STRETCH)), s_ref[i]) for i in range(owned)], axis=0
        )
        kept = by_head(jnp.exp(columns[0]), jnp.exp(columns[1]), prefill)
        skipped = by_head(skip[:, :1], skip[:, 1:], prefill)
        result = result + kept * carried + skipped * values
        n_ref[...] = normalise(result, gates(x_ref, rows, now), g_ref)
        at = [slice(prefill + s * slot_count, prefill + (s + 1) * slot_count) for s in range(STEPS)]
        run = [[], []]
        for h in range(HEAD_DEV):
            total = jnp.zeros((slot_count, 1), F32)
            for s in range(STEPS):
                total = total - lengths[h][at[s]] * rate[:, h : h + 1]
                run[h].append(total)
        skipped = by_head(skip[:, :1], skip[:, 1:], slot_count)
        for s in range(STEPS):
            total = skipped * v_ref[at[s]]
            for u in range(s + 1):
                score = jnp.sum(piece(x_ref, 3, rows, at[s]) * piece(x_ref, 2, rows, at[u]), axis=1, keepdims=True)
                factor = [jnp.exp(run[h][s] - run[h][u]) * lengths[h][at[u]] * score for h in range(HEAD_DEV)]
                total = total + by_head(factor[0], factor[1], slot_count) * v_ref[at[u]]
            y_ref[s * slot_count : (s + 1) * slot_count] = total

    return pl.pallas_call(
        body,
        out_shape=(
            jax.ShapeDtypeStruct((prefill, LANES), BF16),
            jax.ShapeDtypeStruct((rows - prefill, LANES), F32),
        ),
        in_specs=[VMEM] * 7,
        out_specs=(VMEM, VMEM),
        compiler_params=pltpu.CompilerParams(vmem_limit_bytes=BIG),
    )(bias, rate, skip, summed, values, start, norm_scale)


def decode_rows_out(summed, within, prefill_normed, finals, bias, rate, norm_scale, slots, held):
    prefill = prefill_normed.shape[0]
    rows = prefill + within.shape[0]
    owned = finals[0].shape[0] // (LANES + PAD)
    slot_count = slots.shape[0]
    parts = len(finals)

    def body(slots_ref, held_ref, bias_ref, rate_ref, x_ref, y_ref, p_ref, g_ref, *rest):
        f_refs, n_ref = rest[:parts], rest[parts]
        group = lax.axis_index("grp")
        held, rate = numbers(held_ref), as_row(rate_ref)
        now = slice(prefill, rows)
        prompts = row_prompts(slots_ref, slot_count)
        prompts = jnp.concatenate([prompts] * STEPS, axis=0)
        reader = piece(x_ref, 3, rows, now)
        carried = jnp.zeros((rows - prefill, LANES), F32)
        for j in range(parts):
            for i in range(owned):
                mine = prompts == entry(held, (group ^ j) * owned + i)
                part = dot_nt(jnp.where(mine, reader, 0.0), f_refs[j][i * LANES : (i + 1) * LANES])
                at = owned * LANES + i * PAD
                carried = carried + part * jnp.exp2(f_refs[j][at : at + 1])
        lengths = step_lengths(mixed_rows(x_ref, rows)[now], bias_ref)
        kept = []
        for h in range(HEAD_DEV):
            total = jnp.zeros((slot_count, 1), F32)
            runs = []
            for s in range(STEPS):
                total = total - lengths[h][s * slot_count : (s + 1) * slot_count] * rate[:, h : h + 1]
                runs.append(total)
            kept.append(jnp.exp(jnp.concatenate(runs, axis=0)))
        result = y_ref[...] + by_head(kept[0], kept[1], rows - prefill) * carried
        n_ref[:prefill] = p_ref[...]
        n_ref[prefill:] = normalise(result, gates(x_ref, rows, now), g_ref)

    return pl.pallas_call(
        body,
        out_shape=jax.ShapeDtypeStruct((rows, LANES), BF16),
        in_specs=[VMEM] * (8 + parts),
        out_specs=VMEM,
        compiler_params=pltpu.CompilerParams(vmem_limit_bytes=BIG),
    )(slots, held, bias, rate, summed, within, prefill_normed, norm_scale, *finals)


def output_rows(sources, near, far, weights, prefill_rows, decode_rows):
    chips, rows, _ = near.shape
    prefill, width = prefill_rows.shape
    parts = len(weights)
    per_part = chips // parts
    tile = width // 4 if width % 512 == 0 else width
    tiles = width // tile
    flat = [w for part in weights for w in part]

    def body(a_ref, b_ref, up_ref, ud_ref, *rest):
        w_refs = rest[: len(flat)]
        op_ref, od_ref, total_ref, sems = rest[len(flat) :]
        lefts, rights, at = [], [], 0
        for j in range(parts):
            for k in range(per_part):
                chip = looked_up(sources[k], lax.axis_index("grp") ^ j, lax.axis_index("head") // 2)
                if len(weights[j]) == 1:
                    lefts.append(jnp.concatenate([a_ref[chip], b_ref[chip]], axis=1))
                    rights.append((w_refs[at], (k,), 2))
                else:
                    lefts.extend([a_ref[chip], b_ref[chip]])
                    rights.extend([(w_refs[at], (k,), 1), (w_refs[at + 1], (k,), 1)])
            at += len(weights[j])
        copies = []
        for t in range(tiles):
            columns = slice(t * tile, (t + 1) * tile)
            total = jnp.concatenate([up_ref[:, columns], ud_ref[:, columns]], axis=0).astype(F32)
            for left, (w_ref, (k,), cores) in zip(lefts, rights):
                if cores == 2:
                    total = total + mxu(left, w_ref[k, :, :, columns].reshape(left.shape[1], tile))
                else:
                    total = total + mxu(left, w_ref[k, :, columns])
            total_ref[t] = total
            copies.append(pltpu.make_async_copy(total_ref.at[t, :prefill], op_ref.at[:, columns], sems.at[2 * t]))
            copies.append(pltpu.make_async_copy(total_ref.at[t, prefill:], od_ref.at[:, columns], sems.at[2 * t + 1]))
            copies[-2].start()
            copies[-1].start()
        for copy in copies:
            copy.wait()

    return pl.pallas_call(
        body,
        out_shape=(
            jax.ShapeDtypeStruct(prefill_rows.shape, F32),
            jax.ShapeDtypeStruct(decode_rows.shape, F32),
        ),
        in_specs=[VMEM] * (4 + len(flat)),
        out_specs=(pl.BlockSpec(memory_space=pltpu.HBM),) * 2,
        scratch_shapes=[pltpu.VMEM((tiles, rows, tile), F32), pltpu.SemaphoreType.DMA((2 * tiles,))],
        compiler_params=pltpu.CompilerParams(vmem_limit_bytes=BIG),
    )(near, far, prefill_rows, decode_rows, *flat)


def solution(mesh):
    groups, heads = mesh.shape["grp"], mesh.shape["head"]
    chips = heads // 2
    stages = [1 << b for b in range(chips.bit_length() - 1)]

    def across(x, distance):
        return lax.ppermute(x, "head", [(i, i ^ distance) for i in range(heads)])

    def over_groups(x, distance):
        return lax.ppermute(x, "grp", [(i, i ^ distance) for i in range(groups)])

    routes = chip_routes(chips, groups)

    def weights_over_head(pieces):
        parts = []
        for k, rows in enumerate(routes):
            pairs = [
                (g * heads + h, g * heads + 2 * rows[g][h // 2] + h % 2) for g in range(groups) for h in range(heads)
            ]
            crossed = [(a, b ^ 1) for a, b in pairs]
            parts.append(
                jnp.stack(
                    [lax.ppermute(pieces[k, 0], ("grp", "head"), pairs), lax.ppermute(pieces[k, 1], ("grp", "head"), crossed)]
                )
            )
        return parts

    def weights_over_groups(parts, summed):
        both = jnp.stack(parts)
        if groups != 4:
            return [(both,)] + [(over_groups(both, j),) for j in range(1, groups)], summed
        near, side = over_groups(both, 1), over_groups(both, 2)
        summed, near = lax.optimization_barrier((summed, near))
        return [(both,), (near,), (side,), (over_groups(side[:, 0], 1), over_groups(near[:, 1], 2))], summed

    sources = [[[z ^ row.index(z) for z in range(chips)] for row in rows] for rows in routes]

    def on_device(
        prefill_token_rows,
        decode_token_rows,
        input_weight,
        lowrank_weight,
        step_size_weight,
        adapter_up_weight,
        output_weight,
        head_decay_rate,
        head_step_bias,
        head_skip_scale,
        gated_norm_scale,
        prompt_start_state,
        prompt_at_position,
        slot_sample_index,
        prompt_adapter_index,
    ):
        owned = prompt_start_state.shape[0]
        slots = slot_sample_index.shape[0]
        start = prompt_start_state.reshape(owned, HEAD_DEV * HEAD_CHANNELS, STATE)
        decode_rows = decode_token_rows.reshape(STEPS * slots, decode_token_rows.shape[2])
        norm_scale = gated_norm_scale.reshape(1, HEAD_DEV * HEAD_CHANNELS)
        send, keep, pieces = project(
            routes, prefill_token_rows, decode_rows, input_weight, lowrank_weight, step_size_weight.T,
            slot_sample_index, prompt_at_position, prompt_adapter_index, output_weight, owned,
        )
        parts = weights_over_head(pieces)
        rows = prefill_token_rows.shape[0] + decode_rows.shape[0]
        split = keep.shape[0]
        summed = jnp.concatenate([keep, send[split:]]) + across(send, 1)
        for distance in stages:
            half = split // 2
            outgoing = jnp.concatenate([summed[:half], summed[split:]]).astype(F16)
            summed = summed[half:] + across(outgoing, 2 * distance).astype(F32)
            split = half
        weights, summed = weights_over_groups(parts, summed)
        values, finals = end_states(
            rows, summed, adapter_up_weight, head_step_bias, head_decay_rate, start,
            slot_sample_index, prompt_at_position, prompt_adapter_index,
        )
        message = finals.astype(F16)
        all_finals = [finals] + [over_groups(message, j).astype(F32) for j in range(1, groups)]
        prefill_normed, within = rows_within(
            summed, values, start, head_step_bias, head_decay_rate, head_skip_scale, norm_scale
        )
        normed = decode_rows_out(
            summed, within, prefill_normed, all_finals, head_step_bias, head_decay_rate, norm_scale,
            slot_sample_index, prompt_at_position,
        )
        near = normed[None]
        have = [0]
        for distance in reversed(stages):
            if distance == stages[0]:
                near, last = lax.optimization_barrier((near, weights[-1][-1]))
                weights = weights[:-1] + [weights[-1][:-1] + (last,)]
            near = jnp.concatenate([near, across(near, 2 * distance)])
            have = have + [c ^ distance for c in have]
        near = jnp.concatenate([near[have.index(c)][None] for c in range(chips)])
        far = across(near, 1)
        prefill_out, decode_out = output_rows(sources, near, far, weights, prefill_token_rows, decode_rows)
        return prefill_out, decode_out.reshape(decode_token_rows.shape)

    placed = (
        P("grp", "head"),
        P(None, "grp", "head"),
        P("head", None),
        P("head", None),
        P("head", None),
        P(None, "head"),
        P("head", None),
        P("head"),
        P("head"),
        P("head"),
        P("head"),
        P("grp", "head", None, None),
        P(),
        P("grp"),
        P(),
    )
    return jax.shard_map(
        on_device,
        mesh=mesh,
        in_specs=placed,
        out_specs=(P("grp", "head"), P(None, "grp", "head")),
        check_vma=False,
    )
```

```python
import itertools

import jax
import jax.numpy as jnp
from jax import lax
from jax.experimental import pallas as pl
from jax.experimental.pallas import tpu as pltpu
from jax.sharding import PartitionSpec as P

HEAD_CHANNELS = 64
STATE = 128
HEAD_DEV = 2
STRETCH = 32
SAMPLES = 16
STEPS = 3
ADAPTER_RANK = 16
LANES = 128
F32 = jnp.float32
BF16 = jnp.bfloat16
F16 = jnp.float16
VMEM = pl.BlockSpec(memory_space=pltpu.VMEM)
PAD = 16
BIG = 24 * 1024 * 1024


def mxu(a, b):
    return jnp.dot(a, b, preferred_element_type=F32)


def in_hbm(x):
    return pltpu.with_memory_space_constraint(x, pltpu.HBM)


def split_dot(a, b, dims):
    a_high, b_high = a.astype(BF16), b.astype(BF16)
    a_low, b_low = (a - a_high.astype(F32)).astype(BF16), (b - b_high.astype(F32)).astype(BF16)

    def part(x, y):
        return lax.dot_general(x, y, (dims, ((), ())), preferred_element_type=F32)

    return part(a_high, b_high) + (part(a_high, b_low) + part(a_low, b_high))


def dot_nt(a, b):
    return split_dot(a, b, ((1,), (1,)))


def dot_tn(a, b):
    return split_dot(a, b, ((0,), (0,)))


def lane_ids(rows):
    return lax.broadcasted_iota(jnp.int32, (rows, LANES), 1)


def row_ids(rows, width=1):
    return lax.broadcasted_iota(jnp.int32, (rows, width), 0)


def as_row(ref):
    return ref[...].reshape(1, ref.shape[0])


def entry(row, at):
    lanes = lax.broadcasted_iota(jnp.int32, row.shape, 1)
    return jnp.sum(jnp.where(lanes == at, row, 0.0), axis=1, keepdims=True)


def numbers(ref):
    return as_row(ref).astype(F32)


def row_prompts(slots_ref, slots):
    row = (as_row(slots_ref) // SAMPLES).astype(F32)
    return jnp.sum(jnp.where(row_ids(slots, slots) == lax.broadcasted_iota(jnp.int32, (slots, slots), 1), row, 0.0), axis=1, keepdims=True)


def row_tenants(slots_ref, held_ref, tenants_ref, group, owned, slots):
    prompts = row_prompts(slots_ref, slots)
    tenants, held = numbers(tenants_ref), numbers(held_ref)
    lanes = lax.broadcasted_iota(jnp.int32, tenants.shape, 1).astype(F32)
    decode = jnp.sum(jnp.where(lanes == prompts, tenants, 0.0), axis=1, keepdims=True)
    prefill = []
    for i in range(owned):
        prompt = entry(held, group * owned + i)
        tenant = jnp.sum(jnp.where(lanes == prompt, tenants, 0.0), axis=1, keepdims=True)
        prefill.append(jnp.broadcast_to(tenant, (STRETCH, 1)))
    return jnp.concatenate(prefill + [decode] * STEPS, axis=0)


def tenant_lanes(rows):
    return (lane_ids(rows) // ADAPTER_RANK).astype(F32)


def place_order(chips):
    bits = chips.bit_length() - 1
    order = []
    for p in range(chips):
        j = chips - 1 - p
        order.append(sum(((j >> b) & 1) << (bits - 1 - b) for b in range(bits)))
    return order


def packing(rows, heads):
    lanes = ADAPTER_RANK + heads
    pack = 1
    while 2 * pack * lanes <= LANES and rows % (2 * pack * 8) == 0:
        pack *= 2
    return pack


def pack_rows(mixed, pack):
    part, span = mixed.shape[0] // pack, LANES // pack
    total = mixed[:part]
    for q in range(1, pack):
        total = total + pltpu.roll(mixed[q * part : (q + 1) * part], q * span, 1)
    return total


def unpack_rows(packed, pack):
    span = LANES // pack
    parts = [packed] + [pltpu.roll(packed, LANES - q * span, 1) for q in range(1, pack)]
    return jnp.concatenate(parts, axis=0)


def project(
    routes, prefill_rows, decode_rows, input_weight, lowrank_weight, step_lines, slots, held, tenants, output_weight, owned
):
    rows_prefill, depth = prefill_rows.shape
    rows = rows_prefill + decode_rows.shape[0]
    width = 2 * HEAD_DEV * HEAD_CHANNELS
    pieces = width // LANES
    chips = input_weight.shape[1] // width // 2
    order = place_order(chips)
    low_blocks = 2 * STATE // LANES
    heads = step_lines.shape[0]
    pack = packing(rows, heads)
    packed = rows // pack
    base = chips * pieces * rows
    total = base + low_blocks * rows + packed
    slot_count = slots.shape[0]
    count = len(routes)
    column_width = output_weight.shape[1] // (2 * chips)

    def piece_copies(v_ref, p_ref, sems):
        group, head = lax.axis_index("grp"), lax.axis_index("head")
        copies = []
        for k, rows_of in enumerate(routes):
            target = looked_up(rows_of, group, head // 2)
            for side in range(2):
                column = pl.multiple_of((2 * target + ((head % 2) ^ side)) * column_width, column_width)
                copies.append(
                    pltpu.make_async_copy(
                        v_ref.at[:, pl.ds(column, column_width)], p_ref.at[k, side], sems.at[2 * k + side]
                    )
                )
        return copies

    def fetches(up_ref, ud_ref, w_ref, u_ref, w_all, sems, odd):
        me = lax.axis_index("head")
        copies = [
            pltpu.make_async_copy(up_ref, u_ref.at[:rows_prefill], sems.at[0]),
            pltpu.make_async_copy(ud_ref, u_ref.at[rows_prefill:], sems.at[1]),
        ]
        for i in range(chips):
            column = pl.multiple_of(((order[i] * 2 + odd) ^ me) * width, width)
            copies.append(pltpu.make_async_copy(w_ref.at[:, pl.ds(column, width)], w_all.at[i], sems.at[2 + i]))
        return copies

    def products(copies, u_ref, w_all, o_ref):
        for i in range(chips):
            copies[2 + i].wait()
            part = mxu(u_ref[...], w_all[i])
            for k in range(pieces):
                at = (i * pieces + k) * rows
                o_ref[at : at + rows] = part[:, k * LANES : (k + 1) * LANES]

    def send_body(
        slots_hbm, held_hbm, tenants_hbm, up_ref, ud_ref, w_ref, l_ref, s_ref, v_ref, o_ref, p_ref,
        u_ref, w_all, l_all, s_all, m_ref, slots_ref, held_ref, tenants_ref, sems, piece_sems,
    ):
        copies = fetches(up_ref, ud_ref, w_ref, u_ref, w_all, sems, 1)
        low_copies = [
            pltpu.make_async_copy(l_ref, l_all, sems.at[2 + chips]),
            pltpu.make_async_copy(s_ref, s_all, sems.at[3 + chips]),
        ]
        index_copies = [
            pltpu.make_async_copy(slots_hbm, slots_ref, sems.at[4 + chips]),
            pltpu.make_async_copy(held_hbm, held_ref, sems.at[5 + chips]),
            pltpu.make_async_copy(tenants_hbm, tenants_ref, sems.at[6 + chips]),
        ]
        moved = piece_copies(v_ref, p_ref, piece_sems)
        for copy in index_copies + copies[:2] + low_copies + copies[2:] + moved:
            copy.start()
        for copy in index_copies:
            copy.wait()
        lanes = tenant_lanes(rows)
        mine = lanes == row_tenants(slots_ref, held_ref, tenants_ref, lax.axis_index("grp"), owned, slot_count)
        for copy in copies[:2] + low_copies:
            copy.wait()
        low = mxu(u_ref[...], l_all[...])
        for k in range(low_blocks):
            o_ref[base + k * rows : base + (k + 1) * rows] = low[:, k * LANES : (k + 1) * LANES]
        picked = jnp.where(mine, low[:, 2 * STATE :], 0.0)
        shift = LANES // 2
        while shift >= ADAPTER_RANK:
            picked = picked + pltpu.roll(picked, shift, 1)
            shift //= 2
        m_ref[...] = jnp.where(lane_ids(rows) < ADAPTER_RANK, picked, 0.0)
        m_ref[:, ADAPTER_RANK : ADAPTER_RANK + heads] = lax.dot_general(
            u_ref[...], s_all[...], (((1,), (1,)), ((), ())), preferred_element_type=F32
        )
        o_ref[base + low_blocks * rows :] = pack_rows(m_ref[...], pack)
        products(copies, u_ref, w_all, o_ref)
        for copy in moved:
            copy.wait()

    def keep_body(up_ref, ud_ref, w_ref, o_ref, u_ref, w_all, sems):
        copies = fetches(up_ref, ud_ref, w_ref, u_ref, w_all, sems, 0)
        for copy in copies:
            copy.start()
        for copy in copies[:2]:
            copy.wait()
        products(copies, u_ref, w_all, o_ref)

    hbm = pl.BlockSpec(memory_space=pltpu.HBM)
    scratch = [pltpu.VMEM((rows, depth), BF16), pltpu.VMEM((chips, depth, width), BF16)]
    cost = pl.CostEstimate(
        flops=2 * rows * depth * width * chips, bytes_accessed=2 * depth * width * chips, transcendentals=0
    )
    params = pltpu.CompilerParams(vmem_limit_bytes=BIG)
    send, pieces_out = pl.pallas_call(
        send_body,
        out_shape=(
            jax.ShapeDtypeStruct((total, LANES), F32),
            jax.ShapeDtypeStruct((count, 2, output_weight.shape[0], column_width), BF16),
        ),
        in_specs=[hbm] * 9,
        out_specs=(VMEM, VMEM),
        scratch_shapes=scratch
        + [
            pltpu.VMEM(lowrank_weight.shape, BF16),
            pltpu.VMEM(step_lines.shape, BF16),
            pltpu.VMEM((rows, LANES), F32),
            pltpu.VMEM(slots.shape, jnp.int32),
            pltpu.VMEM(held.shape, jnp.int32),
            pltpu.VMEM(tenants.shape, jnp.int32),
            pltpu.SemaphoreType.DMA((chips + 7,)),
            pltpu.SemaphoreType.DMA((2 * count,)),
        ],
        compiler_params=params,
        cost_estimate=cost,
    )(
        *[
            in_hbm(x)
            for x in (
                slots, held, tenants, prefill_rows, decode_rows, input_weight, lowrank_weight, step_lines, output_weight
            )
        ]
    )
    keep = pl.pallas_call(
        keep_body,
        out_shape=jax.ShapeDtypeStruct((base, LANES), F32),
        in_specs=[hbm] * 3,
        out_specs=VMEM,
        scratch_shapes=scratch + [pltpu.SemaphoreType.DMA((chips + 2,))],
        compiler_params=params,
        cost_estimate=cost,
    )(*[in_hbm(x) for x in (prefill_rows, decode_rows, input_weight)])
    return send, keep, pieces_out


def line_load(route):
    steps = [0] * (2 * len(route))
    for a, b in enumerate(route):
        for link in range(min(a, b), max(a, b)):
            steps[2 * link + (a < b)] += 1
    return max(steps)


def chip_routes(chips, groups):
    wanted = [tuple(z ^ shift for z in range(chips)) for shift in range(chips)]
    if chips <= 4:
        ranked = sorted(itertools.permutations(range(chips)), key=lambda route: (line_load(route), route))

        def fill(rows, most):
            if len(rows) == chips:
                return rows
            for route in ranked:
                if line_load(route) <= most and all(a != b for row in rows for a, b in zip(row, route)):
                    found = fill(rows + [route], most)
                    if found:
                        return found
            return None

        for most in range(chips + 1):
            found = fill([], most)
            if found:
                wanted = found
                break
    return [wanted[groups * k : groups * (k + 1)] for k in range(chips // groups)]


def piece(x_ref, k, rows, at=slice(None)):
    low, high, _ = at.indices(rows)
    return x_ref[k * rows + low : k * rows + high]


def mixed_rows(x_ref, rows):
    return unpack_rows(x_ref[4 * rows :], rows // (x_ref.shape[0] - 4 * rows))


def piece(x_ref, k, rows, at=slice(None)):
    low, high, _ = at.indices(rows)
    return x_ref[k * rows + low : k * rows + high]


def mixed_rows(x_ref, rows):
    return unpack_rows(x_ref[4 * rows :], rows // (x_ref.shape[0] - 4 * rows))


def looked_up(table, group, chip):
    found = jnp.int32(0)
    for g, row in enumerate(table):
        for z, value in enumerate(row):
            found = jnp.where((group == g) & (chip == z), value, found)
    return found


def piece(x_ref, k, rows, at=slice(None)):
    low, high, _ = at.indices(rows)
    return x_ref[k * rows + low : k * rows + high]


def mixed_rows(x_ref, rows):
    return unpack_rows(x_ref[4 * rows :], rows // (x_ref.shape[0] - 4 * rows))


def looked_up(table, group, chip):
    found = jnp.int32(0)
    for g, row in enumerate(table):
        for z, value in enumerate(row):
            found = jnp.where((group == g) & (chip == z), value, found)
    return found


def weight_pieces(output_weight, routes, heads):
    own_rows, all_width = output_weight.shape
    width = all_width // heads
    count = len(routes)

    def body(w_ref, o_ref, sems):
        group, head = lax.axis_index("grp"), lax.axis_index("head")
        copies = []
        for k, rows in enumerate(routes):
            target = looked_up(rows, group, head // 2)
            for side in range(2):
                column = pl.multiple_of((2 * target + ((head % 2) ^ side)) * width, width)
                copies.append(
                    pltpu.make_async_copy(w_ref.at[:, pl.ds(column, width)], o_ref.at[k, side], sems.at[2 * k + side])
                )
        for copy in copies:
            copy.start()
        for copy in copies:
            copy.wait()

    return pl.pallas_call(
        body,
        out_shape=jax.ShapeDtypeStruct((count, 2, own_rows, width), BF16),
        in_specs=[pl.BlockSpec(memory_space=pltpu.HBM)],
        out_specs=VMEM,
        scratch_shapes=[pltpu.SemaphoreType.DMA((2 * count,))],
        compiler_params=pltpu.CompilerParams(vmem_limit_bytes=BIG),
    )(in_hbm(output_weight))


def step_lengths(mixed, bias_ref):
    lanes = lane_ids(mixed.shape[0])
    me = lax.axis_index("head")
    bias = as_row(bias_ref)
    lengths = []
    for h in range(HEAD_DEV):
        raw = jnp.sum(jnp.where(lanes == ADAPTER_RANK + me * HEAD_DEV + h, mixed, 0.0), axis=1, keepdims=True)
        raw = raw + bias[:, h : h + 1]
        lengths.append(jnp.maximum(raw, 0.0) + jnp.log1p(jnp.exp(-jnp.abs(raw))))
    return lengths


def by_head(first, second, rows):
    return jnp.where(lane_ids(rows) < HEAD_CHANNELS, first, second)


def prefill_decay(lengths, rate_ref, rows):
    t_at = lax.broadcasted_iota(jnp.int32, (rows, rows), 0)
    s_at = lax.broadcasted_iota(jnp.int32, (rows, rows), 1)
    same = t_at // STRETCH == s_at // STRETCH
    columns, lines, steps = [], [], []
    rate = as_row(rate_ref)
    for h in range(HEAD_DEV):
        length = lengths[h][:rows]
        decay = -(length * rate[:, h : h + 1])
        line = jnp.sum(jnp.where(same & (t_at <= s_at), decay, 0.0), axis=0, keepdims=True)
        lines.append(line)
        columns.append(jnp.sum(jnp.where(t_at == s_at, line, 0.0), axis=1, keepdims=True))
        steps.append(jnp.sum(jnp.where(t_at == s_at, length, 0.0), axis=0, keepdims=True))
    return columns, lines, steps, same & (t_at >= s_at)


def end_states(rows, summed, adapter_up, bias, rate, start, slots, held, tenants):
    owned = start.shape[0]
    prefill = owned * STRETCH
    slot_count = slots.shape[0]

    def body(slots_ref, held_ref, tenants_ref, bias_ref, rate_ref, x_ref, a_ref, s_ref, v_ref, f_ref):
        corner = row_ids(LANES, LANES) == lane_ids(LANES)
        group = lax.axis_index("grp")
        mixed = mixed_rows(x_ref, rows)
        lanes = lane_ids(rows)
        mine = tenant_lanes(rows) == row_tenants(slots_ref, held_ref, tenants_ref, group, owned, slot_count)
        picked = jnp.where(lanes < ADAPTER_RANK, mixed, 0.0)
        shift = ADAPTER_RANK
        while shift < LANES:
            picked = picked + pltpu.roll(picked, shift, 1)
            shift *= 2
        picked = jnp.where(mine, picked, 0.0).astype(BF16)
        values = by_head(piece(x_ref, 0, rows), pltpu.roll(piece(x_ref, 1, rows), HEAD_CHANNELS, 1), rows)
        values = values + mxu(picked, a_ref[...])
        v_ref[...] = values
        lengths = step_lengths(mixed[:prefill], bias_ref)
        columns, _, _, _ = prefill_decay(lengths, rate_ref, prefill)
        for i in range(owned):
            lo, hi = i * STRETCH, (i + 1) * STRETCH
            ends = [columns[h][hi - 1 : hi] for h in range(HEAD_DEV)]
            tails = [jnp.exp(ends[h] - columns[h][lo:hi]) * lengths[h][lo:hi] for h in range(HEAD_DEV)]
            added = dot_tn(by_head(tails[0], tails[1], STRETCH) * values[lo:hi], piece(x_ref, 2, rows, slice(lo, hi)))
            kept = jnp.where(row_ids(LANES) < HEAD_CHANNELS, jnp.exp(ends[0]), jnp.exp(ends[1]))
            state = kept * s_ref[i] + added
            largest = jnp.max(jnp.abs(state), axis=1, keepdims=True)
            power = jnp.ceil(jnp.log2(jnp.maximum(largest, 1e-30)))
            f_ref[i * LANES : (i + 1) * LANES] = state * jnp.exp2(-power)
            line = jnp.sum(jnp.where(corner, power, 0.0), axis=0, keepdims=True)
            f_ref[owned * LANES + i * PAD : owned * LANES + (i + 1) * PAD] = jnp.broadcast_to(line, (PAD, LANES))

    return pl.pallas_call(
        body,
        out_shape=(
            jax.ShapeDtypeStruct((rows, LANES), F32),
            jax.ShapeDtypeStruct((owned * (LANES + PAD), STATE), F32),
        ),
        in_specs=[VMEM] * 8,
        out_specs=(VMEM, VMEM),
        compiler_params=pltpu.CompilerParams(vmem_limit_bytes=BIG),
    )(slots, held, tenants, bias, rate, summed, adapter_up, start)


def normalise(result, gate, scale_ref):
    gated = result * (gate * (1.0 / (1.0 + jnp.exp(-gate))))
    spread = jnp.mean(gated * gated, axis=1, keepdims=True)
    return (gated * lax.rsqrt(spread + 1e-05) * scale_ref[...]).astype(BF16)


def gates(x_ref, rows, at):
    first, second = piece(x_ref, 0, rows, at), piece(x_ref, 1, rows, at)
    return by_head(pltpu.roll(first, HEAD_CHANNELS, 1), second, first.shape[0])


def rows_within(summed, values, start, bias, rate, skip, norm_scale):
    rows = values.shape[0]
    owned = start.shape[0]
    prefill = owned * STRETCH
    slot_count = (rows - prefill) // STEPS

    def body(bias_ref, rate_ref, skip_ref, x_ref, v_ref, s_ref, g_ref, n_ref, y_ref):
        rate, skip = as_row(rate_ref), as_row(skip_ref)
        lengths = step_lengths(mixed_rows(x_ref, rows), bias_ref)
        columns, lines, steps, later = prefill_decay(lengths, rate_ref, prefill)
        now = slice(0, prefill)
        values = v_ref[now]
        scores = dot_nt(piece(x_ref, 3, rows, now), piece(x_ref, 2, rows, now))
        sums = []
        for h in range(HEAD_DEV):
            weights = jnp.where(later, jnp.exp(jnp.where(later, columns[h] - lines[h], 0.0)), 0.0) * steps[h]
            sums.append(split_dot(weights * scores, values, ((1,), (0,))))
        result = by_head(sums[0], sums[1], prefill)
        carried = jnp.concatenate(
            [dot_nt(piece(x_ref, 3, rows, slice(i * STRETCH, (i + 1) * STRETCH)), s_ref[i]) for i in range(owned)], axis=0
        )
        kept = by_head(jnp.exp(columns[0]), jnp.exp(columns[1]), prefill)
        skipped = by_head(skip[:, :1], skip[:, 1:], prefill)
        result = result + kept * carried + skipped * values
        n_ref[...] = normalise(result, gates(x_ref, rows, now), g_ref)
        at = [slice(prefill + s * slot_count, prefill + (s + 1) * slot_count) for s in range(STEPS)]
        run = [[], []]
        for h in range(HEAD_DEV):
            total = jnp.zeros((slot_count, 1), F32)
            for s in range(STEPS):
                total = total - lengths[h][at[s]] * rate[:, h : h + 1]
                run[h].append(total)
        skipped = by_head(skip[:, :1], skip[:, 1:], slot_count)
        for s in range(STEPS):
            total = skipped * v_ref[at[s]]
            for u in range(s + 1):
                score = jnp.sum(piece(x_ref, 3, rows, at[s]) * piece(x_ref, 2, rows, at[u]), axis=1, keepdims=True)
                factor = [jnp.exp(run[h][s] - run[h][u]) * lengths[h][at[u]] * score for h in range(HEAD_DEV)]
                total = total + by_head(factor[0], factor[1], slot_count) * v_ref[at[u]]
            y_ref[s * slot_count : (s + 1) * slot_count] = total

    return pl.pallas_call(
        body,
        out_shape=(
            jax.ShapeDtypeStruct((prefill, LANES), BF16),
            jax.ShapeDtypeStruct((rows - prefill, LANES), F32),
        ),
        in_specs=[VMEM] * 7,
        out_specs=(VMEM, VMEM),
        compiler_params=pltpu.CompilerParams(vmem_limit_bytes=BIG),
    )(bias, rate, skip, summed, values, start, norm_scale)


def decode_rows_out(summed, within, prefill_normed, finals, bias, rate, norm_scale, slots, held):
    prefill = prefill_normed.shape[0]
    rows = prefill + within.shape[0]
    owned = finals[0].shape[0] // (LANES + PAD)
    slot_count = slots.shape[0]
    parts = len(finals)

    def body(slots_ref, held_ref, bias_ref, rate_ref, x_ref, y_ref, p_ref, g_ref, *rest):
        f_refs, n_ref = rest[:parts], rest[parts]
        group = lax.axis_index("grp")
        held, rate = numbers(held_ref), as_row(rate_ref)
        now = slice(prefill, rows)
        prompts = row_prompts(slots_ref, slot_count)
        prompts = jnp.concatenate([prompts] * STEPS, axis=0)
        reader = piece(x_ref, 3, rows, now)
        carried = jnp.zeros((rows - prefill, LANES), F32)
        for j in range(parts):
            for i in range(owned):
                mine = prompts == entry(held, (group ^ j) * owned + i)
                part = dot_nt(jnp.where(mine, reader, 0.0), f_refs[j][i * LANES : (i + 1) * LANES])
                at = owned * LANES + i * PAD
                carried = carried + part * jnp.exp2(f_refs[j][at : at + 1])
        lengths = step_lengths(mixed_rows(x_ref, rows)[now], bias_ref)
        kept = []
        for h in range(HEAD_DEV):
            total = jnp.zeros((slot_count, 1), F32)
            runs = []
            for s in range(STEPS):
                total = total - lengths[h][s * slot_count : (s + 1) * slot_count] * rate[:, h : h + 1]
                runs.append(total)
            kept.append(jnp.exp(jnp.concatenate(runs, axis=0)))
        result = y_ref[...] + by_head(kept[0], kept[1], rows - prefill) * carried
        n_ref[:prefill] = p_ref[...]
        n_ref[prefill:] = normalise(result, gates(x_ref, rows, now), g_ref)

    return pl.pallas_call(
        body,
        out_shape=jax.ShapeDtypeStruct((rows, LANES), BF16),
        in_specs=[VMEM] * (8 + parts),
        out_specs=VMEM,
        compiler_params=pltpu.CompilerParams(vmem_limit_bytes=BIG),
    )(slots, held, bias, rate, summed, within, prefill_normed, norm_scale, *finals)


def output_rows(sources, near, far, weights, prefill_rows, decode_rows):
    chips, rows, _ = near.shape
    prefill, width = prefill_rows.shape
    parts = len(weights)
    per_part = chips // parts
    tile = width // 4 if width % 512 == 0 else width
    tiles = width // tile
    flat = [w for part in weights for w in part]

    def body(a_ref, b_ref, up_ref, ud_ref, *rest):
        w_refs = rest[: len(flat)]
        op_ref, od_ref, total_ref, sems = rest[len(flat) :]
        lefts, rights, at = [], [], 0
        for j in range(parts):
            for k in range(per_part):
                chip = looked_up(sources[k], lax.axis_index("grp") ^ j, lax.axis_index("head") // 2)
                if len(weights[j]) == 1:
                    lefts.append(jnp.concatenate([a_ref[chip], b_ref[chip]], axis=1))
                    rights.append((w_refs[at], (k,), 2))
                else:
                    lefts.extend([a_ref[chip], b_ref[chip]])
                    rights.extend([(w_refs[at], (k,), 1), (w_refs[at + 1], (k,), 1)])
            at += len(weights[j])
        copies = []
        for t in range(tiles):
            columns = slice(t * tile, (t + 1) * tile)
            total = jnp.concatenate([up_ref[:, columns], ud_ref[:, columns]], axis=0).astype(F32)
            for left, (w_ref, (k,), cores) in zip(lefts, rights):
                if cores == 2:
                    total = total + mxu(left, w_ref[k, :, :, columns].reshape(left.shape[1], tile))
                else:
                    total = total + mxu(left, w_ref[k, :, columns])
            total_ref[t] = total
            copies.append(pltpu.make_async_copy(total_ref.at[t, :prefill], op_ref.at[:, columns], sems.at[2 * t]))
            copies.append(pltpu.make_async_copy(total_ref.at[t, prefill:], od_ref.at[:, columns], sems.at[2 * t + 1]))
            copies[-2].start()
            copies[-1].start()
        for copy in copies:
            copy.wait()

    return pl.pallas_call(
        body,
        out_shape=(
            jax.ShapeDtypeStruct(prefill_rows.shape, F32),
            jax.ShapeDtypeStruct(decode_rows.shape, F32),
        ),
        in_specs=[VMEM] * (4 + len(flat)),
        out_specs=(pl.BlockSpec(memory_space=pltpu.HBM),) * 2,
        scratch_shapes=[pltpu.VMEM((tiles, rows, tile), F32), pltpu.SemaphoreType.DMA((2 * tiles,))],
        compiler_params=pltpu.CompilerParams(vmem_limit_bytes=BIG),
    )(near, far, prefill_rows, decode_rows, *flat)


def solution(mesh):
    groups, heads = mesh.shape["grp"], mesh.shape["head"]
    chips = heads // 2
    stages = [1 << b for b in range(chips.bit_length() - 1)]

    def across(x, distance):
        return lax.ppermute(x, "head", [(i, i ^ distance) for i in range(heads)])

    def over_groups(x, distance):
        return lax.ppermute(x, "grp", [(i, i ^ distance) for i in range(groups)])

    routes = chip_routes(chips, groups)

    def weights_over_head(pieces):
        parts = []
        for k, rows in enumerate(routes):
            pairs = [
                (g * heads + h, g * heads + 2 * rows[g][h // 2] + h % 2) for g in range(groups) for h in range(heads)
            ]
            crossed = [(a, b ^ 1) for a, b in pairs]
            parts.append(
                jnp.stack(
                    [lax.ppermute(pieces[k, 0], ("grp", "head"), pairs), lax.ppermute(pieces[k, 1], ("grp", "head"), crossed)]
                )
            )
        return parts

    def weights_over_groups(parts, summed):
        both = jnp.stack(parts)
        if groups != 4:
            return [(both,)] + [(over_groups(both, j),) for j in range(1, groups)], summed
        near, side = over_groups(both, 1), over_groups(both, 2)
        summed, near = lax.optimization_barrier((summed, near))
        return [(both,), (near,), (side,), (over_groups(side[:, 0], 1), over_groups(near[:, 1], 2))], summed

    sources = [[[z ^ row.index(z) for z in range(chips)] for row in rows] for rows in routes]

    def on_device(
        prefill_token_rows,
        decode_token_rows,
        input_weight,
        lowrank_weight,
        step_size_weight,
        adapter_up_weight,
        output_weight,
        head_decay_rate,
        head_step_bias,
        head_skip_scale,
        gated_norm_scale,
        prompt_start_state,
        prompt_at_position,
        slot_sample_index,
        prompt_adapter_index,
    ):
        owned = prompt_start_state.shape[0]
        slots = slot_sample_index.shape[0]
        start = prompt_start_state.reshape(owned, HEAD_DEV * HEAD_CHANNELS, STATE)
        decode_rows = decode_token_rows.reshape(STEPS * slots, decode_token_rows.shape[2])
        norm_scale = gated_norm_scale.reshape(1, HEAD_DEV * HEAD_CHANNELS)
        send, keep, pieces = project(
            routes, prefill_token_rows, decode_rows, input_weight, lowrank_weight, step_size_weight.T,
            slot_sample_index, prompt_at_position, prompt_adapter_index, output_weight, owned,
        )
        parts = weights_over_head(pieces)
        rows = prefill_token_rows.shape[0] + decode_rows.shape[0]
        split = keep.shape[0]
        summed = jnp.concatenate([keep, send[split:]]) + across(send, 1)
        for distance in stages:
            half = split // 2
            outgoing = jnp.concatenate([summed[:half], summed[split:]]).astype(F16)
            summed = summed[half:] + across(outgoing, 2 * distance).astype(F32)
            split = half
        weights, summed = weights_over_groups(parts, summed)
        values, finals = end_states(
            rows, summed, adapter_up_weight, head_step_bias, head_decay_rate, start,
            slot_sample_index, prompt_at_position, prompt_adapter_index,
        )
        message = finals.astype(F16)
        all_finals = [finals] + [over_groups(message, j).astype(F32) for j in range(1, groups)]
        prefill_normed, within = rows_within(
            summed, values, start, head_step_bias, head_decay_rate, head_skip_scale, norm_scale
        )
        normed = decode_rows_out(
            summed, within, prefill_normed, all_finals, head_step_bias, head_decay_rate, norm_scale,
            slot_sample_index, prompt_at_position,
        )
        near = normed[None]
        have = [0]
        for distance in reversed(stages):
            if distance == stages[0]:
                near, last = lax.optimization_barrier((near, weights[-1][-1]))
                weights = weights[:-1] + [weights[-1][:-1] + (last,)]
            near = jnp.concatenate([near, across(near, 2 * distance)])
            have = have + [c ^ distance for c in have]
        near = jnp.concatenate([near[have.index(c)][None] for c in range(chips)])
        far = across(near, 1)
        prefill_out, decode_out = output_rows(sources, near, far, weights, prefill_token_rows, decode_rows)
        return prefill_out, decode_out.reshape(decode_token_rows.shape)

    placed = (
        P("grp", "head"),
        P(None, "grp", "head"),
        P("head", None),
        P("head", None),
        P("head", None),
        P(None, "head"),
        P("head", None),
        P("head"),
        P("head"),
        P("head"),
        P("head"),
        P("grp", "head", None, None),
        P(),
        P("grp"),
        P(),
    )
    return jax.shard_map(
        on_device,
        mesh=mesh,
        in_specs=placed,
        out_specs=(P("grp", "head"), P(None, "grp", "head")),
        check_vma=False,
    )
```

```python
import itertools

import jax
import jax.numpy as jnp
from jax import lax
from jax.experimental import pallas as pl
from jax.experimental.pallas import tpu as pltpu
from jax.sharding import PartitionSpec as P

HEAD_CHANNELS = 64
STATE = 128
HEAD_DEV = 2
STRETCH = 32
SAMPLES = 16
STEPS = 3
ADAPTER_RANK = 16
LANES = 128
F32 = jnp.float32
BF16 = jnp.bfloat16
F16 = jnp.float16
VMEM = pl.BlockSpec(memory_space=pltpu.VMEM)
PAD = 16
BIG = 24 * 1024 * 1024


def mxu(a, b):
    return jnp.dot(a, b, preferred_element_type=F32)


def in_hbm(x):
    return pltpu.with_memory_space_constraint(x, pltpu.HBM)


def split_dot(a, b, dims):
    a_high, b_high = a.astype(BF16), b.astype(BF16)
    a_low, b_low = (a - a_high.astype(F32)).astype(BF16), (b - b_high.astype(F32)).astype(BF16)

    def part(x, y):
        return lax.dot_general(x, y, (dims, ((), ())), preferred_element_type=F32)

    return part(a_high, b_high) + (part(a_high, b_low) + part(a_low, b_high))


def dot_nt(a, b):
    return split_dot(a, b, ((1,), (1,)))


def dot_tn(a, b):
    return split_dot(a, b, ((0,), (0,)))


def lane_ids(rows):
    return lax.broadcasted_iota(jnp.int32, (rows, LANES), 1)


def row_ids(rows, width=1):
    return lax.broadcasted_iota(jnp.int32, (rows, width), 0)


def as_row(ref):
    return ref[...].reshape(1, ref.shape[0])


def entry(row, at):
    lanes = lax.broadcasted_iota(jnp.int32, row.shape, 1)
    return jnp.sum(jnp.where(lanes == at, row, 0.0), axis=1, keepdims=True)


def numbers(ref):
    return as_row(ref).astype(F32)


def row_prompts(slots_ref, slots):
    row = (as_row(slots_ref) // SAMPLES).astype(F32)
    return jnp.sum(jnp.where(row_ids(slots, slots) == lax.broadcasted_iota(jnp.int32, (slots, slots), 1), row, 0.0), axis=1, keepdims=True)


def row_tenants(slots_ref, held_ref, tenants_ref, group, owned, slots):
    prompts = row_prompts(slots_ref, slots)
    tenants, held = numbers(tenants_ref), numbers(held_ref)
    lanes = lax.broadcasted_iota(jnp.int32, tenants.shape, 1).astype(F32)
    decode = jnp.sum(jnp.where(lanes == prompts, tenants, 0.0), axis=1, keepdims=True)
    prefill = []
    for i in range(owned):
        prompt = entry(held, group * owned + i)
        tenant = jnp.sum(jnp.where(lanes == prompt, tenants, 0.0), axis=1, keepdims=True)
        prefill.append(jnp.broadcast_to(tenant, (STRETCH, 1)))
    return jnp.concatenate(prefill + [decode] * STEPS, axis=0)


def tenant_lanes(rows):
    return (lane_ids(rows) // ADAPTER_RANK).astype(F32)


def place_order(chips):
    bits = chips.bit_length() - 1
    order = []
    for p in range(chips):
        j = chips - 1 - p
        order.append(sum(((j >> b) & 1) << (bits - 1 - b) for b in range(bits)))
    return order


def packing(rows, heads):
    lanes = ADAPTER_RANK + heads
    pack = 1
    while 2 * pack * lanes <= LANES and rows % (2 * pack * 8) == 0:
        pack *= 2
    return pack


def pack_rows(mixed, pack):
    part, span = mixed.shape[0] // pack, LANES // pack
    total = mixed[:part]
    for q in range(1, pack):
        total = total + pltpu.roll(mixed[q * part : (q + 1) * part], q * span, 1)
    return total


def unpack_rows(packed, pack):
    span = LANES // pack
    parts = [packed] + [pltpu.roll(packed, LANES - q * span, 1) for q in range(1, pack)]
    return jnp.concatenate(parts, axis=0)


def project(
    routes, prefill_rows, decode_rows, input_weight, lowrank_weight, step_lines, slots, held, tenants, output_weight, owned
):
    rows_prefill, depth = prefill_rows.shape
    rows = rows_prefill + decode_rows.shape[0]
    width = 2 * HEAD_DEV * HEAD_CHANNELS
    pieces = width // LANES
    chips = input_weight.shape[1] // width // 2
    order = place_order(chips)
    low_blocks = 2 * STATE // LANES
    heads = step_lines.shape[0]
    pack = packing(rows, heads)
    packed = rows // pack
    base = chips * pieces * rows
    total = base + low_blocks * rows + packed
    slot_count = slots.shape[0]
    count = len(routes)
    column_width = output_weight.shape[1] // (2 * chips)

    def piece_copies(v_ref, p_ref, sems):
        group, head = lax.axis_index("grp"), lax.axis_index("head")
        copies = []
        for k, rows_of in enumerate(routes):
            target = looked_up(rows_of, group, head // 2)
            for side in range(2):
                column = pl.multiple_of((2 * target + ((head % 2) ^ side)) * column_width, column_width)
                copies.append(
                    pltpu.make_async_copy(
                        v_ref.at[:, pl.ds(column, column_width)], p_ref.at[k, side], sems.at[2 * k + side]
                    )
                )
        return copies

    def fetches(up_ref, ud_ref, w_ref, u_ref, w_all, sems, odd):
        me = lax.axis_index("head")
        copies = [
            pltpu.make_async_copy(up_ref, u_ref.at[:rows_prefill], sems.at[0]),
            pltpu.make_async_copy(ud_ref, u_ref.at[rows_prefill:], sems.at[1]),
        ]
        for i in range(chips):
            column = pl.multiple_of(((order[i] * 2 + odd) ^ me) * width, width)
            copies.append(pltpu.make_async_copy(w_ref.at[:, pl.ds(column, width)], w_all.at[i], sems.at[2 + i]))
        return copies

    def products(copies, u_ref, w_all, o_ref):
        for i in range(chips):
            copies[2 + i].wait()
            part = mxu(u_ref[...], w_all[i])
            for k in range(pieces):
                at = (i * pieces + k) * rows
                o_ref[at : at + rows] = part[:, k * LANES : (k + 1) * LANES]

    def send_body(
        slots_hbm, held_hbm, tenants_hbm, up_ref, ud_ref, w_ref, l_ref, s_ref, v_ref, o_ref, p_ref,
        u_ref, w_all, l_all, s_all, m_ref, slots_ref, held_ref, tenants_ref, sems, piece_sems,
    ):
        copies = fetches(up_ref, ud_ref, w_ref, u_ref, w_all, sems, 1)
        low_copies = [
            pltpu.make_async_copy(l_ref, l_all, sems.at[2 + chips]),
            pltpu.make_async_copy(s_ref, s_all, sems.at[3 + chips]),
        ]
        index_copies = [
            pltpu.make_async_copy(slots_hbm, slots_ref, sems.at[4 + chips]),
            pltpu.make_async_copy(held_hbm, held_ref, sems.at[5 + chips]),
            pltpu.make_async_copy(tenants_hbm, tenants_ref, sems.at[6 + chips]),
        ]
        moved = piece_copies(v_ref, p_ref, piece_sems)
        for copy in index_copies + copies[:2] + low_copies + copies[2:] + moved:
            copy.start()
        for copy in index_copies:
            copy.wait()
        lanes = tenant_lanes(rows)
        mine = lanes == row_tenants(slots_ref, held_ref, tenants_ref, lax.axis_index("grp"), owned, slot_count)
        for copy in copies[:2] + low_copies:
            copy.wait()
        low = mxu(u_ref[...], l_all[...])
        for k in range(low_blocks):
            o_ref[base + k * rows : base + (k + 1) * rows] = low[:, k * LANES : (k + 1) * LANES]
        picked = jnp.where(mine, low[:, 2 * STATE :], 0.0)
        shift = LANES // 2
        while shift >= ADAPTER_RANK:
            picked = picked + pltpu.roll(picked, shift, 1)
            shift //= 2
        m_ref[...] = jnp.where(lane_ids(rows) < ADAPTER_RANK, picked, 0.0)
        m_ref[:, ADAPTER_RANK : ADAPTER_RANK + heads] = lax.dot_general(
            u_ref[...], s_all[...], (((1,), (1,)), ((), ())), preferred_element_type=F32
        )
        o_ref[base + low_blocks * rows :] = pack_rows(m_ref[...], pack)
        products(copies, u_ref, w_all, o_ref)
        for copy in moved:
            copy.wait()

    def keep_body(up_ref, ud_ref, w_ref, o_ref, u_ref, w_all, sems):
        copies = fetches(up_ref, ud_ref, w_ref, u_ref, w_all, sems, 0)
        for copy in copies:
            copy.start()
        for copy in copies[:2]:
            copy.wait()
        products(copies, u_ref, w_all, o_ref)

    hbm = pl.BlockSpec(memory_space=pltpu.HBM)
    scratch = [pltpu.VMEM((rows, depth), BF16), pltpu.VMEM((chips, depth, width), BF16)]
    cost = pl.CostEstimate(
        flops=2 * rows * depth * width * chips, bytes_accessed=2 * depth * width * chips, transcendentals=0
    )
    params = pltpu.CompilerParams(vmem_limit_bytes=BIG)
    send, pieces_out = pl.pallas_call(
        send_body,
        out_shape=(
            jax.ShapeDtypeStruct((total, LANES), F32),
            jax.ShapeDtypeStruct((count, 2, output_weight.shape[0], column_width), BF16),
        ),
        in_specs=[hbm] * 9,
        out_specs=(VMEM, VMEM),
        scratch_shapes=scratch
        + [
            pltpu.VMEM(lowrank_weight.shape, BF16),
            pltpu.VMEM(step_lines.shape, BF16),
            pltpu.VMEM((rows, LANES), F32),
            pltpu.VMEM(slots.shape, jnp.int32),
            pltpu.VMEM(held.shape, jnp.int32),
            pltpu.VMEM(tenants.shape, jnp.int32),
            pltpu.SemaphoreType.DMA((chips + 7,)),
            pltpu.SemaphoreType.DMA((2 * count,)),
        ],
        compiler_params=params,
        cost_estimate=cost,
    )(
        *[
            in_hbm(x)
            for x in (
                slots, held, tenants, prefill_rows, decode_rows, input_weight, lowrank_weight, step_lines, output_weight
            )
        ]
    )
    keep = pl.pallas_call(
        keep_body,
        out_shape=jax.ShapeDtypeStruct((base, LANES), F32),
        in_specs=[hbm] * 3,
        out_specs=VMEM,
        scratch_shapes=scratch + [pltpu.SemaphoreType.DMA((chips + 2,))],
        compiler_params=params,
        cost_estimate=cost,
    )(*[in_hbm(x) for x in (prefill_rows, decode_rows, input_weight)])
    return send, keep, pieces_out


def line_load(route):
    steps = [0] * (2 * len(route))
    for a, b in enumerate(route):
        for link in range(min(a, b), max(a, b)):
            steps[2 * link + (a < b)] += 1
    return max(steps)


def chip_routes(chips, groups):
    wanted = [tuple(z ^ shift for z in range(chips)) for shift in range(chips)]
    if chips <= 4:
        ranked = sorted(itertools.permutations(range(chips)), key=lambda route: (line_load(route), route))

        def fill(rows, most):
            if len(rows) == chips:
                return rows
            for route in ranked:
                if line_load(route) <= most and all(a != b for row in rows for a, b in zip(row, route)):
                    found = fill(rows + [route], most)
                    if found:
                        return found
            return None

        for most in range(chips + 1):
            found = fill([], most)
            if found:
                wanted = found
                break
    return [wanted[groups * k : groups * (k + 1)] for k in range(chips // groups)]


def piece(x_ref, k, rows, at=slice(None)):
    low, high, _ = at.indices(rows)
    return x_ref[k * rows + low : k * rows + high]


def mixed_rows(x_ref, rows):
    return unpack_rows(x_ref[4 * rows :], rows // (x_ref.shape[0] - 4 * rows))


def piece(x_ref, k, rows, at=slice(None)):
    low, high, _ = at.indices(rows)
    return x_ref[k * rows + low : k * rows + high]


def mixed_rows(x_ref, rows):
    return unpack_rows(x_ref[4 * rows :], rows // (x_ref.shape[0] - 4 * rows))


def looked_up(table, group, chip):
    found = jnp.int32(0)
    for g, row in enumerate(table):
        for z, value in enumerate(row):
            found = jnp.where((group == g) & (chip == z), value, found)
    return found


def piece(x_ref, k, rows, at=slice(None)):
    low, high, _ = at.indices(rows)
    return x_ref[k * rows + low : k * rows + high]


def mixed_rows(x_ref, rows):
    return unpack_rows(x_ref[4 * rows :], rows // (x_ref.shape[0] - 4 * rows))


def looked_up(table, group, chip):
    found = jnp.int32(0)
    for g, row in enumerate(table):
        for z, value in enumerate(row):
            found = jnp.where((group == g) & (chip == z), value, found)
    return found


def weight_pieces(output_weight, routes, heads):
    own_rows, all_width = output_weight.shape
    width = all_width // heads
    count = len(routes)

    def body(w_ref, o_ref, sems):
        group, head = lax.axis_index("grp"), lax.axis_index("head")
        copies = []
        for k, rows in enumerate(routes):
            target = looked_up(rows, group, head // 2)
            for side in range(2):
                column = pl.multiple_of((2 * target + ((head % 2) ^ side)) * width, width)
                copies.append(
                    pltpu.make_async_copy(w_ref.at[:, pl.ds(column, width)], o_ref.at[k, side], sems.at[2 * k + side])
                )
        for copy in copies:
            copy.start()
        for copy in copies:
            copy.wait()

    return pl.pallas_call(
        body,
        out_shape=jax.ShapeDtypeStruct((count, 2, own_rows, width), BF16),
        in_specs=[pl.BlockSpec(memory_space=pltpu.HBM)],
        out_specs=VMEM,
        scratch_shapes=[pltpu.SemaphoreType.DMA((2 * count,))],
        compiler_params=pltpu.CompilerParams(vmem_limit_bytes=BIG),
    )(in_hbm(output_weight))


def step_lengths(mixed, bias_ref):
    lanes = lane_ids(mixed.shape[0])
    me = lax.axis_index("head")
    bias = as_row(bias_ref)
    lengths = []
    for h in range(HEAD_DEV):
        raw = jnp.sum(jnp.where(lanes == ADAPTER_RANK + me * HEAD_DEV + h, mixed, 0.0), axis=1, keepdims=True)
        raw = raw + bias[:, h : h + 1]
        lengths.append(jnp.maximum(raw, 0.0) + jnp.log1p(jnp.exp(-jnp.abs(raw))))
    return lengths


def by_head(first, second, rows):
    return jnp.where(lane_ids(rows) < HEAD_CHANNELS, first, second)


def prefill_decay(lengths, rate_ref, rows):
    t_at = lax.broadcasted_iota(jnp.int32, (rows, rows), 0)
    s_at = lax.broadcasted_iota(jnp.int32, (rows, rows), 1)
    same = t_at // STRETCH == s_at // STRETCH
    columns, lines, steps = [], [], []
    rate = as_row(rate_ref)
    for h in range(HEAD_DEV):
        length = lengths[h][:rows]
        decay = -(length * rate[:, h : h + 1])
        line = jnp.sum(jnp.where(same & (t_at <= s_at), decay, 0.0), axis=0, keepdims=True)
        lines.append(line)
        columns.append(jnp.sum(jnp.where(t_at == s_at, line, 0.0), axis=1, keepdims=True))
        steps.append(jnp.sum(jnp.where(t_at == s_at, length, 0.0), axis=0, keepdims=True))
    return columns, lines, steps, same & (t_at >= s_at)


def end_states(rows, summed, adapter_up, bias, rate, start, slots, held, tenants):
    owned = start.shape[0]
    prefill = owned * STRETCH
    slot_count = slots.shape[0]

    def body(slots_ref, held_ref, tenants_ref, bias_ref, rate_ref, x_ref, a_ref, s_ref, v_ref, f_ref):
        corner = row_ids(LANES, LANES) == lane_ids(LANES)
        group = lax.axis_index("grp")
        mixed = mixed_rows(x_ref, rows)
        lanes = lane_ids(rows)
        mine = tenant_lanes(rows) == row_tenants(slots_ref, held_ref, tenants_ref, group, owned, slot_count)
        picked = jnp.where(lanes < ADAPTER_RANK, mixed, 0.0)
        shift = ADAPTER_RANK
        while shift < LANES:
            picked = picked + pltpu.roll(picked, shift, 1)
            shift *= 2
        picked = jnp.where(mine, picked, 0.0).astype(BF16)
        values = by_head(piece(x_ref, 0, rows), pltpu.roll(piece(x_ref, 1, rows), HEAD_CHANNELS, 1), rows)
        values = values + mxu(picked, a_ref[...])
        v_ref[...] = values
        lengths = step_lengths(mixed[:prefill], bias_ref)
        columns, _, _, _ = prefill_decay(lengths, rate_ref, prefill)
        for i in range(owned):
            lo, hi = i * STRETCH, (i + 1) * STRETCH
            ends = [columns[h][hi - 1 : hi] for h in range(HEAD_DEV)]
            tails = [jnp.exp(ends[h] - columns[h][lo:hi]) * lengths[h][lo:hi] for h in range(HEAD_DEV)]
            added = dot_tn(by_head(tails[0], tails[1], STRETCH) * values[lo:hi], piece(x_ref, 2, rows, slice(lo, hi)))
            kept = jnp.where(row_ids(LANES) < HEAD_CHANNELS, jnp.exp(ends[0]), jnp.exp(ends[1]))
            state = kept * s_ref[i] + added
            largest = jnp.max(jnp.abs(state), axis=1, keepdims=True)
            power = jnp.ceil(jnp.log2(jnp.maximum(largest, 1e-30)))
            f_ref[i * LANES : (i + 1) * LANES] = state * jnp.exp2(-power)
            line = jnp.sum(jnp.where(corner, power, 0.0), axis=0, keepdims=True)
            f_ref[owned * LANES + i * PAD : owned * LANES + (i + 1) * PAD] = jnp.broadcast_to(line, (PAD, LANES))

    return pl.pallas_call(
        body,
        out_shape=(
            jax.ShapeDtypeStruct((rows, LANES), F32),
            jax.ShapeDtypeStruct((owned * (LANES + PAD), STATE), F32),
        ),
        in_specs=[VMEM] * 8,
        out_specs=(VMEM, VMEM),
        compiler_params=pltpu.CompilerParams(vmem_limit_bytes=BIG),
    )(slots, held, tenants, bias, rate, summed, adapter_up, start)


def normalise(result, gate, scale_ref):
    gated = result * (gate * (1.0 / (1.0 + jnp.exp(-gate))))
    spread = jnp.mean(gated * gated, axis=1, keepdims=True)
    return (gated * lax.rsqrt(spread + 1e-05) * scale_ref[...]).astype(BF16)


def gates(x_ref, rows, at):
    first, second = piece(x_ref, 0, rows, at), piece(x_ref, 1, rows, at)
    return by_head(pltpu.roll(first, HEAD_CHANNELS, 1), second, first.shape[0])


def rows_within(summed, values, start, bias, rate, skip, norm_scale):
    rows = values.shape[0]
    owned = start.shape[0]
    prefill = owned * STRETCH
    slot_count = (rows - prefill) // STEPS

    def body(bias_ref, rate_ref, skip_ref, x_ref, v_ref, s_ref, g_ref, n_ref, y_ref):
        rate, skip = as_row(rate_ref), as_row(skip_ref)
        lengths = step_lengths(mixed_rows(x_ref, rows), bias_ref)
        columns, lines, steps, later = prefill_decay(lengths, rate_ref, prefill)
        now = slice(0, prefill)
        values = v_ref[now]
        scores = dot_nt(piece(x_ref, 3, rows, now), piece(x_ref, 2, rows, now))
        sums = []
        for h in range(HEAD_DEV):
            weights = jnp.where(later, jnp.exp(jnp.where(later, columns[h] - lines[h], 0.0)), 0.0) * steps[h]
            sums.append(split_dot(weights * scores, values, ((1,), (0,))))
        result = by_head(sums[0], sums[1], prefill)
        carried = jnp.concatenate(
            [dot_nt(piece(x_ref, 3, rows, slice(i * STRETCH, (i + 1) * STRETCH)), s_ref[i]) for i in range(owned)], axis=0
        )
        kept = by_head(jnp.exp(columns[0]), jnp.exp(columns[1]), prefill)
        skipped = by_head(skip[:, :1], skip[:, 1:], prefill)
        result = result + kept * carried + skipped * values
        n_ref[...] = normalise(result, gates(x_ref, rows, now), g_ref)
        at = [slice(prefill + s * slot_count, prefill + (s + 1) * slot_count) for s in range(STEPS)]
        run = [[], []]
        for h in range(HEAD_DEV):
            total = jnp.zeros((slot_count, 1), F32)
            for s in range(STEPS):
                total = total - lengths[h][at[s]] * rate[:, h : h + 1]
                run[h].append(total)
        skipped = by_head(skip[:, :1], skip[:, 1:], slot_count)
        for s in range(STEPS):
            total = skipped * v_ref[at[s]]
            for u in range(s + 1):
                score = jnp.sum(piece(x_ref, 3, rows, at[s]) * piece(x_ref, 2, rows, at[u]), axis=1, keepdims=True)
                factor = [jnp.exp(run[h][s] - run[h][u]) * lengths[h][at[u]] * score for h in range(HEAD_DEV)]
                total = total + by_head(factor[0], factor[1], slot_count) * v_ref[at[u]]
            y_ref[s * slot_count : (s + 1) * slot_count] = total

    return pl.pallas_call(
        body,
        out_shape=(
            jax.ShapeDtypeStruct((prefill, LANES), BF16),
            jax.ShapeDtypeStruct((rows - prefill, LANES), F32),
        ),
        in_specs=[VMEM] * 7,
        out_specs=(VMEM, VMEM),
        compiler_params=pltpu.CompilerParams(vmem_limit_bytes=BIG),
    )(bias, rate, skip, summed, values, start, norm_scale)


def decode_rows_out(summed, within, prefill_normed, finals, bias, rate, norm_scale, slots, held):
    prefill = prefill_normed.shape[0]
    rows = prefill + within.shape[0]
    owned = finals[0].shape[0] // (LANES + PAD)
    slot_count = slots.shape[0]
    parts = len(finals)

    def body(slots_ref, held_ref, bias_ref, rate_ref, x_ref, y_ref, p_ref, g_ref, *rest):
        f_refs, n_ref = rest[:parts], rest[parts]
        group = lax.axis_index("grp")
        held, rate = numbers(held_ref), as_row(rate_ref)
        now = slice(prefill, rows)
        prompts = row_prompts(slots_ref, slot_count)
        prompts = jnp.concatenate([prompts] * STEPS, axis=0)
        reader = piece(x_ref, 3, rows, now)
        carried = jnp.zeros((rows - prefill, LANES), F32)
        for j in range(parts):
            for i in range(owned):
                mine = prompts == entry(held, (group ^ j) * owned + i)
                part = dot_nt(jnp.where(mine, reader, 0.0), f_refs[j][i * LANES : (i + 1) * LANES])
                at = owned * LANES + i * PAD
                carried = carried + part * jnp.exp2(f_refs[j][at : at + 1])
        lengths = step_lengths(mixed_rows(x_ref, rows)[now], bias_ref)
        kept = []
        for h in range(HEAD_DEV):
            total = jnp.zeros((slot_count, 1), F32)
            runs = []
            for s in range(STEPS):
                total = total - lengths[h][s * slot_count : (s + 1) * slot_count] * rate[:, h : h + 1]
                runs.append(total)
            kept.append(jnp.exp(jnp.concatenate(runs, axis=0)))
        result = y_ref[...] + by_head(kept[0], kept[1], rows - prefill) * carried
        n_ref[:prefill] = p_ref[...]
        n_ref[prefill:] = normalise(result, gates(x_ref, rows, now), g_ref)

    return pl.pallas_call(
        body,
        out_shape=jax.ShapeDtypeStruct((rows, LANES), BF16),
        in_specs=[VMEM] * (8 + parts),
        out_specs=VMEM,
        compiler_params=pltpu.CompilerParams(vmem_limit_bytes=BIG),
    )(slots, held, bias, rate, summed, within, prefill_normed, norm_scale, *finals)


def core_products(sources, weights, core, x_ref, w_refs):
    pairs, at = [], 0
    for j, part in enumerate(weights):
        for k in range(len(sources)):
            chip = looked_up(sources[k], lax.axis_index("grp") ^ j, lax.axis_index("head") // 2)
            place = (w_refs[at], (k, core)) if len(part) == 1 else (w_refs[at + core], (k,))
            pairs.append((x_ref[chip], place))
        at += len(part)
    return pairs


def near_rows(sources, near, weights, prefill_rows, decode_rows):
    width = prefill_rows.shape[1]
    rows = near.shape[1]
    flat = [w for part in weights for w in part]

    def body(a_ref, up_ref, ud_ref, *rest):
        w_refs, o_ref = rest[:-1], rest[-1]
        total = jnp.concatenate([up_ref[...], ud_ref[...]], axis=0).astype(F32)
        for left, (w_ref, at) in core_products(sources, weights, 0, a_ref, w_refs):
            total = total + mxu(left, w_ref[at])
        o_ref[...] = total

    return pl.pallas_call(
        body,
        out_shape=jax.ShapeDtypeStruct((rows, width), F32),
        in_specs=[VMEM] * (3 + len(flat)),
        out_specs=VMEM,
        compiler_params=pltpu.CompilerParams(vmem_limit_bytes=BIG),
    )(near, prefill_rows, decode_rows, *flat)


def output_rows(sources, near, far, weights, prefill_rows, decode_rows):
    rows = near.shape[1]
    prefill, width = prefill_rows.shape
    tile = width // 4 if width % 512 == 0 else width
    tiles = width // tile
    flat = [w for part in weights for w in part]
    begun = near_rows(sources, near, weights, prefill_rows, decode_rows)

    def body(b_ref, t_ref, *rest):
        w_refs = rest[: len(flat)]
        op_ref, od_ref, total_ref, sems = rest[len(flat) :]
        pairs = core_products(sources, weights, 1, b_ref, w_refs)
        copies = []
        for t in range(tiles):
            columns = slice(t * tile, (t + 1) * tile)
            total = t_ref[:, columns]
            for left, (w_ref, at) in pairs:
                total = total + mxu(left, w_ref[at + (slice(None), columns)])
            total_ref[t] = total
            copies.append(pltpu.make_async_copy(total_ref.at[t, :prefill], op_ref.at[:, columns], sems.at[2 * t]))
            copies.append(pltpu.make_async_copy(total_ref.at[t, prefill:], od_ref.at[:, columns], sems.at[2 * t + 1]))
            copies[-2].start()
            copies[-1].start()
        for copy in copies:
            copy.wait()

    return pl.pallas_call(
        body,
        out_shape=(
            jax.ShapeDtypeStruct(prefill_rows.shape, F32),
            jax.ShapeDtypeStruct(decode_rows.shape, F32),
        ),
        in_specs=[VMEM] * (2 + len(flat)),
        out_specs=(pl.BlockSpec(memory_space=pltpu.HBM),) * 2,
        scratch_shapes=[pltpu.VMEM((tiles, rows, tile), F32), pltpu.SemaphoreType.DMA((2 * tiles,))],
        compiler_params=pltpu.CompilerParams(vmem_limit_bytes=BIG),
    )(far, begun, *flat)


def solution(mesh):
    groups, heads = mesh.shape["grp"], mesh.shape["head"]
    chips = heads // 2
    stages = [1 << b for b in range(chips.bit_length() - 1)]

    def across(x, distance):
        return lax.ppermute(x, "head", [(i, i ^ distance) for i in range(heads)])

    def over_groups(x, distance):
        return lax.ppermute(x, "grp", [(i, i ^ distance) for i in range(groups)])

    routes = chip_routes(chips, groups)

    def weights_over_head(pieces):
        parts = []
        for k, rows in enumerate(routes):
            pairs = [
                (g * heads + h, g * heads + 2 * rows[g][h // 2] + h % 2) for g in range(groups) for h in range(heads)
            ]
            crossed = [(a, b ^ 1) for a, b in pairs]
            parts.append(
                jnp.stack(
                    [lax.ppermute(pieces[k, 0], ("grp", "head"), pairs), lax.ppermute(pieces[k, 1], ("grp", "head"), crossed)]
                )
            )
        return parts

    def weights_over_groups(parts, summed):
        both = jnp.stack(parts)
        if groups != 4:
            return [(both,)] + [(over_groups(both, j),) for j in range(1, groups)], summed
        near, side = over_groups(both, 1), over_groups(both, 2)
        summed, near = lax.optimization_barrier((summed, near))
        return [(both,), (near,), (side,), (over_groups(side[:, 0], 1), over_groups(near[:, 1], 2))], summed

    sources = [[[z ^ row.index(z) for z in range(chips)] for row in rows] for rows in routes]

    def on_device(
        prefill_token_rows,
        decode_token_rows,
        input_weight,
        lowrank_weight,
        step_size_weight,
        adapter_up_weight,
        output_weight,
        head_decay_rate,
        head_step_bias,
        head_skip_scale,
        gated_norm_scale,
        prompt_start_state,
        prompt_at_position,
        slot_sample_index,
        prompt_adapter_index,
    ):
        owned = prompt_start_state.shape[0]
        slots = slot_sample_index.shape[0]
        start = prompt_start_state.reshape(owned, HEAD_DEV * HEAD_CHANNELS, STATE)
        decode_rows = decode_token_rows.reshape(STEPS * slots, decode_token_rows.shape[2])
        norm_scale = gated_norm_scale.reshape(1, HEAD_DEV * HEAD_CHANNELS)
        send, keep, pieces = project(
            routes, prefill_token_rows, decode_rows, input_weight, lowrank_weight, step_size_weight.T,
            slot_sample_index, prompt_at_position, prompt_adapter_index, output_weight, owned,
        )
        parts = weights_over_head(pieces)
        rows = prefill_token_rows.shape[0] + decode_rows.shape[0]
        split = keep.shape[0]
        summed = jnp.concatenate([keep, send[split:]]) + across(send, 1)
        for distance in stages:
            half = split // 2
            outgoing = jnp.concatenate([summed[:half], summed[split:]]).astype(F16)
            summed = summed[half:] + across(outgoing, 2 * distance).astype(F32)
            split = half
        weights, summed = weights_over_groups(parts, summed)
        values, finals = end_states(
            rows, summed, adapter_up_weight, head_step_bias, head_decay_rate, start,
            slot_sample_index, prompt_at_position, prompt_adapter_index,
        )
        message = finals.astype(F16)
        all_finals = [finals] + [over_groups(message, j).astype(F32) for j in range(1, groups)]
        prefill_normed, within = rows_within(
            summed, values, start, head_step_bias, head_decay_rate, head_skip_scale, norm_scale
        )
        normed = decode_rows_out(
            summed, within, prefill_normed, all_finals, head_step_bias, head_decay_rate, norm_scale,
            slot_sample_index, prompt_at_position,
        )
        near = normed[None]
        have = [0]
        for distance in reversed(stages):
            if distance == stages[0]:
                near, last = lax.optimization_barrier((near, weights[-1][-1]))
                weights = weights[:-1] + [weights[-1][:-1] + (last,)]
            near = jnp.concatenate([near, across(near, 2 * distance)])
            have = have + [c ^ distance for c in have]
        near = jnp.concatenate([near[have.index(c)][None] for c in range(chips)])
        far = across(near, 1)
        prefill_out, decode_out = output_rows(sources, near, far, weights, prefill_token_rows, decode_rows)
        return prefill_out, decode_out.reshape(decode_token_rows.shape)

    placed = (
        P("grp", "head"),
        P(None, "grp", "head"),
        P("head", None),
        P("head", None),
        P("head", None),
        P(None, "head"),
        P("head", None),
        P("head"),
        P("head"),
        P("head"),
        P("head"),
        P("grp", "head", None, None),
        P(),
        P("grp"),
        P(),
    )
    return jax.shard_map(
        on_device,
        mesh=mesh,
        in_specs=placed,
        out_specs=(P("grp", "head"), P(None, "grp", "head")),
        check_vma=False,
    )
```
